32 devices in a mesh: seq: 8 (over y, x, core), tp: 4 (over z).
Axes of the slice: x: 2, y: 2, z: 4, core: 2. Of those that a mesh axis runs over, the one named last changes fastest.
Arguments:
- tokens: bfloat16 [4096, 4096], P(('seq', 'tp')), may hold values from -6 to 6
- norm_gain: float32 [4096], replicated, may hold values from 0.1 to 1.9
- in_weight: bfloat16 [3, 4096, 4096], P(None, 'seq', 'tp'), may hold values from -0.09375 to 0.09375
- filters: float32 [7, 256], P(None, 'tp'), may hold values from -4 to 4
- out_weight: bfloat16 [4096, 4096], P('tp', 'seq'), may hold values from -0.09375 to 0.09375
- keep_mask: int32 [4096, 4096], P(('seq', 'tp')), may hold values 0 or 1
Outputs:
- block_out: bfloat16 [4096, 4096], P(('seq', 'tp'))
The draws below stay inside these ranges and needn't reach their ends.
All inputs are finite; a program needn't handle non-finite values. No bound on the sum of `keep_mask` on one device may be relied on, other than what follows from the above.
Results may differ from the reference program's by a relative error of at most 0.013.
Values may be sent and summed in bfloat16 or wider, within the bound.
No kernel may reach another device: no remote copies, remote signals or barrier semaphores. Data moves between devices by JAX's collectives and lax.ppermute only.
A program may use at most 128 MiB of HBM per device.

```python
import jax
import jax.numpy as jnp
from jax import lax

D = 4096
C = 4096
GROUP = 16
TAPS = 7
TOKENS = 4096
N_TP = 4


def with_ends(drawn, stream_key, smallest, high):
    extent = drawn.shape
    index_at = [jax.random.randint(jax.random.fold_in(stream_key, axis), (), 0, extent[axis]) for axis in range(len(extent))]
    drawn = drawn.at[tuple(index_at)].set(smallest)
    longest = extent.index(max(extent))
    index_at[longest] = (index_at[longest] + 1) % extent[longest]
    return drawn.at[tuple(index_at)].set(high)


def level_of(stream_key, extent, split, least, high):
    gain = 1.0
    for dim, parts in split:
        steps = jax.random.uniform(jax.random.fold_in(jax.random.fold_in(stream_key, 6), dim), (parts,), jnp.float32, least / len(split), high / len(split))
        gain = gain * jnp.repeat(jnp.exp(steps), extent[dim] // parts).reshape((-1,) + (1,) * (len(extent) - 1 - dim))
    return gain


def normal_values(own_key, extent, scale, reach, split=(), kind=jnp.bfloat16):
    gain = level_of(own_key, extent, split, -0.22, 0.18) if split else 1.0
    result = jax.random.normal(own_key, extent, jnp.float32) * scale * gain
    return jnp.minimum(jnp.maximum(result, -reach), reach).astype(kind)


def setup_inputs(seed: int = 0) -> dict:
    key_of = jax.random.split(jax.random.key(seed), 7)
    tokens = normal_values(key_of[0], (TOKENS, D), 1.0, 6.0, ((0, 32),))
    norm_gain = jnp.clip(1.0 + 0.18 * jax.random.normal(key_of[1], (D,), jnp.float32), 0.1, 1.9)
    in_weight = normal_values(key_of[2], (3, D, C), D ** -0.5, 0.09375, ((1, 8), (2, 4)))
    filters = normal_values(key_of[3], (TAPS, C // GROUP), 0.4, 4.0, ((1, 4),), jnp.float32)
    out_weight = normal_values(key_of[4], (C, D), C ** -0.5, 0.09375, ((0, 4), (1, 8)))
    keep_mask = with_ends((jax.random.randint(key_of[5], (TOKENS, D), 0, 10) < 9).astype(jnp.int32), jax.random.fold_in(key_of[5], 1), 0, 1)
    return dict(tokens=tokens, norm_gain=norm_gain, in_weight=in_weight, filters=filters, out_weight=out_weight, keep_mask=keep_mask)


def reference(tokens, norm_gain, in_weight, filters, out_weight, keep_mask):
    widened = tokens.astype(jnp.float32)
    mean_sq = lax.optimization_barrier(jnp.mean(widened * widened, axis=1, keepdims=True))
    normed = (widened * lax.rsqrt(mean_sq + 1e-06) * norm_gain).astype(jnp.bfloat16)
    query = jnp.dot(normed, in_weight[0], preferred_element_type=jnp.float32).astype(jnp.bfloat16)
    key_rows = jnp.dot(normed, in_weight[1], preferred_element_type=jnp.float32).astype(jnp.bfloat16)
    value_rows = jnp.dot(normed, in_weight[2], preferred_element_type=jnp.float32).astype(jnp.bfloat16)
    product = key_rows.astype(jnp.float32) * value_rows.astype(jnp.float32)
    padded = jnp.concatenate([jnp.zeros((TAPS - 1, C), jnp.float32), product], axis=0)
    tap_weights = jnp.repeat(filters, GROUP, axis=1)
    filtered = jnp.zeros((TOKENS, C), jnp.float32)
    for offset in range(TAPS):
        filtered = filtered + tap_weights[offset] * padded[TAPS - 1 - offset:TAPS - 1 - offset + TOKENS]
    gated = (query.astype(jnp.float32) * filtered).astype(jnp.bfloat16)
    share = C // N_TP
    mixed = jnp.zeros((TOKENS, D), jnp.float32)
    for index in range(N_TP):
        term = jnp.dot(gated[:, index * share:(index + 1) * share], out_weight[index * share:(index + 1) * share], preferred_element_type=jnp.float32)
        term = lax.optimization_barrier(term.astype(jnp.bfloat16)).astype(jnp.float32)
        mixed = mixed + term
    return (widened + keep_mask.astype(jnp.float32) * mixed * (1.0 / 0.9)).astype(jnp.bfloat16)
```

```python
import math

import jax
import jax.numpy as jnp
from jax import lax
from jax.sharding import PartitionSpec as P

F32 = jnp.float32
BF16 = jnp.bfloat16


def grid_of(chips):
    ny = max(d for d in range(1, math.isqrt(chips) + 1) if chips % d == 0)
    return ny, chips // ny


def on_device(tokens, norm_gain, in_weight, filters, out_weight, keep_mask):
    n_seq, n_tp = lax.axis_size("seq"), lax.axis_size("tp")
    chips = n_seq // 2
    ny, nx = grid_of(chips)
    seq = lax.axis_index("seq")
    core, here = seq % 2, seq // 2
    my_y, my_x = here // nx, here % nx
    rows, model = tokens.shape
    length = rows * n_tp
    deep, channels = in_weight.shape[1:]
    half = channels // 2
    wide = out_weight.shape[1]

    def place(y, x, c):
        return ((y % ny) * nx + x % nx) * 2 + c

    def from_chip(block, dy, dx):
        route = [
            (place(y + dy, x + dx, c), place(y, x, c))
            for y in range(ny)
            for x in range(nx)
            for c in range(2)
        ]
        return lax.ppermute(block, "seq", route)

    def from_partner(block):
        return lax.ppermute(block, "seq", [(s, s ^ 1) for s in range(n_seq)])

    def by_core(mine, other, axis):
        return jnp.where(
            core == 0,
            jnp.concatenate([mine, other], axis=axis),
            jnp.concatenate([other, mine], axis=axis),
        )

    def spread(block):
        cut = block.shape[0] // 2
        along_x = [block] + [from_chip(block, 0, dx) for dx in range(1, nx)]
        along_y = [block] + [from_chip(block, dy, 0) for dy in range(1, ny)]
        found = {(0, dx): [along_x[dx]] for dx in range(nx)}
        found.update({(dy, 0): [along_y[dy]] for dy in range(1, ny)})
        for dy in range(1, ny):
            for dx in range(1, nx):
                found[dy, dx] = [
                    from_chip(along_x[dx][:cut], dy, 0),
                    from_chip(along_y[dy][cut:], 0, dx),
                ]
        return found

    def turned(array, sign):
        parts = array.reshape(array.shape[0], ny, nx, -1)
        parts = jnp.roll(parts, (sign * my_y, sign * my_x), axis=(1, 2))
        return parts.reshape(array.shape)

    widened = tokens.astype(F32)
    mean_sq = jnp.mean(widened * widened, axis=1, keepdims=True)
    normed = (widened * lax.rsqrt(mean_sq + 1e-06) * norm_gain).astype(BF16)
    own_rows = lax.all_gather(turned(normed, -1), "tp", axis=0, tiled=True)
    other_rows = from_partner(own_rows)

    mine = lax.dynamic_slice_in_dim(in_weight, core * half, half, axis=2)
    away = lax.dynamic_slice_in_dim(in_weight, (1 - core) * half, half, axis=2)
    brought = from_partner(away)
    projected = {}
    for index in (1, 2, 0):
        chip_block = by_core(mine[index], brought[index], 0)
        found = spread(chip_block)
        totals = [jnp.zeros((length, half), F32)] * 2
        for (dy, dx), pieces in found.items():
            at = (dy * nx + dx) * 2 * deep
            for piece in pieces:
                depth = piece.shape[0]
                totals = [
                    total
                    + jnp.dot(
                        block[:, at : at + depth], piece, preferred_element_type=F32
                    )
                    for total, block in zip(totals, (own_rows, other_rows))
                ]
                at += depth
        projected[index] = by_core(totals[0].astype(BF16), totals[1].astype(BF16), 0)
    query, key, value = projected[0], projected[1], projected[2]

    reach = filters.shape[0] - 1
    groups = filters.shape[1] // 2
    product = key.astype(F32) * value.astype(F32)
    tail = product[2 * length - reach :]
    rim = lax.ppermute(
        tail, "seq", [(2 * i + c, 2 * i + 2 + c) for i in range(chips - 1) for c in range(2)]
    )
    product = jnp.concatenate([rim, product], axis=0)
    taps = jnp.repeat(
        lax.dynamic_slice_in_dim(filters, core * groups, groups, axis=1), half // groups, axis=1
    )
    filtered = jnp.zeros((2 * length, half), F32)
    for offset in range(reach + 1):
        filtered = filtered + taps[offset] * product[reach - offset : reach - offset + 2 * length]
    gated = (query.astype(F32) * filtered).astype(BF16)

    stays = lax.dynamic_slice_in_dim(gated, core * length, length, axis=0)
    leaves = lax.dynamic_slice_in_dim(gated, (1 - core) * length, length, axis=0)
    gated = by_core(stays, from_partner(leaves), 1)

    out_found = spread(out_weight)
    position = lax.axis_index("tp")
    up = [(i, i + 1) for i in range(n_tp - 1)]
    down = [(i + 1, i) for i in range(n_tp - 1)]

    def summed(terms):
        terms = terms.reshape(n_tp, rows, -1)

        def rows_of(where):
            where = jnp.clip(where, 0, n_tp - 1)
            return lax.dynamic_index_in_dim(terms, where, 0, keepdims=False)

        rising = falling = None
        for step in range(n_tp - 1):
            ahead = n_tp - 1 - step
            send_up, send_down = rows_of(position + ahead), rows_of(position - ahead)
            if step:
                send_up = (send_up.astype(F32) + rising.astype(F32)).astype(BF16)
                send_down = (send_down.astype(F32) + falling.astype(F32)).astype(BF16)
            rising = lax.ppermute(send_up, "tp", up)
            falling = lax.ppermute(send_down, "tp", down)
        total = rows_of(position).astype(F32)
        return total + rising.astype(F32) + falling.astype(F32)

    result = jnp.zeros((rows, model), BF16)
    for (dy, dx), pieces in out_found.items():
        sides = []
        for side in (pieces, [from_partner(piece) for piece in pieces]):
            total, at = 0.0, 0
            for piece in side:
                depth = piece.shape[0]
                total = total + jnp.dot(
                    gated[:, at : at + depth], piece, preferred_element_type=F32
                )
                at += depth
            sides.append(total.astype(BF16))
        mixed = summed(by_core(sides[0], sides[1], 1))
        chip = ((my_y + dy) % ny) * nx + (my_x + dx) % nx
        at = chip * 2 * wide
        kept = lax.dynamic_slice_in_dim(keep_mask, at, 2 * wide, axis=1).astype(F32)
        base = lax.dynamic_slice_in_dim(tokens, at, 2 * wide, axis=1).astype(F32)
        part = (base + kept * mixed * (1.0 / 0.9)).astype(BF16)
        result = lax.dynamic_update_slice_in_dim(result, part, at, axis=1)
    return result


def solution(mesh):
    in_specs = (
        P(("seq", "tp"), None),
        P(),
        P(None, "seq", "tp"),
        P(None, "tp"),
        P("tp", "seq"),
        P(("seq", "tp"), None),
    )
    out_specs = P(("seq", "tp"), None)
    return jax.shard_map(
        on_device, mesh=mesh, in_specs=in_specs, out_specs=out_specs, check_vma=False
    )
```

```python
import functools
import math

import jax
import jax.numpy as jnp
from jax import lax
from jax.experimental import pallas as pl
from jax.experimental.pallas import tpu as pltpu
from jax.sharding import PartitionSpec as P

F32 = jnp.float32
BF16 = jnp.bfloat16
MIB = 1 << 20
WHOLE = pl.BlockSpec(memory_space=pltpu.VMEM)


def grid_of(chips):
    ny = max(d for d in range(1, math.isqrt(chips) + 1) if chips % d == 0)
    return ny, chips // ny


def dot(a, b):
    return jnp.dot(a, b, preferred_element_type=F32)


def cost(flops, *arrays):
    moved = sum(math.prod(a.shape) * a.dtype.itemsize for a in arrays)
    return pl.CostEstimate(flops=flops, bytes_accessed=moved, transcendentals=0)


def columns_of(x_ref, at_ref, index, deep):
    return x_ref[:, pl.ds(pl.multiple_of(at_ref[index], deep), deep)]


def product_kernel(at_ref, x_ref, *refs):
    pieces, out_ref = refs[:-1], refs[-1]
    deep = pieces[0].shape[1]
    key = value = None
    for index, piece in enumerate(pieces):
        x = columns_of(x_ref, at_ref, index, deep)
        new_key, new_value = dot(x, piece[0]), dot(x, piece[1])
        key = new_key if key is None else key + new_key
        value = new_value if value is None else value + new_value
    out_ref[...] = key.astype(BF16).astype(F32) * value.astype(BF16).astype(F32)


def gate_kernel(at_ref, x_ref, filtered_ref, *refs):
    pieces, out_ref = refs[:-1], refs[-1]
    deep = pieces[0].shape[0]
    query = None
    for index, piece in enumerate(pieces):
        new = dot(columns_of(x_ref, at_ref, index, deep), piece[...])
        query = new if query is None else query + new
    out_ref[...] = (query.astype(BF16).astype(F32) * filtered_ref[...]).astype(BF16)


def project(kernel, at, x, extra, pieces, out_dtype):
    length, model = x.shape
    half = pieces[0].shape[-1]
    tile = math.gcd(half, 256)
    lead = pieces[0].shape[:-1]
    count = 2 if len(lead) == 2 else 1
    out = jax.ShapeDtypeStruct((length, half), out_dtype)
    by_tile = pl.BlockSpec((length, tile), lambda j, at: (0, j))
    return pl.pallas_call(
        kernel,
        out_shape=out,
        grid_spec=pltpu.PrefetchScalarGridSpec(
            num_scalar_prefetch=1,
            grid=(half // tile,),
            in_specs=[pl.BlockSpec((length, model), lambda j, at: (0, 0))]
            + [by_tile] * len(extra)
            + [
                pl.BlockSpec(lead + (tile,), lambda j, at: (0,) * len(lead) + (j,))
                for _ in pieces
            ],
            out_specs=by_tile,
        ),
        compiler_params=pltpu.CompilerParams(vmem_limit_bytes=36 * MIB),
        cost_estimate=cost(2 * count * length * model * half, x, out, *extra, *pieces),
    )(at, x, *extra, *pieces)


def filter_kernel(product_ref, halo_ref, taps_ref, out_ref, held):
    length, pad = product_ref.shape[0], halo_ref.shape[0]
    held[:pad] = halo_ref[...]
    held[pad:] = product_ref[...]
    total = None
    for offset in range(taps_ref.shape[0]):
        term = taps_ref[offset : offset + 1] * held[pad - offset : pad - offset + length]
        total = term if total is None else total + term
    out_ref[...] = total


def causal_filter(product, halo, taps):
    length, half = product.shape
    pad = halo.shape[0]
    tile = math.gcd(half, 256)
    return pl.pallas_call(
        filter_kernel,
        out_shape=jax.ShapeDtypeStruct(product.shape, F32),
        grid=(half // tile,),
        in_specs=[
            pl.BlockSpec((rows, tile), lambda j: (0, j)) for rows in (length, pad, taps.shape[0])
        ],
        out_specs=pl.BlockSpec((length, tile), lambda j: (0, j)),
        scratch_shapes=[pltpu.VMEM((pad + length, tile), F32)],
        compiler_params=pltpu.CompilerParams(vmem_limit_bytes=16 * MIB),
        cost_estimate=cost(14 * length * half, product, product),
    )(product, halo, taps)


def terms_kernel(count, n_tp, z_ref, gated_ref, *refs):
    pieces, refs = refs[:count], refs[count:]
    given, outs, held = (refs[0], refs[1:-1], refs[-1]) if len(refs) > 2 else (None, refs[:1], refs[-1])
    length = gated_ref.shape[0]
    rows = length // n_tp
    for slot in range(n_tp):
        owner = lax.rem(z_ref[0] + slot, n_tp)
        held[slot * rows : (slot + 1) * rows] = gated_ref[
            pl.ds(pl.multiple_of(owner * rows, rows), rows)
        ]
    wide = pieces[0].shape[1]
    for index, piece in enumerate(pieces):
        at = slice(index * wide, (index + 1) * wide)
        total = dot(held[...], piece[...])
        if given is None:
            outs[0][:, at] = total.astype(BF16)
        else:
            total = total + given[:, at].astype(F32)
            for slot in range(n_tp):
                outs[slot][:, at] = total[slot * rows : (slot + 1) * rows].astype(BF16)


def terms(n_tp, z, gated, pieces, given=None):
    length, half = gated.shape
    cols = len(pieces) * pieces[0].shape[1]
    if given is None:
        out = [jax.ShapeDtypeStruct((length, cols), BF16)]
    else:
        out = [jax.ShapeDtypeStruct((length // n_tp, cols), BF16)] * n_tp
    extra = [] if given is None else [given]
    result = pl.pallas_call(
        functools.partial(terms_kernel, len(pieces), n_tp),
        out_shape=out,
        in_specs=[pl.BlockSpec(memory_space=pltpu.SMEM)]
        + [WHOLE] * (1 + len(pieces) + len(extra)),
        out_specs=[WHOLE] * len(out),
        scratch_shapes=[pltpu.VMEM((length, half), BF16)],
        compiler_params=pltpu.CompilerParams(vmem_limit_bytes=36 * MIB),
        cost_estimate=cost(2 * length * half * cols, gated, *pieces, *extra, *out),
    )(z, gated, *pieces, *extra)
    return result[0] if given is None else result


def on_device(tokens, norm_gain, in_weight, filters, out_weight, keep_mask):
    n_seq, n_tp = lax.axis_size("seq"), lax.axis_size("tp")
    chips = n_seq // 2
    ny, nx = grid_of(chips)
    seq = lax.axis_index("seq")
    core, here = seq % 2, seq // 2
    my_y, my_x = here // nx, here % nx
    rows, model = tokens.shape
    length = rows * n_tp
    deep, channels = in_weight.shape[1:]
    half = channels // 2
    wide = out_weight.shape[1]

    def place(y, x, c):
        return ((y % ny) * nx + x % nx) * 2 + c

    def from_chip(block, dy, dx):
        route = [
            (place(y + dy, x + dx, c), place(y, x, c))
            for y in range(ny)
            for x in range(nx)
            for c in range(2)
        ]
        return lax.ppermute(block, "seq", route)

    def from_partner(block):
        return lax.ppermute(block, "seq", [(s, s ^ 1) for s in range(n_seq)])

    def direct(mine, brought):
        along_x = [(mine, brought)]
        along_y = [(mine, brought)]
        along_x += [tuple(from_chip(b, 0, dx) for b in (mine, brought)) for dx in range(1, nx)]
        along_y += [tuple(from_chip(b, dy, 0) for b in (mine, brought)) for dy in range(1, ny)]
        return along_x, along_y

    def onward(along_x, along_y):
        return {
            (dy, dx): (from_chip(along_x[dx][0], dy, 0), from_chip(along_y[dy][1], 0, dx))
            for dy in range(1, ny)
            for dx in range(1, nx)
        }

    def listed(along_x, along_y, rest):
        found = {(0, dx): pair for dx, pair in enumerate(along_x)}
        found.update({(dy, 0): pair for dy, pair in enumerate(along_y)})
        found.update(rest)
        return found

    def halves(array, axis, at):
        size = array.shape[axis] // 2
        return lax.dynamic_slice_in_dim(array, at * size, size, axis=axis)

    def columns(array, first, count, at):
        return lax.dynamic_slice(array, (first, 0, at * half), (count, deep, half))

    mine_kv = columns(in_weight, 1, 2, core)
    away_kv = columns(in_weight, 1, 2, 1 - core)
    brought_kv = from_partner(away_kv)
    kv_x, kv_y = direct(mine_kv, brought_kv)

    tokens_then, _ = lax.optimization_barrier((tokens, away_kv))
    widened = tokens_then.astype(F32)
    mean_sq = jnp.mean(widened * widened, axis=1, keepdims=True)
    normed = (widened * lax.rsqrt(mean_sq + 1e-06) * norm_gain).astype(BF16)
    own_rows = lax.all_gather(normed, "tp", axis=0, tiled=True)
    in_weight_then, out_weight_then, _ = lax.optimization_barrier((in_weight, out_weight, normed))
    mine_q = columns(in_weight_then, 0, 1, core)[0]
    brought_q = from_partner(columns(in_weight_then, 0, 1, 1 - core)[0])
    mine_o = halves(out_weight_then, 0, core)
    brought_o = from_partner(halves(out_weight_then, 0, 1 - core))

    kv_rest = onward(kv_x, kv_y)
    mine_q, brought_q, _ = lax.optimization_barrier((mine_q, brought_q, (kv_x[1:], kv_y[1:])))
    q_x, q_y = direct(mine_q, brought_q)
    q_x, q_y, kv_rest = lax.optimization_barrier((q_x, q_y, kv_rest))
    q_rest = onward(q_x, q_y)
    mine_o, brought_o, _ = lax.optimization_barrier((mine_o, brought_o, q_rest))
    o_x, o_y = direct(mine_o, brought_o)
    o_rest = onward(o_x, o_y)

    own_rows, _ = lax.optimization_barrier((own_rows, kv_rest))
    other_rows = from_partner(own_rows)
    kv = listed(kv_x, kv_y, kv_rest)
    q = listed(q_x, q_y, q_rest)
    order = list(kv)
    at = jnp.stack(
        [place(my_y + dy, my_x + dx, core ^ rc) * deep for dy, dx in order for rc in range(2)]
    ).astype(jnp.int32)
    kv_pieces = [piece for key in order for piece in kv[key]]
    q_pieces = [piece for key in order for piece in q[key]]

    reach = filters.shape[0] - 1
    pad = -(-reach // 8) * 8
    own_product = project(product_kernel, at, own_rows, [], kv_pieces, F32)
    other_product = project(product_kernel, at, other_rows, [], kv_pieces, F32)
    own_tail, other_tail = own_product[length - pad :], other_product[length - pad :]
    first_tail = jnp.where(core == 0, own_tail, other_tail)
    last_tail = jnp.where(core == 0, other_tail, own_tail)
    rim = lax.ppermute(
        last_tail,
        "seq",
        [(2 * i + c, 2 * i + 2 + c) for i in range(chips - 1) for c in range(2)],
    )
    groups = filters.shape[1] // 2
    taps = jnp.repeat(
        lax.dynamic_slice_in_dim(filters, core * groups, groups, axis=1), half // groups, axis=1
    )
    own_filtered = causal_filter(own_product, jnp.where(core == 0, rim, first_tail), taps)
    other_filtered = causal_filter(other_product, jnp.where(core == 0, first_tail, rim), taps)
    other_gated = project(gate_kernel, at, other_rows, [other_filtered], q_pieces, BF16)
    own_gated = project(gate_kernel, at, own_rows, [own_filtered], q_pieces, BF16)

    position = lax.axis_index("tp")
    z = position.astype(jnp.int32).reshape(1)
    up = [(i, i + 1) for i in range(n_tp - 1)]
    down = [(i + 1, i) for i in range(n_tp - 1)]

    def plus(a, b):
        return (a.astype(F32) + b.astype(F32)).astype(BF16)

    def summed(pairs, own_gated, other_gated):
        pieces = [piece for pair in pairs for piece in pair]
        leaving = terms(n_tp, z, other_gated, [piece for pair in pairs for piece in pair[::-1]])
        slots = terms(n_tp, z, own_gated, pieces, from_partner(leaving))
        rising = falling = None
        for step in range(n_tp - 1):
            send_up, send_down = slots[n_tp - 1 - step], slots[step + 1]
            if step:
                send_up, send_down = plus(send_up, rising), plus(send_down, falling)
            rising = lax.ppermute(send_up, "tp", up)
            falling = lax.ppermute(send_down, "tp", down)
        return slots[0].astype(F32) + rising.astype(F32) + falling.astype(F32), slots[0]

    groups_of = [[(0, 0)], [key for key in order if (key[0] == 0) != (key[1] == 0)], list(o_rest)]
    out_pieces = listed(o_x, o_y, o_rest)
    result = jnp.zeros((rows, model), BF16)
    for keys in groups_of:
        mixed, done = summed([out_pieces[key] for key in keys], own_gated, other_gated)
        own_gated, other_gated, _ = lax.optimization_barrier((own_gated, other_gated, done))
        for index, (dy, dx) in enumerate(keys):
            start = place(my_y + dy, my_x + dx, 0) * wide
            pair = mixed[:, index * 2 * wide : (index + 1) * 2 * wide]
            swapped = jnp.concatenate([pair[:, wide:], pair[:, :wide]], axis=1)
            kept = lax.dynamic_slice_in_dim(keep_mask, start, 2 * wide, axis=1).astype(F32)
            base = lax.dynamic_slice_in_dim(tokens, start, 2 * wide, axis=1).astype(F32)
            pair = jnp.where(core == 0, pair, swapped)
            part = (base + kept * pair * (1.0 / 0.9)).astype(BF16)
            result = lax.dynamic_update_slice_in_dim(result, part, start, axis=1)
    return result


def solution(mesh):
    in_specs = (
        P(("seq", "tp"), None),
        P(),
        P(None, "seq", "tp"),
        P(None, "tp"),
        P("tp", "seq"),
        P(("seq", "tp"), None),
    )
    out_specs = P(("seq", "tp"), None)
    return jax.shard_map(
        on_device, mesh=mesh, in_specs=in_specs, out_specs=out_specs, check_vma=False
    )
```

```python
import functools
import math

import jax
import jax.numpy as jnp
from jax import lax
from jax.experimental import pallas as pl
from jax.experimental.pallas import tpu as pltpu
from jax.sharding import PartitionSpec as P

F32 = jnp.float32
BF16 = jnp.bfloat16
GRANT = 58 << 20


def grid_of(chips):
    ny = max(d for d in range(1, math.isqrt(chips) + 1) if chips % d == 0)
    return ny, chips // ny


def whole(array):
    return pl.BlockSpec(array.shape, lambda *_: (0,) * len(array.shape))


def dot(a, b):
    return jnp.dot(a, b, preferred_element_type=F32)


def cost(flops, *arrays):
    moved = sum(math.prod(a.shape) * a.dtype.itemsize for a in arrays)
    return pl.CostEstimate(flops=1, bytes_accessed=1, transcendentals=0)


def columns_of(x_ref, at_ref, index, deep):
    return x_ref[:, pl.ds(pl.multiple_of(at_ref[index], deep), deep)]


def product_kernel(at_ref, x_ref, *refs):
    pieces, out_ref = refs[:-1], refs[-1]
    deep = pieces[0].shape[1]
    key = value = None
    for index, piece in enumerate(pieces):
        x = columns_of(x_ref, at_ref, index, deep)
        new_key, new_value = dot(x, piece[0]), dot(x, piece[1])
        key = new_key if key is None else key + new_key
        value = new_value if value is None else value + new_value
    out_ref[...] = key.astype(BF16).astype(F32) * value.astype(BF16).astype(F32)


def query_kernel(at_ref, x_ref, *refs):
    pairs, out_ref = refs[:-1], refs[-1]
    deep = pairs[0].shape[1]
    query = None
    for index in range(2 * len(pairs)):
        new = dot(columns_of(x_ref, at_ref, index, deep), pairs[index // 2][index % 2])
        query = new if query is None else query + new
    out_ref[...] = query


def gate_kernel(at_ref, x_ref, filtered_ref, partial_ref, *refs):
    pieces, out_ref = refs[:-1], refs[-1]
    deep = pieces[0].shape[0]
    query = partial_ref[...]
    for index, piece in enumerate(pieces):
        query = query + dot(columns_of(x_ref, at_ref, index, deep), piece[...])
    out_ref[...] = (query.astype(BF16).astype(F32) * filtered_ref[...]).astype(BF16)


def project(kernel, at, x, extra, pieces, out_dtype):
    length, model = x.shape
    half = pieces[0].shape[-1]
    tile = math.gcd(half, 256)
    lead = pieces[0].shape[:-1]
    count = 2 if len(lead) == 2 else 1
    out = jax.ShapeDtypeStruct((length, half), out_dtype)
    by_tile = pl.BlockSpec((length, tile), lambda j, at: (0, j))
    return pl.pallas_call(
        kernel,
        out_shape=out,
        grid_spec=pltpu.PrefetchScalarGridSpec(
            num_scalar_prefetch=1,
            grid=(half // tile,),
            in_specs=[pl.BlockSpec((length, model), lambda j, at: (0, 0))]
            + [by_tile] * len(extra)
            + [
                pl.BlockSpec(lead + (tile,), lambda j, at: (0,) * len(lead) + (j,))
                for _ in pieces
            ],
            out_specs=by_tile,
        ),
        compiler_params=pltpu.CompilerParams(vmem_limit_bytes=GRANT),
        cost_estimate=cost(2 * count * length * model * half, x, out, *extra, *pieces),
    )(at, x, *extra, *pieces)


def filter_kernel(product_ref, halo_ref, taps_ref, out_ref, held):
    length, pad = product_ref.shape[0], halo_ref.shape[0]
    held[:pad] = halo_ref[...]
    held[pad:] = product_ref[...]
    total = None
    for offset in range(taps_ref.shape[0]):
        term = taps_ref[offset : offset + 1] * held[pad - offset : pad - offset + length]
        total = term if total is None else total + term
    out_ref[...] = total


def causal_filter(product, halo, taps):
    length, half = product.shape
    pad = halo.shape[0]
    tile = math.gcd(half, 256)
    return pl.pallas_call(
        filter_kernel,
        out_shape=jax.ShapeDtypeStruct(product.shape, F32),
        grid=(half // tile,),
        in_specs=[
            pl.BlockSpec((rows, tile), lambda j: (0, j)) for rows in (length, pad, taps.shape[0])
        ],
        out_specs=pl.BlockSpec((length, tile), lambda j: (0, j)),
        scratch_shapes=[pltpu.VMEM((pad + length, tile), F32)],
        compiler_params=pltpu.CompilerParams(vmem_limit_bytes=GRANT),
        cost_estimate=cost(14 * length * half, product, product),
    )(product, halo, taps)


def terms_kernel(count, order, n_tp, z_ref, gated_ref, *refs):
    pairs, refs, held = refs[:count], refs[count:-1], refs[-1]
    given, outs = (refs[0], refs[1:]) if len(refs) > 1 else (None, refs)
    length = gated_ref.shape[0]
    rows = length // n_tp
    for slot in range(n_tp):
        owner = lax.rem(z_ref[0] + slot, n_tp)
        held[slot * rows : (slot + 1) * rows] = gated_ref[
            pl.ds(pl.multiple_of(owner * rows, rows), rows)
        ]
    wide = pairs[0].shape[2]
    for index, (pair, side) in enumerate((p, s) for p in pairs for s in order):
        at = slice(index * wide, (index + 1) * wide)
        total = dot(held[...], pair[side])
        if given is None:
            outs[0][:, at] = total.astype(BF16)
        else:
            total = total + given[:, at].astype(F32)
            for slot in range(n_tp):
                outs[slot][:, at] = total[slot * rows : (slot + 1) * rows].astype(BF16)


def terms(n_tp, z, gated, pairs, order, given=None):
    length, half = gated.shape
    cols = len(pairs) * 2 * pairs[0].shape[2]
    if given is None:
        out = [jax.ShapeDtypeStruct((length, cols), BF16)]
    else:
        out = [jax.ShapeDtypeStruct((length // n_tp, cols), BF16)] * n_tp
    extra = [] if given is None else [given]
    result = pl.pallas_call(
        functools.partial(terms_kernel, len(pairs), order, n_tp),
        out_shape=out,
        grid=(1,),
        in_specs=[pl.BlockSpec(memory_space=pltpu.SMEM)]
        + [whole(a) for a in (gated, *pairs, *extra)],
        out_specs=[whole(a) for a in out],
        scratch_shapes=[pltpu.VMEM((length, half), BF16)],
        compiler_params=pltpu.CompilerParams(vmem_limit_bytes=GRANT),
        cost_estimate=cost(2 * length * half * cols, gated, *pairs, *extra, *out),
    )(z, gated, *pairs, *extra)
    return result[0] if given is None else result


def on_device(tokens, norm_gain, in_weight, filters, out_weight, keep_mask):
    n_seq, n_tp = lax.axis_size("seq"), lax.axis_size("tp")
    chips = n_seq // 2
    ny, nx = grid_of(chips)
    seq = lax.axis_index("seq")
    core, here = seq % 2, seq // 2
    my_y, my_x = here // nx, here % nx
    rows, model = tokens.shape
    length = rows * n_tp
    deep, channels = in_weight.shape[1:]
    half = channels // 2
    wide = out_weight.shape[1]

    def place(y, x, c):
        return ((y % ny) * nx + x % nx) * 2 + c

    def from_chip(block, dy, dx):
        route = [
            (place(y + dy, x + dx, c), place(y, x, c))
            for y in range(ny)
            for x in range(nx)
            for c in range(2)
        ]
        return lax.ppermute(block, "seq", route)

    def from_partner(block):
        return lax.ppermute(block, "seq", [(s, s ^ 1) for s in range(n_seq)])

    def direct(mine, brought):
        along_x = [(mine, brought)]
        along_y = [(mine, brought)]
        along_x += [tuple(from_chip(b, 0, dx) for b in (mine, brought)) for dx in range(1, nx)]
        along_y += [tuple(from_chip(b, dy, 0) for b in (mine, brought)) for dy in range(1, ny)]
        return along_x, along_y

    def onward(along_x, along_y):
        return {
            (dy, dx): (from_chip(along_x[dx][0], dy, 0), from_chip(along_y[dy][1], 0, dx))
            for dy in range(1, ny)
            for dx in range(1, nx)
        }

    def listed(along_x, along_y, rest):
        found = {(0, dx): pair for dx, pair in enumerate(along_x)}
        found.update({(dy, 0): pair for dy, pair in enumerate(along_y)})
        found.update(rest)
        return found

    def halves(array, axis, at):
        size = array.shape[axis] // 2
        return lax.dynamic_slice_in_dim(array, at * size, size, axis=axis)

    def columns(array, first, count, at):
        return lax.dynamic_slice(array, (first, 0, at * half), (count, deep, half))

    mine_kv = columns(in_weight, 1, 2, core)
    away_kv = columns(in_weight, 1, 2, 1 - core)
    brought_kv = from_partner(away_kv)
    kv_x, kv_y = direct(mine_kv, brought_kv)

    tokens_then, _ = lax.optimization_barrier((tokens, away_kv))
    widened = tokens_then.astype(F32)
    mean_sq = jnp.mean(widened * widened, axis=1, keepdims=True)
    normed = (widened * lax.rsqrt(mean_sq + 1e-06) * norm_gain).astype(BF16)
    own_rows = lax.all_gather(normed, "tp", axis=0, tiled=True)
    in_weight_then, out_weight_then, _ = lax.optimization_barrier((in_weight, out_weight, normed))
    mine_q = columns(in_weight_then, 0, 1, core)[0]
    both_q = jnp.stack([mine_q, from_partner(columns(in_weight_then, 0, 1, 1 - core)[0])])
    mine_o = halves(out_weight_then, 0, core)
    both_o = jnp.stack([mine_o, from_partner(halves(out_weight_then, 0, 1 - core))])

    kv_x, kv_y, both_q = lax.optimization_barrier((kv_x, kv_y, both_q))
    kv_rest = onward(kv_x, kv_y)
    q_x = {(0, dx): from_chip(both_q, 0, dx) for dx in range(1, nx)}
    q_y = {(dy, 0): from_chip(both_q, dy, 0) for dy in range(1, ny)}
    arrived = (kv_x, kv_y, kv_rest, q_x, q_y)
    own_rows, arrived = lax.optimization_barrier((own_rows, arrived))
    kv_x, kv_y, kv_rest, q_x, q_y = arrived
    kv = listed(kv_x, kv_y, kv_rest)
    order = list(kv)
    kv_pieces = [piece for key in order for piece in kv[key]]
    at = jnp.stack(
        [place(my_y + dy, my_x + dx, core ^ rc) * deep for dy, dx in order for rc in range(2)]
    ).astype(jnp.int32)
    early = 2 * (ny + nx - 1)

    other_rows = from_partner(own_rows)
    own_product = project(product_kernel, at, own_rows, [], kv_pieces, F32)
    q_rest = {
        (dy, dx): (from_chip(q_x[0, dx][0], dy, 0), from_chip(q_y[dy, 0][1], 0, dx))
        for dy, _ in q_y
        for _, dx in q_x
    }
    q_pairs = {(0, 0): both_q, **q_x, **q_y}
    q_early = [q_pairs[key] for key in order if key in q_pairs]
    other_product = project(product_kernel, at, other_rows, [], kv_pieces, F32)

    reach = filters.shape[0] - 1
    pad = -(-reach // 8) * 8
    own_tail, other_tail = own_product[length - pad :], other_product[length - pad :]
    first_tail = jnp.where(core == 0, own_tail, other_tail)
    last_tail = jnp.where(core == 0, other_tail, own_tail)
    rim = lax.ppermute(
        last_tail,
        "seq",
        [(2 * i + c, 2 * i + 2 + c) for i in range(chips - 1) for c in range(2)],
    )
    other_query = project(query_kernel, at, other_rows, [], q_early, F32)
    own_query = project(query_kernel, at, own_rows, [], q_early, F32)
    groups = filters.shape[1] // 2
    taps = jnp.repeat(
        lax.dynamic_slice_in_dim(filters, core * groups, groups, axis=1), half // groups, axis=1
    )
    own_filtered = causal_filter(own_product, jnp.where(core == 0, rim, first_tail), taps)
    other_filtered = causal_filter(other_product, jnp.where(core == 0, first_tail, rim), taps)

    ready = (own_filtered, other_filtered, own_query, other_query)
    both_o, q_rest, ready = lax.optimization_barrier((both_o, q_rest, ready))
    own_filtered, other_filtered, own_query, other_query = ready
    o_x = {(0, dx): from_chip(both_o, 0, dx) for dx in range(1, nx)}
    o_y = {(dy, 0): from_chip(both_o, dy, 0) for dy in range(1, ny)}
    late = [piece for pair in q_rest.values() for piece in pair]
    other_gated = project(
        gate_kernel, at[early:], other_rows, [other_filtered, other_query], late, BF16
    )
    own_gated = project(gate_kernel, at[early:], own_rows, [own_filtered, own_query], late, BF16)

    position = lax.axis_index("tp")
    z = position.astype(jnp.int32).reshape(1)
    up = [(i, i + 1) for i in range(n_tp - 1)]
    down = [(i + 1, i) for i in range(n_tp - 1)]

    def plus(a, b):
        return (a.astype(F32) + b.astype(F32)).astype(BF16)

    def summed(pairs, own_gated, other_gated):
        leaving = terms(n_tp, z, other_gated, pairs, (1, 0))
        slots = terms(n_tp, z, own_gated, pairs, (0, 1), from_partner(leaving))
        rising = falling = first = None
        for step in range(n_tp - 1):
            send_up, send_down = slots[n_tp - 1 - step], slots[step + 1]
            if step:
                send_up, send_down = plus(send_up, rising), plus(send_down, falling)
            rising = lax.ppermute(send_up, "tp", up)
            falling = lax.ppermute(send_down, "tp", down)
            first = (rising, falling) if step == 0 else first
        return slots[0].astype(F32) + rising.astype(F32) + falling.astype(F32), first

    o_rest = {(dy, dx): from_chip(o_x[0, dx], dy, 0) for dy, _ in o_y for _, dx in o_x}
    out_pairs = {(0, 0): both_o, **o_x, **o_y, **o_rest}
    result = jnp.zeros((rows, model), BF16)
    for keys in ([(0, 0)], [*o_x, *o_y], list(o_rest)):
        mixed, done = summed([out_pairs[key] for key in keys], own_gated, other_gated)
        own_gated, other_gated, _ = lax.optimization_barrier((own_gated, other_gated, done))
        for index, (dy, dx) in enumerate(keys):
            start = place(my_y + dy, my_x + dx, 0) * wide
            pair = mixed[:, index * 2 * wide : (index + 1) * 2 * wide]
            swapped = jnp.concatenate([pair[:, wide:], pair[:, :wide]], axis=1)
            kept = lax.dynamic_slice_in_dim(keep_mask, start, 2 * wide, axis=1).astype(F32)
            base = lax.dynamic_slice_in_dim(tokens, start, 2 * wide, axis=1).astype(F32)
            pair = jnp.where(core == 0, pair, swapped)
            part = (base + kept * pair * (1.0 / 0.9)).astype(BF16)
            result = lax.dynamic_update_slice_in_dim(result, part, start, axis=1)
    return result


def solution(mesh):
    in_specs = (
        P(("seq", "tp"), None),
        P(),
        P(None, "seq", "tp"),
        P(None, "tp"),
        P("tp", "seq"),
        P(("seq", "tp"), None),
    )
    out_specs = P(("seq", "tp"), None)
    return jax.shard_map(
        on_device, mesh=mesh, in_specs=in_specs, out_specs=out_specs, check_vma=False
    )
```

```python
import functools
import math

import jax
import jax.numpy as jnp
from jax import lax
from jax.experimental import pallas as pl
from jax.experimental.pallas import tpu as pltpu
from jax.sharding import PartitionSpec as P

F32 = jnp.float32
BF16 = jnp.bfloat16
GRANT = 16 << 20
WHOLE = pl.BlockSpec(memory_space=pltpu.VMEM)


def grid_of(chips):
    ny = max(d for d in range(1, math.isqrt(chips) + 1) if chips % d == 0)
    return ny, chips // ny


def dot(a, b):
    return jnp.dot(a, b, preferred_element_type=F32)


def columns_of(x_ref, at_ref, index, deep):
    return x_ref[:, pl.ds(pl.multiple_of(at_ref[index], deep), deep)]


def tiles_of(out_ref):
    tile = math.gcd(out_ref.shape[1], 256)
    return [slice(at, at + tile) for at in range(0, out_ref.shape[1], tile)]


def product_kernel(at_ref, x_ref, *refs):
    pieces, out_ref = refs[:-1], refs[-1]
    deep = pieces[0].shape[1]
    for tile in tiles_of(out_ref):
        key = value = None
        for index, piece in enumerate(pieces):
            x = columns_of(x_ref, at_ref, index, deep)
            new_key, new_value = dot(x, piece[0, :, tile]), dot(x, piece[1, :, tile])
            key = new_key if key is None else key + new_key
            value = new_value if value is None else value + new_value
        out_ref[:, tile] = key.astype(BF16).astype(F32) * value.astype(BF16).astype(F32)


def query_kernel(at_ref, x_ref, *refs):
    pairs, out_ref = refs[:-1], refs[-1]
    deep = pairs[0].shape[1]
    for tile in tiles_of(out_ref):
        query = None
        for index in range(2 * len(pairs)):
            x = columns_of(x_ref, at_ref, index, deep)
            new = dot(x, pairs[index // 2][index % 2, :, tile])
            query = new if query is None else query + new
        out_ref[:, tile] = query


def gate_kernel(at_ref, x_ref, filtered_ref, partial_ref, *refs):
    pieces, out_ref = refs[:-1], refs[-1]
    deep = pieces[0].shape[0]
    for tile in tiles_of(out_ref):
        query = partial_ref[:, tile]
        for index, piece in enumerate(pieces):
            query = query + dot(columns_of(x_ref, at_ref, index, deep), piece[:, tile])
        out_ref[:, tile] = (query.astype(BF16).astype(F32) * filtered_ref[:, tile]).astype(BF16)


def call(kernel, scalars, operands, out, scratch=()):
    return pl.pallas_call(
        kernel,
        out_shape=out,
        in_specs=[pl.BlockSpec(memory_space=pltpu.SMEM)] + [WHOLE] * len(operands),
        out_specs=jax.tree.map(lambda _: WHOLE, out),
        scratch_shapes=scratch,
        compiler_params=pltpu.CompilerParams(vmem_limit_bytes=GRANT),
        cost_estimate=pl.CostEstimate(flops=1, bytes_accessed=1, transcendentals=0),
    )(scalars, *operands)


def project(kernel, at, x, extra, pieces, out_dtype):
    half = pieces[0].shape[-1]
    out = jax.ShapeDtypeStruct((x.shape[0], half), out_dtype)
    return call(kernel, at, (x, *extra, *pieces), out)


def filter_kernel(_, product_ref, halo_ref, taps_ref, out_ref, held):
    length, pad = product_ref.shape[0], halo_ref.shape[0]
    held[:pad] = halo_ref[...]
    held[pad:] = product_ref[...]
    for tile in tiles_of(out_ref):
        total = None
        for offset in range(taps_ref.shape[0]):
            term = taps_ref[offset : offset + 1, tile] * held[pad - offset : pad - offset + length, tile]
            total = term if total is None else total + term
        out_ref[:, tile] = total


def causal_filter(at, product, halo, taps):
    length, half = product.shape
    out = jax.ShapeDtypeStruct(product.shape, F32)
    scratch = [pltpu.VMEM((halo.shape[0] + length, half), F32)]
    return call(filter_kernel, at, (product, halo, taps), out, scratch)


def terms_kernel(count, order, turned, n_tp, z_ref, gated_ref, *refs):
    pairs, refs = refs[:count], refs[count:]
    length = gated_ref.shape[0]
    rows = length // n_tp
    held = gated_ref
    if turned:
        refs, held = refs[:-1], refs[-1]
        for slot in range(n_tp):
            owner = lax.rem(z_ref[0] + slot, n_tp)
            held[slot * rows : (slot + 1) * rows] = gated_ref[
                pl.ds(pl.multiple_of(owner * rows, rows), rows)
            ]
    given, outs = (refs[0], refs[1:]) if len(refs) > 1 else (None, refs)
    wide = pairs[0].shape[2]
    for index, (pair, side) in enumerate((p, s) for p in pairs for s in order):
        at = slice(index * wide, (index + 1) * wide)
        total = dot(held[...], pair[side])
        if given is not None:
            total = total + given[:, at].astype(F32)
        share = length // len(outs)
        for slot, out in enumerate(outs):
            out[:, at] = total[slot * share : (slot + 1) * share].astype(BF16)


def terms(n_tp, z, gated, pairs, order, turned, given=None):
    length, half = gated.shape
    cols = len(pairs) * 2 * pairs[0].shape[2]
    slots = n_tp if turned and given is not None else 1
    out = [jax.ShapeDtypeStruct((length // slots, cols), BF16)] * slots
    kernel = functools.partial(terms_kernel, len(pairs), order, turned, n_tp)
    extra = () if given is None else (given,)
    scratch = [pltpu.VMEM((length, half), BF16)] if turned else []
    result = call(kernel, z, (gated, *pairs, *extra), out, scratch)
    return result if slots > 1 else result[0]


def on_device(tokens, norm_gain, in_weight, filters, out_weight, keep_mask):
    n_seq, n_tp = lax.axis_size("seq"), lax.axis_size("tp")
    chips = n_seq // 2
    ny, nx = grid_of(chips)
    seq = lax.axis_index("seq")
    core, here = seq % 2, seq // 2
    my_y, my_x = here // nx, here % nx
    rows, model = tokens.shape
    length = rows * n_tp
    deep, channels = in_weight.shape[1:]
    half = channels // 2
    wide = out_weight.shape[1]

    def place(y, x, c):
        return ((y % ny) * nx + x % nx) * 2 + c

    def from_chip(block, dy, dx):
        route = [
            (place(y + dy, x + dx, c), place(y, x, c))
            for y in range(ny)
            for x in range(nx)
            for c in range(2)
        ]
        return lax.ppermute(block, "seq", route)

    def from_partner(block):
        return lax.ppermute(block, "seq", [(s, s ^ 1) for s in range(n_seq)])

    def direct(mine, brought):
        along_x = [(mine, brought)]
        along_y = [(mine, brought)]
        along_x += [tuple(from_chip(b, 0, dx) for b in (mine, brought)) for dx in range(1, nx)]
        along_y += [tuple(from_chip(b, dy, 0) for b in (mine, brought)) for dy in range(1, ny)]
        return along_x, along_y

    def onward(along_x, along_y):
        return {
            (dy, dx): (from_chip(along_x[dx][0], dy, 0), from_chip(along_y[dy][1], 0, dx))
            for dy in range(1, ny)
            for dx in range(1, nx)
        }

    def listed(along_x, along_y, rest):
        found = {(0, dx): pair for dx, pair in enumerate(along_x)}
        found.update({(dy, 0): pair for dy, pair in enumerate(along_y)})
        found.update(rest)
        return found

    def halves(array, axis, at):
        size = array.shape[axis] // 2
        return lax.dynamic_slice_in_dim(array, at * size, size, axis=axis)

    def columns(array, first, count, at):
        return lax.dynamic_slice(array, (first, 0, at * half), (count, deep, half))

    mine_kv = columns(in_weight, 1, 2, core)
    away_kv = columns(in_weight, 1, 2, 1 - core)
    brought_kv = from_partner(away_kv)
    kv_x, kv_y = direct(mine_kv, brought_kv)

    tokens_then, _ = lax.optimization_barrier((tokens, away_kv))
    widened = tokens_then.astype(F32)
    mean_sq = jnp.mean(widened * widened, axis=1, keepdims=True)
    normed = (widened * lax.rsqrt(mean_sq + 1e-06) * norm_gain).astype(BF16)
    own_rows = lax.all_gather(normed, "tp", axis=0, tiled=True)
    in_weight_then, out_weight_then, _ = lax.optimization_barrier((in_weight, out_weight, normed))
    mine_q = columns(in_weight_then, 0, 1, core)[0]
    both_q = jnp.stack([mine_q, from_partner(columns(in_weight_then, 0, 1, 1 - core)[0])])
    mine_o = halves(out_weight_then, 0, core)
    both_o = jnp.stack([mine_o, from_partner(halves(out_weight_then, 0, 1 - core))])

    kv_x, kv_y, both_q = lax.optimization_barrier((kv_x, kv_y, both_q))
    kv_rest = onward(kv_x, kv_y)
    q_x = {(0, dx): from_chip(both_q, 0, dx) for dx in range(1, nx)}
    q_y = {(dy, 0): from_chip(both_q, dy, 0) for dy in range(1, ny)}
    arrived = (kv_x, kv_y, kv_rest, q_x, q_y)
    own_rows, arrived = lax.optimization_barrier((own_rows, arrived))
    kv_x, kv_y, kv_rest, q_x, q_y = arrived
    kv = listed(kv_x, kv_y, kv_rest)
    order = list(kv)
    kv_pieces = [piece for key in order for piece in kv[key]]
    at = jnp.stack(
        [place(my_y + dy, my_x + dx, core ^ rc) * deep for dy, dx in order for rc in range(2)]
    ).astype(jnp.int32)
    early = 2 * (ny + nx - 1)

    other_rows = from_partner(own_rows)
    own_product = project(product_kernel, at, own_rows, [], kv_pieces, F32)
    q_rest = {
        (dy, dx): (from_chip(q_x[0, dx][0], dy, 0), from_chip(q_y[dy, 0][1], 0, dx))
        for dy, _ in q_y
        for _, dx in q_x
    }
    q_pairs = {(0, 0): both_q, **q_x, **q_y}
    q_early = [q_pairs[key] for key in order if key in q_pairs]
    other_product = project(product_kernel, at, other_rows, [], kv_pieces, F32)

    reach = filters.shape[0] - 1
    pad = -(-reach // 8) * 8
    own_tail, other_tail = own_product[length - pad :], other_product[length - pad :]
    first_tail = jnp.where(core == 0, own_tail, other_tail)
    last_tail = jnp.where(core == 0, other_tail, own_tail)
    rim = lax.ppermute(
        last_tail,
        "seq",
        [(2 * i + c, 2 * i + 2 + c) for i in range(chips - 1) for c in range(2)],
    )
    other_query = project(query_kernel, at, other_rows, [], q_early, F32)
    own_query = project(query_kernel, at, own_rows, [], q_early, F32)
    groups = filters.shape[1] // 2
    taps = jnp.repeat(
        lax.dynamic_slice_in_dim(filters, core * groups, groups, axis=1), half // groups, axis=1
    )
    own_filtered = causal_filter(at, own_product, jnp.where(core == 0, rim, first_tail), taps)
    other_filtered = causal_filter(at, other_product, jnp.where(core == 0, first_tail, rim), taps)

    ready = (own_filtered, other_filtered, own_query, other_query)
    both_o, q_rest, ready = lax.optimization_barrier((both_o, q_rest, ready))
    own_filtered, other_filtered, own_query, other_query = ready
    o_x = {(0, dx): from_chip(both_o, 0, dx) for dx in range(1, nx)}
    o_y = {(dy, 0): from_chip(both_o, dy, 0) for dy in range(1, ny)}
    late = [piece for pair in q_rest.values() for piece in pair]
    other_gated = project(
        gate_kernel, at[early:], other_rows, [other_filtered, other_query], late, BF16
    )
    own_gated = project(gate_kernel, at[early:], own_rows, [own_filtered, own_query], late, BF16)

    position = lax.axis_index("tp")
    z = position.astype(jnp.int32).reshape(1)
    up = [(i, i + 1) for i in range(n_tp - 1)]
    down = [(i + 1, i) for i in range(n_tp - 1)]

    def plus(a, b):
        return (a.astype(F32) + b.astype(F32)).astype(BF16)

    def terms_of(pairs, gates, turned):
        own, other = gates
        leaving = terms(n_tp, z, other, pairs, (1, 0), turned)
        return terms(n_tp, z, own, pairs, (0, 1), turned, from_partner(leaving))

    def chained(slots):
        rising = falling = hop = None
        for step in range(n_tp - 1):
            send_up, send_down = slots[n_tp - 1 - step], slots[step + 1]
            if step:
                send_up, send_down = plus(send_up, rising), plus(send_down, falling)
            rising = lax.ppermute(send_up, "tp", up)
            falling = lax.ppermute(send_down, "tp", down)
            hop = hop or (rising, falling)
        total = slots[0].astype(F32) + rising.astype(F32) + falling.astype(F32)
        return total, hop

    o_rest = {(dy, dx): from_chip(o_x[0, dx], dy, 0) for dy, _ in o_y for _, dx in o_x}
    out_pairs = {(0, 0): both_o, **o_x, **o_y, **o_rest}
    result = jnp.zeros((rows, model), BF16)
    gates = (own_gated, other_gated)
    sets = [(0, 0)], [*o_x, *o_y], list(o_rest)
    first_sum, hop = chained(terms_of([out_pairs[key] for key in sets[0]], gates, True))
    gates, _ = lax.optimization_barrier((gates, hop))
    middle = terms_of([out_pairs[key] for key in sets[1]], gates, False)
    gates, middle = lax.optimization_barrier((gates, middle))
    middle_sum = lax.psum_scatter(middle, "tp", scatter_dimension=0, tiled=True).astype(F32)
    last_sum, _ = chained(terms_of([out_pairs[key] for key in sets[2]], gates, True))
    for keys, mixed in zip(sets, (first_sum, middle_sum, last_sum)):
        for index, (dy, dx) in enumerate(keys):
            start = place(my_y + dy, my_x + dx, 0) * wide
            pair = mixed[:, index * 2 * wide : (index + 1) * 2 * wide]
            swapped = jnp.concatenate([pair[:, wide:], pair[:, :wide]], axis=1)
            kept = lax.dynamic_slice_in_dim(keep_mask, start, 2 * wide, axis=1).astype(F32)
            base = lax.dynamic_slice_in_dim(tokens, start, 2 * wide, axis=1).astype(F32)
            pair = jnp.where(core == 0, pair, swapped)
            part = (base + kept * pair * (1.0 / 0.9)).astype(BF16)
            result = lax.dynamic_update_slice_in_dim(result, part, start, axis=1)
    return result


def solution(mesh):
    in_specs = (
        P(("seq", "tp"), None),
        P(),
        P(None, "seq", "tp"),
        P(None, "tp"),
        P("tp", "seq"),
        P(("seq", "tp"), None),
    )
    out_specs = P(("seq", "tp"), None)
    return jax.shard_map(
        on_device, mesh=mesh, in_specs=in_specs, out_specs=out_specs, check_vma=False
    )
```

```python
import functools
import math

import jax
import jax.numpy as jnp
from jax import lax
from jax.experimental import pallas as pl
from jax.experimental.pallas import tpu as pltpu
from jax.sharding import PartitionSpec as P

F32 = jnp.float32
BF16 = jnp.bfloat16
GRANT = 16 << 20
WHOLE = pl.BlockSpec(memory_space=pltpu.VMEM)


def grid_of(chips):
    ny = max(d for d in range(1, math.isqrt(chips) + 1) if chips % d == 0)
    return ny, chips // ny


def dot(a, b):
    return jnp.dot(a, b, preferred_element_type=F32)


def columns_of(x_ref, at_ref, index, deep):
    return x_ref[:, pl.ds(pl.multiple_of(at_ref[index], deep), deep)]


def tiles_of(out_ref):
    tile = math.gcd(out_ref.shape[1], 256)
    return [slice(at, at + tile) for at in range(0, out_ref.shape[1], tile)]


def blocks_of(xs, out_ref):
    tile = math.gcd(out_ref.shape[1], 256)
    size = xs[0].shape[0]
    for at in range(0, out_ref.shape[1], tile):
        for index, x_ref in enumerate(xs):
            yield x_ref, slice(index * size, (index + 1) * size), slice(at, at + tile)


def product_kernel(parts, at_ref, *refs):
    xs, pieces, out_ref = refs[:parts], refs[parts:-1], refs[-1]
    deep = pieces[0].shape[1]
    for x_ref, rows, tile in blocks_of(xs, out_ref):
        key = value = None
        for index, piece in enumerate(pieces):
            x = columns_of(x_ref, at_ref, index, deep)
            new_key, new_value = dot(x, piece[0, :, tile]), dot(x, piece[1, :, tile])
            key = new_key if key is None else key + new_key
            value = new_value if value is None else value + new_value
        out_ref[rows, tile] = key.astype(BF16).astype(F32) * value.astype(BF16).astype(F32)


def query_kernel(parts, at_ref, *refs):
    xs, pairs, out_ref = refs[:parts], refs[parts:-1], refs[-1]
    deep = pairs[0].shape[1]
    for x_ref, rows, tile in blocks_of(xs, out_ref):
        query = None
        for index in range(2 * len(pairs)):
            x = columns_of(x_ref, at_ref, index, deep)
            new = dot(x, pairs[index // 2][index % 2, :, tile])
            query = new if query is None else query + new
        out_ref[rows, tile] = query


def gate_kernel(parts, at_ref, *refs):
    xs, refs = refs[:parts], refs[parts:]
    filtered_ref, partial_ref, pieces, out_ref = refs[0], refs[1], refs[2:-1], refs[-1]
    deep = pieces[0].shape[0]
    for x_ref, rows, tile in blocks_of(xs, out_ref):
        query = partial_ref[rows, tile]
        for index, piece in enumerate(pieces):
            query = query + dot(columns_of(x_ref, at_ref, index, deep), piece[:, tile])
        gated = query.astype(BF16).astype(F32) * filtered_ref[rows, tile]
        out_ref[rows, tile] = gated.astype(BF16)


def call(kernel, scalars, operands, out, scratch=()):
    return pl.pallas_call(
        kernel,
        out_shape=out,
        in_specs=[pl.BlockSpec(memory_space=pltpu.SMEM)] + [WHOLE] * len(operands),
        out_specs=jax.tree.map(lambda _: WHOLE, out),
        scratch_shapes=scratch,
        compiler_params=pltpu.CompilerParams(vmem_limit_bytes=GRANT),
        cost_estimate=pl.CostEstimate(flops=1, bytes_accessed=1, transcendentals=0),
    )(scalars, *operands)


def project(kernel, at, xs, extra, pieces, out_dtype):
    rows = sum(x.shape[0] for x in xs)
    out = jax.ShapeDtypeStruct((rows, pieces[0].shape[-1]), out_dtype)
    return call(functools.partial(kernel, len(xs)), at, (*xs, *extra, *pieces), out)


def filter_kernel(_, product_ref, halo_ref, taps_ref, out_ref, held):
    length, pad = product_ref.shape[0], halo_ref.shape[0]
    held[:pad] = halo_ref[...]
    held[pad:] = product_ref[...]
    for tile in tiles_of(out_ref):
        total = None
        for offset in range(taps_ref.shape[0]):
            term = taps_ref[offset : offset + 1, tile] * held[pad - offset : pad - offset + length, tile]
            total = term if total is None else total + term
        out_ref[:, tile] = total


def causal_filter(at, product, halo, taps):
    length, half = product.shape
    out = jax.ShapeDtypeStruct(product.shape, F32)
    scratch = [pltpu.VMEM((halo.shape[0] + length, half), F32)]
    return call(filter_kernel, at, (product, halo, taps), out, scratch)


def terms_kernel(count, order, turned, n_tp, z_ref, gated_ref, *refs):
    pairs, refs = refs[:count], refs[count:]
    length = gated_ref.shape[0]
    rows = length // n_tp
    held = gated_ref
    if turned:
        refs, held = refs[:-1], refs[-1]
        for slot in range(n_tp):
            owner = lax.rem(z_ref[0] + slot, n_tp)
            held[slot * rows : (slot + 1) * rows] = gated_ref[
                pl.ds(pl.multiple_of(owner * rows, rows), rows)
            ]
    given, outs = (refs[0], refs[1:]) if len(refs) > 1 else (None, refs)
    wide = pairs[0].shape[2]
    for index, (pair, side) in enumerate((p, s) for p in pairs for s in order):
        at = slice(index * wide, (index + 1) * wide)
        total = dot(held[...], pair[side])
        if given is not None:
            total = total + given[:, at].astype(F32)
        share = length // len(outs)
        for slot, out in enumerate(outs):
            out[:, at] = total[slot * share : (slot + 1) * share].astype(BF16)


def terms(n_tp, z, gated, pairs, order, turned, given=None):
    length, half = gated.shape
    cols = len(pairs) * 2 * pairs[0].shape[2]
    slots = n_tp if turned and given is not None else 1
    out = [jax.ShapeDtypeStruct((length // slots, cols), BF16)] * slots
    kernel = functools.partial(terms_kernel, len(pairs), order, turned, n_tp)
    extra = () if given is None else (given,)
    scratch = [pltpu.VMEM((length, half), BF16)] if turned else []
    result = call(kernel, z, (gated, *pairs, *extra), out, scratch)
    return result if slots > 1 else result[0]


def on_device(tokens, norm_gain, in_weight, filters, out_weight, keep_mask):
    n_seq, n_tp = lax.axis_size("seq"), lax.axis_size("tp")
    chips = n_seq // 2
    ny, nx = grid_of(chips)
    seq = lax.axis_index("seq")
    core, here = seq % 2, seq // 2
    my_y, my_x = here // nx, here % nx
    rows, model = tokens.shape
    length = rows * n_tp
    deep, channels = in_weight.shape[1:]
    half = channels // 2
    wide = out_weight.shape[1]

    def place(y, x, c):
        return ((y % ny) * nx + x % nx) * 2 + c

    def from_chip(block, dy, dx):
        route = [
            (place(y + dy, x + dx, c), place(y, x, c))
            for y in range(ny)
            for x in range(nx)
            for c in range(2)
        ]
        return lax.ppermute(block, "seq", route)

    def from_partner(block):
        return lax.ppermute(block, "seq", [(s, s ^ 1) for s in range(n_seq)])

    def direct(mine, brought):
        along_x = [(mine, brought)]
        along_y = [(mine, brought)]
        along_x += [tuple(from_chip(b, 0, dx) for b in (mine, brought)) for dx in range(1, nx)]
        along_y += [tuple(from_chip(b, dy, 0) for b in (mine, brought)) for dy in range(1, ny)]
        return along_x, along_y

    def onward(along_x, along_y):
        return {
            (dy, dx): (from_chip(along_x[dx][0], dy, 0), from_chip(along_y[dy][1], 0, dx))
            for dy in range(1, ny)
            for dx in range(1, nx)
        }

    def listed(along_x, along_y, rest):
        found = {(0, dx): pair for dx, pair in enumerate(along_x)}
        found.update({(dy, 0): pair for dy, pair in enumerate(along_y)})
        found.update(rest)
        return found

    def halves(array, axis, at):
        size = array.shape[axis] // 2
        return lax.dynamic_slice_in_dim(array, at * size, size, axis=axis)

    def columns(array, first, count, at):
        return lax.dynamic_slice(array, (first, 0, at * half), (count, deep, half))

    mine_kv = columns(in_weight, 1, 2, core)
    away_kv = columns(in_weight, 1, 2, 1 - core)
    brought_kv = from_partner(away_kv)
    kv_x, kv_y = direct(mine_kv, brought_kv)

    tokens_then, _ = lax.optimization_barrier((tokens, away_kv))
    widened = tokens_then.astype(F32)
    mean_sq = jnp.mean(widened * widened, axis=1, keepdims=True)
    normed = (widened * lax.rsqrt(mean_sq + 1e-06) * norm_gain).astype(BF16)
    own_rows = lax.all_gather(normed, "tp", axis=0, tiled=True)
    in_weight_then, out_weight_then, _ = lax.optimization_barrier((in_weight, out_weight, normed))
    mine_q = columns(in_weight_then, 0, 1, core)[0]
    both_q = jnp.stack([mine_q, from_partner(columns(in_weight_then, 0, 1, 1 - core)[0])])
    mine_o = halves(out_weight_then, 0, core)
    both_o = jnp.stack([mine_o, from_partner(halves(out_weight_then, 0, 1 - core))])

    kv_x, kv_y, both_q = lax.optimization_barrier((kv_x, kv_y, both_q))
    kv_rest = onward(kv_x, kv_y)
    q_x = {(0, dx): from_chip(both_q, 0, dx) for dx in range(1, nx)}
    q_y = {(dy, 0): from_chip(both_q, dy, 0) for dy in range(1, ny)}
    arrived = (kv_x, kv_y, kv_rest)
    own_rows, arrived = lax.optimization_barrier((own_rows, arrived))
    kv_x, kv_y, kv_rest = arrived
    kv = listed(kv_x, kv_y, kv_rest)
    order = list(kv)
    kv_pieces = [piece for key in order for piece in kv[key]]
    at = jnp.stack(
        [place(my_y + dy, my_x + dx, core ^ rc) * deep for dy, dx in order for rc in range(2)]
    ).astype(jnp.int32)
    early = 2 * (ny + nx - 1)

    own_product = project(product_kernel, at, [own_rows], [], kv_pieces, F32)
    rows_then, q_x, q_y, own_product = lax.optimization_barrier((own_rows, q_x, q_y, own_product))
    other_rows = from_partner(rows_then)
    q_rest = {
        (dy, dx): (from_chip(q_x[0, dx][0], dy, 0), from_chip(q_y[dy, 0][1], 0, dx))
        for dy, _ in q_y
        for _, dx in q_x
    }
    q_pairs = {(0, 0): both_q, **q_x, **q_y}
    q_early = [q_pairs[key] for key in order if key in q_pairs]
    own_query = project(query_kernel, at, [own_rows], [], q_early, F32)
    other_rows, own_query = lax.optimization_barrier((other_rows, own_query))
    other_product = project(product_kernel, at, [other_rows], [], kv_pieces, F32)

    reach = filters.shape[0] - 1
    pad = -(-reach // 8) * 8
    own_tail, other_tail = own_product[length - pad :], other_product[length - pad :]
    first_tail = jnp.where(core == 0, own_tail, other_tail)
    last_tail = jnp.where(core == 0, other_tail, own_tail)
    rim = lax.ppermute(
        last_tail,
        "seq",
        [(2 * i + c, 2 * i + 2 + c) for i in range(chips - 1) for c in range(2)],
    )
    other_query = project(query_kernel, at, [other_rows], [], q_early, F32)
    groups = filters.shape[1] // 2
    taps = jnp.repeat(
        lax.dynamic_slice_in_dim(filters, core * groups, groups, axis=1), half // groups, axis=1
    )
    own_filtered = causal_filter(at, own_product, jnp.where(core == 0, rim, first_tail), taps)
    other_filtered = causal_filter(at, other_product, jnp.where(core == 0, first_tail, rim), taps)

    ready = (own_filtered, other_filtered, own_query, other_query)
    both_o, q_rest, ready = lax.optimization_barrier((both_o, q_rest, ready))
    own_filtered, other_filtered, own_query, other_query = ready
    o_x = {(0, dx): from_chip(both_o, 0, dx) for dx in range(1, nx)}
    o_y = {(dy, 0): from_chip(both_o, dy, 0) for dy in range(1, ny)}
    late = [piece for pair in q_rest.values() for piece in pair]
    other_gated = project(
        gate_kernel, at[early:], [other_rows], [other_filtered, other_query], late, BF16
    )
    own_gated = project(gate_kernel, at[early:], [own_rows], [own_filtered, own_query], late, BF16)

    position = lax.axis_index("tp")
    z = position.astype(jnp.int32).reshape(1)
    up = [(i, i + 1) for i in range(n_tp - 1)]
    down = [(i + 1, i) for i in range(n_tp - 1)]

    def plus(a, b):
        return (a.astype(F32) + b.astype(F32)).astype(BF16)

    def terms_of(pairs, gates, turned):
        own, other = gates
        leaving = terms(n_tp, z, other, pairs, (1, 0), turned)
        return terms(n_tp, z, own, pairs, (0, 1), turned, from_partner(leaving))

    def chained(slots):
        rising = falling = hop = None
        for step in range(n_tp - 1):
            send_up, send_down = slots[n_tp - 1 - step], slots[step + 1]
            if step:
                send_up, send_down = plus(send_up, rising), plus(send_down, falling)
            rising = lax.ppermute(send_up, "tp", up)
            falling = lax.ppermute(send_down, "tp", down)
            hop = hop or (rising, falling)
        total = slots[0].astype(F32) + rising.astype(F32) + falling.astype(F32)
        return total, hop

    o_rest = {(dy, dx): from_chip(o_x[0, dx], dy, 0) for dy, _ in o_y for _, dx in o_x}
    out_pairs = {(0, 0): both_o, **o_x, **o_y, **o_rest}
    result = jnp.zeros((rows, model), BF16)
    gates = (own_gated, other_gated)
    sets = [(0, 0)], [*o_x, *o_y], list(o_rest)
    first_sum, hop = chained(terms_of([out_pairs[key] for key in sets[0]], gates, True))
    gates, _ = lax.optimization_barrier((gates, hop))
    middle = terms_of([out_pairs[key] for key in sets[1]], gates, False)
    gates, middle = lax.optimization_barrier((gates, middle))
    middle_sum = lax.psum_scatter(middle, "tp", scatter_dimension=0, tiled=True).astype(F32)
    last_sum, _ = chained(terms_of([out_pairs[key] for key in sets[2]], gates, True))
    for keys, mixed in zip(sets, (first_sum, middle_sum, last_sum)):
        for index, (dy, dx) in enumerate(keys):
            start = place(my_y + dy, my_x + dx, 0) * wide
            pair = mixed[:, index * 2 * wide : (index + 1) * 2 * wide]
            swapped = jnp.concatenate([pair[:, wide:], pair[:, :wide]], axis=1)
            kept = lax.dynamic_slice_in_dim(keep_mask, start, 2 * wide, axis=1).astype(F32)
            base = lax.dynamic_slice_in_dim(tokens, start, 2 * wide, axis=1).astype(F32)
            pair = jnp.where(core == 0, pair, swapped)
            part = (base + kept * pair * (1.0 / 0.9)).astype(BF16)
            result = lax.dynamic_update_slice_in_dim(result, part, start, axis=1)
    return result


def solution(mesh):
    in_specs = (
        P(("seq", "tp"), None),
        P(),
        P(None, "seq", "tp"),
        P(None, "tp"),
        P("tp", "seq"),
        P(("seq", "tp"), None),
    )
    out_specs = P(("seq", "tp"), None)
    return jax.shard_map(
        on_device, mesh=mesh, in_specs=in_specs, out_specs=out_specs, check_vma=False
    )
```

```python
import functools
import math

import jax
import jax.numpy as jnp
from jax import lax
from jax.experimental import pallas as pl
from jax.experimental.pallas import tpu as pltpu
from jax.sharding import PartitionSpec as P

F32 = jnp.float32
BF16 = jnp.bfloat16
GRANT = 16 << 20
WHOLE = pl.BlockSpec(memory_space=pltpu.VMEM)


def grid_of(chips):
    ny = max(d for d in range(1, math.isqrt(chips) + 1) if chips % d == 0)
    return ny, chips // ny


def dot(a, b):
    return jnp.dot(a, b, preferred_element_type=F32)


def columns_of(x_ref, at_ref, index, deep):
    return x_ref[:, pl.ds(pl.multiple_of(at_ref[index], deep), deep)]


def tiles_of(out_ref):
    tile = math.gcd(out_ref.shape[1], 256)
    return [slice(at, at + tile) for at in range(0, out_ref.shape[1], tile)]


def blocks_of(xs, out_ref):
    tile = math.gcd(out_ref.shape[1], 256)
    size = xs[0].shape[0]
    for at in range(0, out_ref.shape[1], tile):
        for index, x_ref in enumerate(xs):
            yield x_ref, slice(index * size, (index + 1) * size), slice(at, at + tile)


def product_kernel(parts, at_ref, *refs):
    xs, pieces, out_ref = refs[:parts], refs[parts:-1], refs[-1]
    deep = pieces[0].shape[1]
    for x_ref, rows, tile in blocks_of(xs, out_ref):
        key = value = None
        for index, piece in enumerate(pieces):
            x = columns_of(x_ref, at_ref, index, deep)
            new_key, new_value = dot(x, piece[0, :, tile]), dot(x, piece[1, :, tile])
            key = new_key if key is None else key + new_key
            value = new_value if value is None else value + new_value
        out_ref[rows, tile] = key.astype(BF16).astype(F32) * value.astype(BF16).astype(F32)


def query_kernel(parts, at_ref, *refs):
    xs, pairs, out_ref = refs[:parts], refs[parts:-1], refs[-1]
    deep = pairs[0].shape[1]
    for x_ref, rows, tile in blocks_of(xs, out_ref):
        query = None
        for index in range(2 * len(pairs)):
            x = columns_of(x_ref, at_ref, index, deep)
            new = dot(x, pairs[index // 2][index % 2, :, tile])
            query = new if query is None else query + new
        out_ref[rows, tile] = query


def gate_kernel(parts, at_ref, *refs):
    xs, refs = refs[:parts], refs[parts:]
    filtered_ref, partial_ref, pieces, out_ref = refs[0], refs[1], refs[2:-1], refs[-1]
    deep = pieces[0].shape[0]
    for x_ref, rows, tile in blocks_of(xs, out_ref):
        query = partial_ref[rows, tile]
        for index, piece in enumerate(pieces):
            query = query + dot(columns_of(x_ref, at_ref, index, deep), piece[:, tile])
        gated = query.astype(BF16).astype(F32) * filtered_ref[rows, tile]
        out_ref[rows, tile] = gated.astype(BF16)


def call(kernel, scalars, operands, out, scratch=()):
    return pl.pallas_call(
        kernel,
        out_shape=out,
        in_specs=[pl.BlockSpec(memory_space=pltpu.SMEM)] + [WHOLE] * len(operands),
        out_specs=jax.tree.map(lambda _: WHOLE, out),
        scratch_shapes=scratch,
        compiler_params=pltpu.CompilerParams(vmem_limit_bytes=GRANT),
        cost_estimate=pl.CostEstimate(flops=1, bytes_accessed=1, transcendentals=0),
    )(scalars, *operands)


def project(kernel, at, xs, extra, pieces, out_dtype):
    rows = sum(x.shape[0] for x in xs)
    out = jax.ShapeDtypeStruct((rows, pieces[0].shape[-1]), out_dtype)
    return call(functools.partial(kernel, len(xs)), at, (*xs, *extra, *pieces), out)


def filter_kernel(_, product_ref, halo_ref, taps_ref, out_ref, held):
    length, pad = product_ref.shape[0], halo_ref.shape[0]
    held[:pad] = halo_ref[...]
    held[pad:] = product_ref[...]
    for tile in tiles_of(out_ref):
        total = None
        for offset in range(taps_ref.shape[0]):
            term = taps_ref[offset : offset + 1, tile] * held[pad - offset : pad - offset + length, tile]
            total = term if total is None else total + term
        out_ref[:, tile] = total


def causal_filter(at, product, halo, taps):
    length, half = product.shape
    out = jax.ShapeDtypeStruct(product.shape, F32)
    scratch = [pltpu.VMEM((halo.shape[0] + length, half), F32)]
    return call(filter_kernel, at, (product, halo, taps), out, scratch)


def terms_kernel(plan, turned, n_tp, z_ref, gated_ref, *refs):
    count = 1 + max(which for which, _ in plan)
    weights, refs = refs[:count], refs[count:]
    length = gated_ref.shape[0]
    rows = length // n_tp
    held = gated_ref
    if turned:
        refs, held = refs[:-1], refs[-1]
        for slot in range(n_tp):
            owner = lax.rem(z_ref[0] + slot, n_tp)
            held[slot * rows : (slot + 1) * rows] = gated_ref[
                pl.ds(pl.multiple_of(owner * rows, rows), rows)
            ]
    given, outs = (refs[0], refs[1:]) if len(refs) > 1 else (None, refs)
    wide = weights[0].shape[-1]
    for index, (which, side) in enumerate(plan):
        at = slice(index * wide, (index + 1) * wide)
        weight = weights[which]
        total = dot(held[...], weight[...] if side is None else weight[side])
        if given is not None:
            total = total + given[:, at].astype(F32)
        share = length // len(outs)
        for slot, out in enumerate(outs):
            out[:, at] = total[slot * share : (slot + 1) * share].astype(BF16)


def terms(n_tp, z, gated, pairs, order, turned, given=None):
    length, half = gated.shape
    weights, plan = [], []
    for pair in pairs:
        if isinstance(pair, tuple):
            plan += [(len(weights) + side, None) for side in order]
            weights += pair
        else:
            plan += [(len(weights), side) for side in order]
            weights.append(pair)
    cols = len(plan) * weights[0].shape[-1]
    slots = n_tp if turned and given is not None else 1
    out = [jax.ShapeDtypeStruct((length // slots, cols), BF16)] * slots
    kernel = functools.partial(terms_kernel, plan, turned, n_tp)
    extra = () if given is None else (given,)
    scratch = [pltpu.VMEM((length, half), BF16)] if turned else []
    result = call(kernel, z, (gated, *weights, *extra), out, scratch)
    return result if slots > 1 else result[0]


def on_device(tokens, norm_gain, in_weight, filters, out_weight, keep_mask):
    n_seq, n_tp = lax.axis_size("seq"), lax.axis_size("tp")
    chips = n_seq // 2
    ny, nx = grid_of(chips)
    seq = lax.axis_index("seq")
    core, here = seq % 2, seq // 2
    my_y, my_x = here // nx, here % nx
    rows, model = tokens.shape
    length = rows * n_tp
    deep, channels = in_weight.shape[1:]
    half = channels // 2
    wide = out_weight.shape[1]

    def place(y, x, c):
        return ((y % ny) * nx + x % nx) * 2 + c

    def from_chip(block, dy, dx):
        route = [
            (place(y + dy, x + dx, c), place(y, x, c))
            for y in range(ny)
            for x in range(nx)
            for c in range(2)
        ]
        return lax.ppermute(block, "seq", route)

    def from_partner(block):
        return lax.ppermute(block, "seq", [(s, s ^ 1) for s in range(n_seq)])

    def direct(mine, brought):
        along_x = [(mine, brought)]
        along_y = [(mine, brought)]
        along_x += [tuple(from_chip(b, 0, dx) for b in (mine, brought)) for dx in range(1, nx)]
        along_y += [tuple(from_chip(b, dy, 0) for b in (mine, brought)) for dy in range(1, ny)]
        return along_x, along_y

    def onward(along_x, along_y):
        return {
            (dy, dx): (from_chip(along_x[dx][0], dy, 0), from_chip(along_y[dy][1], 0, dx))
            for dy in range(1, ny)
            for dx in range(1, nx)
        }

    def crossed(along_x, along_y):
        return {
            (dy, dx): (from_chip(along_x[0, dx][0], dy, 0), from_chip(along_y[dy, 0][1], 0, dx))
            for dy, _ in along_y
            for _, dx in along_x
        }

    def listed(along_x, along_y, rest):
        found = {(0, dx): pair for dx, pair in enumerate(along_x)}
        found.update({(dy, 0): pair for dy, pair in enumerate(along_y)})
        found.update(rest)
        return found

    def halves(array, axis, at):
        size = array.shape[axis] // 2
        return lax.dynamic_slice_in_dim(array, at * size, size, axis=axis)

    def columns(array, first, count, at):
        return lax.dynamic_slice(array, (first, 0, at * half), (count, deep, half))

    mine_kv = columns(in_weight, 1, 2, core)
    away_kv = columns(in_weight, 1, 2, 1 - core)
    brought_kv = from_partner(away_kv)
    kv_x, kv_y = direct(mine_kv, brought_kv)

    tokens_then, _ = lax.optimization_barrier((tokens, away_kv))
    widened = tokens_then.astype(F32)
    mean_sq = jnp.mean(widened * widened, axis=1, keepdims=True)
    normed = (widened * lax.rsqrt(mean_sq + 1e-06) * norm_gain).astype(BF16)
    own_rows = lax.all_gather(normed, "tp", axis=0, tiled=True)
    in_weight_then, out_weight_then, _ = lax.optimization_barrier((in_weight, out_weight, normed))
    mine_q = columns(in_weight_then, 0, 1, core)[0]
    both_q = jnp.stack([mine_q, from_partner(columns(in_weight_then, 0, 1, 1 - core)[0])])
    mine_o = halves(out_weight_then, 0, core)
    both_o = jnp.stack([mine_o, from_partner(halves(out_weight_then, 0, 1 - core))])

    kv_x, kv_y, both_q, both_o = lax.optimization_barrier((kv_x, kv_y, both_q, both_o))
    kv_rest = onward(kv_x, kv_y)
    q_x = {(0, dx): from_chip(both_q, 0, dx) for dx in range(1, nx)}
    q_y = {(dy, 0): from_chip(both_q, dy, 0) for dy in range(1, ny)}
    arrived = (kv_x, kv_y, kv_rest)
    own_rows, arrived = lax.optimization_barrier((own_rows, arrived))
    kv_x, kv_y, kv_rest = arrived
    kv = listed(kv_x, kv_y, kv_rest)
    order = list(kv)
    kv_pieces = [piece for key in order for piece in kv[key]]
    at = jnp.stack(
        [place(my_y + dy, my_x + dx, core ^ rc) * deep for dy, dx in order for rc in range(2)]
    ).astype(jnp.int32)
    early = 2 * (ny + nx - 1)

    own_product = project(product_kernel, at, [own_rows], [], kv_pieces, F32)
    rows_then, q_x, q_y, own_product = lax.optimization_barrier((own_rows, q_x, q_y, own_product))
    other_rows = from_partner(rows_then)
    q_rest = crossed(q_x, q_y)
    q_pairs = {(0, 0): both_q, **q_x, **q_y}
    q_early = [q_pairs[key] for key in order if key in q_pairs]
    own_query = project(query_kernel, at, [own_rows], [], q_early, F32)
    other_rows, own_query = lax.optimization_barrier((other_rows, own_query))
    other_product = project(product_kernel, at, [other_rows], [], kv_pieces, F32)

    reach = filters.shape[0] - 1
    pad = -(-reach // 8) * 8
    own_tail, other_tail = own_product[length - pad :], other_product[length - pad :]
    first_tail = jnp.where(core == 0, own_tail, other_tail)
    last_tail = jnp.where(core == 0, other_tail, own_tail)
    rim = lax.ppermute(
        last_tail,
        "seq",
        [(2 * i + c, 2 * i + 2 + c) for i in range(chips - 1) for c in range(2)],
    )
    groups = filters.shape[1] // 2
    taps = jnp.repeat(
        lax.dynamic_slice_in_dim(filters, core * groups, groups, axis=1), half // groups, axis=1
    )
    own_filtered = causal_filter(at, own_product, jnp.where(core == 0, rim, first_tail), taps)
    other_filtered = causal_filter(at, other_product, jnp.where(core == 0, first_tail, rim), taps)

    other_rows, own_filtered, other_filtered = lax.optimization_barrier(
        (other_rows, own_filtered, other_filtered)
    )
    other_query = project(query_kernel, at, [other_rows], [], q_early, F32)
    both_o, q_x, q_y = lax.optimization_barrier((both_o, q_x, q_y))
    o_x = {(0, dx): from_chip(both_o, 0, dx) for dx in range(1, nx)}
    o_y = {(dy, 0): from_chip(both_o, dy, 0) for dy in range(1, ny)}
    late = [piece for pair in q_rest.values() for piece in pair]
    other_gated = project(
        gate_kernel, at[early:], [other_rows], [other_filtered, other_query], late, BF16
    )
    own_gated = project(
        gate_kernel, at[early:], [own_rows], [own_filtered, own_query], late, BF16
    )

    position = lax.axis_index("tp")
    z = position.astype(jnp.int32).reshape(1)
    up = [(i, i + 1) for i in range(n_tp - 1)]
    down = [(i + 1, i) for i in range(n_tp - 1)]

    def plus(a, b):
        return (a.astype(F32) + b.astype(F32)).astype(BF16)

    def leaving_of(pairs, gates, turned):
        return from_partner(terms(n_tp, z, gates[1], pairs, (1, 0), turned))

    def terms_of(pairs, gates, turned, given):
        return terms(n_tp, z, gates[0], pairs, (0, 1), turned, given)

    def chained(slots):
        rising = falling = None
        for step in range(n_tp - 1):
            send_up, send_down = slots[n_tp - 1 - step], slots[step + 1]
            if step:
                send_up, send_down = plus(send_up, rising), plus(send_down, falling)
            rising = lax.ppermute(send_up, "tp", up)
            falling = lax.ppermute(send_down, "tp", down)
        total = slots[0].astype(F32) + rising.astype(F32) + falling.astype(F32)
        return total

    o_rest = crossed(o_x, o_y)
    out_pairs = {(0, 0): both_o, **o_x, **o_y, **o_rest}
    result = jnp.zeros((rows, model), BF16)
    gates = (own_gated, other_gated)
    sets = [(0, 0), *o_x, *o_y], list(o_rest)
    first, last = ([out_pairs[key] for key in keys] for keys in sets)
    found = terms_of(first, gates, False, leaving_of(first, gates, False))
    gates, found = lax.optimization_barrier((gates, found))
    first_sum = lax.psum_scatter(found, "tp", scatter_dimension=0, tiled=True).astype(F32)
    last_sum = chained(terms_of(last, gates, True, leaving_of(last, gates, True)))
    for keys, mixed in zip(sets, (first_sum, last_sum)):
        for index, (dy, dx) in enumerate(keys):
            start = place(my_y + dy, my_x + dx, 0) * wide
            pair = mixed[:, index * 2 * wide : (index + 1) * 2 * wide]
            swapped = jnp.concatenate([pair[:, wide:], pair[:, :wide]], axis=1)
            kept = lax.dynamic_slice_in_dim(keep_mask, start, 2 * wide, axis=1).astype(F32)
            base = lax.dynamic_slice_in_dim(tokens, start, 2 * wide, axis=1).astype(F32)
            pair = jnp.where(core == 0, pair, swapped)
            part = (base + kept * pair * (1.0 / 0.9)).astype(BF16)
            result = lax.dynamic_update_slice_in_dim(result, part, start, axis=1)
    return result


def solution(mesh):
    in_specs = (
        P(("seq", "tp"), None),
        P(),
        P(None, "seq", "tp"),
        P(None, "tp"),
        P("tp", "seq"),
        P(("seq", "tp"), None),
    )
    out_specs = P(("seq", "tp"), None)
    return jax.shard_map(
        on_device, mesh=mesh, in_specs=in_specs, out_specs=out_specs, check_vma=False
    )
```

```python
import functools
import math

import jax
import jax.numpy as jnp
from jax import lax
from jax.experimental import pallas as pl
from jax.experimental.pallas import tpu as pltpu
from jax.sharding import PartitionSpec as P

F32 = jnp.float32
BF16 = jnp.bfloat16
GRANT = 16 << 20
WHOLE = pl.BlockSpec(memory_space=pltpu.VMEM)


def grid_of(chips):
    ny = max(d for d in range(1, math.isqrt(chips) + 1) if chips % d == 0)
    return ny, chips // ny


def dot(a, b):
    return jnp.dot(a, b, preferred_element_type=F32)


def columns_of(x_ref, at_ref, index, deep):
    return x_ref[:, pl.ds(pl.multiple_of(at_ref[index], deep), deep)]


def tiles_of(out_ref):
    tile = math.gcd(out_ref.shape[1], 256)
    return [slice(at, at + tile) for at in range(0, out_ref.shape[1], tile)]


def blocks_of(xs, out_ref):
    tile = math.gcd(out_ref.shape[1], 256)
    size = xs[0].shape[0]
    for at in range(0, out_ref.shape[1], tile):
        for index, x_ref in enumerate(xs):
            yield x_ref, slice(index * size, (index + 1) * size), slice(at, at + tile)


def product_kernel(parts, at_ref, *refs):
    xs, pieces, out_ref = refs[:parts], refs[parts:-1], refs[-1]
    deep = pieces[0].shape[1]
    for x_ref, rows, tile in blocks_of(xs, out_ref):
        key = value = None
        for index, piece in enumerate(pieces):
            x = columns_of(x_ref, at_ref, index, deep)
            new_key, new_value = dot(x, piece[0, :, tile]), dot(x, piece[1, :, tile])
            key = new_key if key is None else key + new_key
            value = new_value if value is None else value + new_value
        out_ref[rows, tile] = key.astype(BF16).astype(F32) * value.astype(BF16).astype(F32)


def joined_kernel(at_ref, before_ref, x_ref, *refs):
    pieces, (rim_ref, out_ref, joined) = refs[:-3], refs[-3:]
    pad = before_ref.shape[0]
    joined[:pad] = before_ref[...]
    joined[pad:] = x_ref[...]
    deep = pieces[0].shape[1]
    for _, _, tile in blocks_of([x_ref], out_ref):
        key = value = None
        for index, piece in enumerate(pieces):
            x = columns_of(joined, at_ref, index, deep)
            new_key, new_value = dot(x, piece[0, :, tile]), dot(x, piece[1, :, tile])
            key = new_key if key is None else key + new_key
            value = new_value if value is None else value + new_value
        product = key.astype(BF16).astype(F32) * value.astype(BF16).astype(F32)
        rim_ref[:, tile] = product[:pad]
        out_ref[:, tile] = product[pad:]


def query_kernel(parts, at_ref, *refs):
    xs, pairs, out_ref = refs[:parts], refs[parts:-1], refs[-1]
    deep = pairs[0].shape[1]
    for x_ref, rows, tile in blocks_of(xs, out_ref):
        query = None
        for index in range(2 * len(pairs)):
            x = columns_of(x_ref, at_ref, index, deep)
            new = dot(x, pairs[index // 2][index % 2, :, tile])
            query = new if query is None else query + new
        out_ref[rows, tile] = query


def gate_kernel(parts, at_ref, *refs):
    xs, refs = refs[:parts], refs[parts:]
    filtered_ref, partial_ref, pieces, out_ref = refs[0], refs[1], refs[2:-1], refs[-1]
    deep = pieces[0].shape[0]
    for x_ref, rows, tile in blocks_of(xs, out_ref):
        query = partial_ref[rows, tile]
        for index, piece in enumerate(pieces):
            query = query + dot(columns_of(x_ref, at_ref, index, deep), piece[:, tile])
        gated = query.astype(BF16).astype(F32) * filtered_ref[rows, tile]
        out_ref[rows, tile] = gated.astype(BF16)


def call(kernel, scalars, operands, out, scratch=()):
    return pl.pallas_call(
        kernel,
        out_shape=out,
        in_specs=[pl.BlockSpec(memory_space=pltpu.SMEM)] + [WHOLE] * len(operands),
        out_specs=jax.tree.map(lambda _: WHOLE, out),
        scratch_shapes=scratch,
        compiler_params=pltpu.CompilerParams(vmem_limit_bytes=GRANT),
        cost_estimate=pl.CostEstimate(flops=1, bytes_accessed=1, transcendentals=0),
    )(scalars, *operands)


def project(kernel, at, xs, extra, pieces, out_dtype):
    rows = sum(x.shape[0] for x in xs)
    out = jax.ShapeDtypeStruct((rows, pieces[0].shape[-1]), out_dtype)
    return call(functools.partial(kernel, len(xs)), at, (*xs, *extra, *pieces), out)


def project_joined(at, before, x, pieces):
    half = pieces[0].shape[-1]
    pad, length = before.shape[0], x.shape[0]
    out = [jax.ShapeDtypeStruct((rows, half), F32) for rows in (pad, length)]
    scratch = [pltpu.VMEM((pad + length, x.shape[1]), BF16)]
    return call(joined_kernel, at, (before, x, *pieces), out, scratch)


def filter_kernel(_, product_ref, halo_ref, taps_ref, out_ref, held):
    length, pad = product_ref.shape[0], halo_ref.shape[0]
    held[:pad] = halo_ref[...]
    held[pad:] = product_ref[...]
    for tile in tiles_of(out_ref):
        total = None
        for offset in range(taps_ref.shape[0]):
            term = taps_ref[offset : offset + 1, tile] * held[pad - offset : pad - offset + length, tile]
            total = term if total is None else total + term
        out_ref[:, tile] = total


def causal_filter(at, product, halo, taps):
    length, half = product.shape
    out = jax.ShapeDtypeStruct(product.shape, F32)
    scratch = [pltpu.VMEM((halo.shape[0] + length, half), F32)]
    return call(filter_kernel, at, (product, halo, taps), out, scratch)


def terms_kernel(plan, turned, n_tp, z_ref, gated_ref, *refs):
    count = 1 + max(which for which, _ in plan)
    weights, refs = refs[:count], refs[count:]
    length = gated_ref.shape[0]
    rows = length // n_tp
    held = gated_ref
    if turned:
        refs, held = refs[:-1], refs[-1]
        for slot in range(n_tp):
            owner = lax.rem(z_ref[0] + slot, n_tp)
            held[slot * rows : (slot + 1) * rows] = gated_ref[
                pl.ds(pl.multiple_of(owner * rows, rows), rows)
            ]
    given, outs = (refs[0], refs[1:]) if len(refs) > 1 else (None, refs)
    wide = weights[0].shape[-1]
    for index, (which, side) in enumerate(plan):
        at = slice(index * wide, (index + 1) * wide)
        weight = weights[which]
        total = dot(held[...], weight[...] if side is None else weight[side])
        if given is not None:
            total = total + given[:, at].astype(F32)
        share = length // len(outs)
        for slot, out in enumerate(outs):
            out[:, at] = total[slot * share : (slot + 1) * share].astype(BF16)


def terms(n_tp, z, gated, pairs, order, turned, given=None):
    length, half = gated.shape
    weights, plan = [], []
    for pair in pairs:
        if isinstance(pair, tuple):
            plan += [(len(weights) + side, None) for side in order]
            weights += pair
        else:
            plan += [(len(weights), side) for side in order]
            weights.append(pair)
    cols = len(plan) * weights[0].shape[-1]
    slots = n_tp if turned and given is not None else 1
    out = [jax.ShapeDtypeStruct((length // slots, cols), BF16)] * slots
    kernel = functools.partial(terms_kernel, plan, turned, n_tp)
    extra = () if given is None else (given,)
    scratch = [pltpu.VMEM((length, half), BF16)] if turned else []
    result = call(kernel, z, (gated, *weights, *extra), out, scratch)
    return result if slots > 1 else result[0]


def on_device(tokens, norm_gain, in_weight, filters, out_weight, keep_mask):
    n_seq, n_tp = lax.axis_size("seq"), lax.axis_size("tp")
    chips = n_seq // 2
    ny, nx = grid_of(chips)
    seq = lax.axis_index("seq")
    core, here = seq % 2, seq // 2
    my_y, my_x = here // nx, here % nx
    rows, model = tokens.shape
    length = rows * n_tp
    deep, channels = in_weight.shape[1:]
    half = channels // 2
    wide = out_weight.shape[1]

    def place(y, x, c):
        return ((y % ny) * nx + x % nx) * 2 + c

    def from_chip(block, dy, dx):
        route = [
            (place(y + dy, x + dx, c), place(y, x, c))
            for y in range(ny)
            for x in range(nx)
            for c in range(2)
        ]
        return lax.ppermute(block, "seq", route)

    def from_partner(block):
        return lax.ppermute(block, "seq", [(s, s ^ 1) for s in range(n_seq)])

    def direct(mine, brought):
        along_x = [(mine, brought)]
        along_y = [(mine, brought)]
        along_x += [tuple(from_chip(b, 0, dx) for b in (mine, brought)) for dx in range(1, nx)]
        along_y += [tuple(from_chip(b, dy, 0) for b in (mine, brought)) for dy in range(1, ny)]
        return along_x, along_y

    def onward(along_x, along_y):
        return {
            (dy, dx): (from_chip(along_x[dx][0], dy, 0), from_chip(along_y[dy][1], 0, dx))
            for dy in range(1, ny)
            for dx in range(1, nx)
        }

    def crossed(along_x, along_y):
        return {
            (dy, dx): (from_chip(along_x[0, dx][0], dy, 0), from_chip(along_y[dy, 0][1], 0, dx))
            for dy, _ in along_y
            for _, dx in along_x
        }

    def listed(along_x, along_y, rest):
        found = {(0, dx): pair for dx, pair in enumerate(along_x)}
        found.update({(dy, 0): pair for dy, pair in enumerate(along_y)})
        found.update(rest)
        return found

    def halves(array, axis, at):
        size = array.shape[axis] // 2
        return lax.dynamic_slice_in_dim(array, at * size, size, axis=axis)

    def columns(array, first, count, at):
        return lax.dynamic_slice(array, (first, 0, at * half), (count, deep, half))

    mine_kv = columns(in_weight, 1, 2, core)
    away_kv = columns(in_weight, 1, 2, 1 - core)
    brought_kv = from_partner(away_kv)
    kv_x, kv_y = direct(mine_kv, brought_kv)

    tokens_then, _ = lax.optimization_barrier((tokens, away_kv))
    widened = tokens_then.astype(F32)
    mean_sq = jnp.mean(widened * widened, axis=1, keepdims=True)
    normed = (widened * lax.rsqrt(mean_sq + 1e-06) * norm_gain).astype(BF16)
    own_rows = lax.all_gather(normed, "tp", axis=0, tiled=True)
    in_weight_then, out_weight_then, _ = lax.optimization_barrier((in_weight, out_weight, normed))
    mine_q = columns(in_weight_then, 0, 1, core)[0]
    both_q = jnp.stack([mine_q, from_partner(columns(in_weight_then, 0, 1, 1 - core)[0])])
    mine_o = halves(out_weight_then, 0, core)
    both_o = jnp.stack([mine_o, from_partner(halves(out_weight_then, 0, 1 - core))])

    kv_x, kv_y, both_q, both_o = lax.optimization_barrier((kv_x, kv_y, both_q, both_o))
    kv_rest = onward(kv_x, kv_y)
    q_x = {(0, dx): from_chip(both_q, 0, dx) for dx in range(1, nx)}
    q_y = {(dy, 0): from_chip(both_q, dy, 0) for dy in range(1, ny)}
    arrived = (kv_x, kv_y, kv_rest)
    own_rows, arrived = lax.optimization_barrier((own_rows, arrived))
    kv_x, kv_y, kv_rest = arrived
    kv = listed(kv_x, kv_y, kv_rest)
    order = list(kv)
    kv_pieces = [piece for key in order for piece in kv[key]]
    at = jnp.stack(
        [place(my_y + dy, my_x + dx, core ^ rc) * deep for dy, dx in order for rc in range(2)]
    ).astype(jnp.int32)
    early = 2 * (ny + nx - 1)

    own_product = project(product_kernel, at, [own_rows], [], kv_pieces, F32)
    reach = filters.shape[0] - 1
    pad = -(-reach // 16) * 16
    ends = [
        lax.ppermute(own_rows[length - pad :], "seq", [(2 * i + 1, 2 * i + 2 + c) for i in range(chips - 1)])
        for c in range(2)
    ]
    before = jnp.where(core == 0, ends[0], ends[1])
    ready = (own_rows, q_x, q_y, own_product, before)
    rows_then, q_x, q_y, own_product, before = lax.optimization_barrier(ready)
    other_rows = from_partner(rows_then)
    q_rest = crossed(q_x, q_y)
    q_pairs = {(0, 0): both_q, **q_x, **q_y}
    q_early = [q_pairs[key] for key in order if key in q_pairs]
    own_query = project(query_kernel, at, [own_rows], [], q_early, F32)
    other_rows, own_query = lax.optimization_barrier((other_rows, own_query))
    rim, other_product = project_joined(at, before, other_rows, kv_pieces)
    own_tail, other_tail = own_product[length - pad :], other_product[length - pad :]
    first_tail = jnp.where(core == 0, own_tail, other_tail)
    groups = filters.shape[1] // 2
    taps = jnp.repeat(
        lax.dynamic_slice_in_dim(filters, core * groups, groups, axis=1), half // groups, axis=1
    )
    own_filtered = causal_filter(at, own_product, jnp.where(core == 0, rim, first_tail), taps)
    other_filtered = causal_filter(at, other_product, jnp.where(core == 0, first_tail, rim), taps)

    other_rows, own_filtered, other_filtered = lax.optimization_barrier(
        (other_rows, own_filtered, other_filtered)
    )
    other_query = project(query_kernel, at, [other_rows], [], q_early, F32)
    both_o, q_x, q_y = lax.optimization_barrier((both_o, q_x, q_y))
    o_x = {(0, dx): from_chip(both_o, 0, dx) for dx in range(1, nx)}
    o_y = {(dy, 0): from_chip(both_o, dy, 0) for dy in range(1, ny)}
    late = [piece for pair in q_rest.values() for piece in pair]
    other_gated = project(
        gate_kernel, at[early:], [other_rows], [other_filtered, other_query], late, BF16
    )
    own_gated = project(
        gate_kernel, at[early:], [own_rows], [own_filtered, own_query], late, BF16
    )

    position = lax.axis_index("tp")
    z = position.astype(jnp.int32).reshape(1)
    up = [(i, i + 1) for i in range(n_tp - 1)]
    down = [(i + 1, i) for i in range(n_tp - 1)]

    def plus(a, b):
        return (a.astype(F32) + b.astype(F32)).astype(BF16)

    def leaving_of(pairs, gates, turned):
        return from_partner(terms(n_tp, z, gates[1], pairs, (1, 0), turned))

    def terms_of(pairs, gates, turned, given):
        return terms(n_tp, z, gates[0], pairs, (0, 1), turned, given)

    def chained(slots):
        rising = falling = None
        for step in range(n_tp - 1):
            send_up, send_down = slots[n_tp - 1 - step], slots[step + 1]
            if step:
                send_up, send_down = plus(send_up, rising), plus(send_down, falling)
            rising = lax.ppermute(send_up, "tp", up)
            falling = lax.ppermute(send_down, "tp", down)
        total = slots[0].astype(F32) + rising.astype(F32) + falling.astype(F32)
        return total

    o_rest = crossed(o_x, o_y)
    out_pairs = {(0, 0): both_o, **o_x, **o_y, **o_rest}
    result = jnp.zeros((rows, model), BF16)
    gates = (own_gated, other_gated)
    sets = [(0, 0), *o_x, *o_y], list(o_rest)
    first, last = ([out_pairs[key] for key in keys] for keys in sets)
    found = terms_of(first, gates, False, leaving_of(first, gates, False))
    gates, found = lax.optimization_barrier((gates, found))
    first_sum = lax.psum_scatter(found, "tp", scatter_dimension=0, tiled=True).astype(F32)
    last_sum = chained(terms_of(last, gates, True, leaving_of(last, gates, True)))
    for keys, mixed in zip(sets, (first_sum, last_sum)):
        for index, (dy, dx) in enumerate(keys):
            start = place(my_y + dy, my_x + dx, 0) * wide
            pair = mixed[:, index * 2 * wide : (index + 1) * 2 * wide]
            swapped = jnp.concatenate([pair[:, wide:], pair[:, :wide]], axis=1)
            kept = lax.dynamic_slice_in_dim(keep_mask, start, 2 * wide, axis=1).astype(F32)
            base = lax.dynamic_slice_in_dim(tokens, start, 2 * wide, axis=1).astype(F32)
            pair = jnp.where(core == 0, pair, swapped)
            part = (base + kept * pair * (1.0 / 0.9)).astype(BF16)
            result = lax.dynamic_update_slice_in_dim(result, part, start, axis=1)
    return result


def solution(mesh):
    in_specs = (
        P(("seq", "tp"), None),
        P(),
        P(None, "seq", "tp"),
        P(None, "tp"),
        P("tp", "seq"),
        P(("seq", "tp"), None),
    )
    out_specs = P(("seq", "tp"), None)
    return jax.shard_map(
        on_device, mesh=mesh, in_specs=in_specs, out_specs=out_specs, check_vma=False
    )
```

```python
import functools
import math

import jax
import jax.numpy as jnp
from jax import lax
from jax.experimental import pallas as pl
from jax.experimental.pallas import tpu as pltpu
from jax.sharding import PartitionSpec as P

F32 = jnp.float32
BF16 = jnp.bfloat16
GRANT = 12 << 20
WHOLE = pl.BlockSpec(memory_space=pltpu.VMEM)


def grid_of(chips):
    ny = max(d for d in range(1, math.isqrt(chips) + 1) if chips % d == 0)
    return ny, chips // ny


def dot(a, b):
    return jnp.dot(a, b, preferred_element_type=F32)


def columns_of(x_ref, at_ref, index, deep):
    return x_ref[:, pl.ds(pl.multiple_of(at_ref[index], deep), deep)]


def tiles_of(out_ref):
    tile = math.gcd(out_ref.shape[1], 256)
    return [slice(at, at + tile) for at in range(0, out_ref.shape[1], tile)]


def blocks_of(xs, out_ref):
    tile = math.gcd(out_ref.shape[1], 256)
    size = xs[0].shape[0]
    for at in range(0, out_ref.shape[1], tile):
        for index, x_ref in enumerate(xs):
            yield x_ref, slice(index * size, (index + 1) * size), slice(at, at + tile)


def product_kernel(parts, at_ref, *refs):
    xs, pieces, out_ref = refs[:parts], refs[parts:-1], refs[-1]
    deep = pieces[0].shape[1]
    for x_ref, rows, tile in blocks_of(xs, out_ref):
        key = value = None
        for index, piece in enumerate(pieces):
            x = columns_of(x_ref, at_ref, index, deep)
            new_key, new_value = dot(x, piece[0, :, tile]), dot(x, piece[1, :, tile])
            key = new_key if key is None else key + new_key
            value = new_value if value is None else value + new_value
        out_ref[rows, tile] = key.astype(BF16).astype(F32) * value.astype(BF16).astype(F32)


def joined_kernel(at_ref, before_ref, x_ref, *refs):
    pieces, (rim_ref, out_ref, joined) = refs[:-3], refs[-3:]
    pad = before_ref.shape[0]
    joined[:pad] = before_ref[...]
    joined[pad:] = x_ref[...]
    deep = pieces[0].shape[1]
    for _, _, tile in blocks_of([x_ref], out_ref):
        key = value = None
        for index, piece in enumerate(pieces):
            x = columns_of(joined, at_ref, index, deep)
            new_key, new_value = dot(x, piece[0, :, tile]), dot(x, piece[1, :, tile])
            key = new_key if key is None else key + new_key
            value = new_value if value is None else value + new_value
        product = key.astype(BF16).astype(F32) * value.astype(BF16).astype(F32)
        rim_ref[:, tile] = product[:pad]
        out_ref[:, tile] = product[pad:]


def query_kernel(parts, at_ref, *refs):
    xs, pairs, out_ref = refs[:parts], refs[parts:-1], refs[-1]
    deep = pairs[0].shape[1]
    for x_ref, rows, tile in blocks_of(xs, out_ref):
        query = None
        for index in range(2 * len(pairs)):
            x = columns_of(x_ref, at_ref, index, deep)
            new = dot(x, pairs[index // 2][index % 2, :, tile])
            query = new if query is None else query + new
        out_ref[rows, tile] = query


def gate_kernel(parts, at_ref, *refs):
    xs, refs = refs[:parts], refs[parts:]
    filtered_ref, partial_ref, pieces, out_ref = refs[0], refs[1], refs[2:-1], refs[-1]
    deep = pieces[0].shape[0]
    for x_ref, rows, tile in blocks_of(xs, out_ref):
        query = partial_ref[rows, tile]
        for index, piece in enumerate(pieces):
            query = query + dot(columns_of(x_ref, at_ref, index, deep), piece[:, tile])
        gated = query.astype(BF16).astype(F32) * filtered_ref[rows, tile]
        out_ref[rows, tile] = gated.astype(BF16)


def call(kernel, scalars, operands, out, scratch=()):
    return pl.pallas_call(
        kernel,
        out_shape=out,
        in_specs=[pl.BlockSpec(memory_space=pltpu.SMEM)] + [WHOLE] * len(operands),
        out_specs=jax.tree.map(lambda _: WHOLE, out),
        scratch_shapes=scratch,
        compiler_params=pltpu.CompilerParams(vmem_limit_bytes=GRANT),
        cost_estimate=pl.CostEstimate(flops=1, bytes_accessed=1, transcendentals=0),
    )(scalars, *operands)


def project(kernel, at, xs, extra, pieces, out_dtype):
    rows = sum(x.shape[0] for x in xs)
    out = jax.ShapeDtypeStruct((rows, pieces[0].shape[-1]), out_dtype)
    return call(functools.partial(kernel, len(xs)), at, (*xs, *extra, *pieces), out)


def project_joined(at, before, x, pieces):
    half = pieces[0].shape[-1]
    pad, length = before.shape[0], x.shape[0]
    out = [jax.ShapeDtypeStruct((rows, half), F32) for rows in (pad, length)]
    scratch = [pltpu.VMEM((pad + length, x.shape[1]), BF16)]
    return call(joined_kernel, at, (before, x, *pieces), out, scratch)


def filter_kernel(_, product_ref, halo_ref, taps_ref, out_ref, held):
    length, pad = product_ref.shape[0], halo_ref.shape[0]
    held[:pad] = halo_ref[...]
    held[pad:] = product_ref[...]
    for tile in tiles_of(out_ref):
        total = None
        for offset in range(taps_ref.shape[0]):
            term = taps_ref[offset : offset + 1, tile] * held[pad - offset : pad - offset + length, tile]
            total = term if total is None else total + term
        out_ref[:, tile] = total


def causal_filter(at, product, halo, taps):
    length, half = product.shape
    out = jax.ShapeDtypeStruct(product.shape, F32)
    scratch = [pltpu.VMEM((halo.shape[0] + length, half), F32)]
    return call(filter_kernel, at, (product, halo, taps), out, scratch)


def terms_kernel(plan, turned, n_tp, at_ref, *refs):
    gates, refs, held = refs[:4], refs[4:-1], refs[-1]
    count = sum(len(parts) for parts in plan)
    weights, outs = refs[:count], refs[count:]
    half = gates[0].shape[1]
    rows = gates[0].shape[0] // n_tp
    for slot in range(n_tp):
        for index, gate in enumerate(gates):
            side, whose = index % 2, index // 2
            place = slice((2 * slot + whose) * rows, (2 * slot + whose + 1) * rows)
            owner = lax.rem(at_ref[1] + slot, n_tp) * rows if turned else slot * rows
            column = (at_ref[0] if side == 0 else 1 - at_ref[0]) * half
            taken = gate[pl.ds(pl.multiple_of(owner, rows), rows)]
            held[place, pl.ds(pl.multiple_of(column, half), half)] = taken
    wide = weights[0].shape[1]
    share = held.shape[0] // len(outs)
    used = 0
    for index, parts in enumerate(plan):
        at = slice(index * wide, (index + 1) * wide)
        for piece in range(0, held.shape[0], share):
            total, depth = None, 0
            for which in range(len(parts)):
                weight = weights[used + which]
                low, depth = depth, depth + weight.shape[0]
                new = dot(held[piece : piece + share, low:depth], weight[...])
                total = new if total is None else total + new
            outs[piece // share][:, at] = total.astype(BF16)
        used += len(parts)


def terms(n_tp, place, gates, blocks, turned):
    length, half = gates[0].shape
    weights = [part for parts in blocks for part in parts]
    cols = len(blocks) * weights[0].shape[1]
    slots = n_tp if turned else 1
    out = [jax.ShapeDtypeStruct((2 * length // slots, cols), BF16)] * slots
    kernel = functools.partial(terms_kernel, blocks_plan(blocks), turned, n_tp)
    scratch = [pltpu.VMEM((2 * length, 2 * half), BF16)]
    result = call(kernel, place, (*gates, *weights), out, scratch)
    return result if turned else result[0]


def blocks_plan(blocks):
    return [range(len(parts)) for parts in blocks]


def on_device(tokens, norm_gain, in_weight, filters, out_weight, keep_mask):
    n_seq, n_tp = lax.axis_size("seq"), lax.axis_size("tp")
    chips = n_seq // 2
    ny, nx = grid_of(chips)
    seq = lax.axis_index("seq")
    core, here = seq % 2, seq // 2
    my_y, my_x = here // nx, here % nx
    rows, model = tokens.shape
    length = rows * n_tp
    deep, channels = in_weight.shape[1:]
    half = channels // 2
    wide = out_weight.shape[1]

    def place(y, x, c):
        return ((y % ny) * nx + x % nx) * 2 + c

    def from_chip(block, dy, dx):
        route = [
            (place(y + dy, x + dx, c), place(y, x, c))
            for y in range(ny)
            for x in range(nx)
            for c in range(2)
        ]
        return lax.ppermute(block, "seq", route)

    def from_partner(block):
        return lax.ppermute(block, "seq", [(s, s ^ 1) for s in range(n_seq)])

    def direct(mine, brought):
        along_x = [(mine, brought)]
        along_y = [(mine, brought)]
        along_x += [tuple(from_chip(b, 0, dx) for b in (mine, brought)) for dx in range(1, nx)]
        along_y += [tuple(from_chip(b, dy, 0) for b in (mine, brought)) for dy in range(1, ny)]
        return along_x, along_y

    def onward(along_x, along_y):
        return {
            (dy, dx): (from_chip(along_x[dx][0], dy, 0), from_chip(along_y[dy][1], 0, dx))
            for dy in range(1, ny)
            for dx in range(1, nx)
        }

    def crossed(along_x, along_y):
        return {
            (dy, dx): (from_chip(along_x[0, dx][0], dy, 0), from_chip(along_y[dy, 0][1], 0, dx))
            for dy, _ in along_y
            for _, dx in along_x
        }

    def listed(along_x, along_y, rest):
        found = {(0, dx): pair for dx, pair in enumerate(along_x)}
        found.update({(dy, 0): pair for dy, pair in enumerate(along_y)})
        found.update(rest)
        return found

    def by_core(mine, other, axis):
        return jnp.where(
            core == 0,
            jnp.concatenate([mine, other], axis=axis),
            jnp.concatenate([other, mine], axis=axis),
        )

    def columns(array, first, count, at):
        return lax.dynamic_slice(array, (first, 0, at * half), (count, deep, half))

    mine_kv = columns(in_weight, 1, 2, core)
    away_kv = columns(in_weight, 1, 2, 1 - core)
    brought_kv = from_partner(away_kv)
    kv_x, kv_y = direct(mine_kv, brought_kv)

    tokens_then, _ = lax.optimization_barrier((tokens, away_kv))
    widened = tokens_then.astype(F32)
    mean_sq = jnp.mean(widened * widened, axis=1, keepdims=True)
    normed = (widened * lax.rsqrt(mean_sq + 1e-06) * norm_gain).astype(BF16)
    own_rows = lax.all_gather(normed, "tp", axis=0, tiled=True)
    in_weight_then, _ = lax.optimization_barrier((in_weight, normed))
    mine_q = columns(in_weight_then, 0, 1, core)[0]
    both_q = jnp.stack([mine_q, from_partner(columns(in_weight_then, 0, 1, 1 - core)[0])])

    kv_x, kv_y, both_q = lax.optimization_barrier((kv_x, kv_y, both_q))
    kv_rest = onward(kv_x, kv_y)
    q_x = {(0, dx): from_chip(both_q, 0, dx) for dx in range(1, nx)}
    q_y = {(dy, 0): from_chip(both_q, dy, 0) for dy in range(1, ny)}
    arrived = (kv_x, kv_y, kv_rest)
    own_rows, arrived = lax.optimization_barrier((own_rows, arrived))
    kv_x, kv_y, kv_rest = arrived
    kv = listed(kv_x, kv_y, kv_rest)
    order = list(kv)
    kv_pieces = [piece for key in order for piece in kv[key]]
    at = jnp.stack(
        [place(my_y + dy, my_x + dx, core ^ rc) * deep for dy, dx in order for rc in range(2)]
    ).astype(jnp.int32)
    early = 2 * (ny + nx - 1)

    own_product = project(product_kernel, at, [own_rows], [], kv_pieces, F32)
    reach = filters.shape[0] - 1
    pad = -(-reach // 16) * 16
    ends = [
        lax.ppermute(own_rows[length - pad :], "seq", [(2 * i + 1, 2 * i + 2 + c) for i in range(chips - 1)])
        for c in range(2)
    ]
    before = jnp.where(core == 0, ends[0], ends[1])
    ready = (own_rows, q_x, q_y, own_product, before)
    rows_then, q_x, q_y, own_product, before = lax.optimization_barrier(ready)
    other_rows = from_partner(rows_then)
    q_rest = crossed(q_x, q_y)
    q_pairs = {(0, 0): both_q, **q_x, **q_y}
    q_early = [q_pairs[key] for key in order if key in q_pairs]
    own_query = project(query_kernel, at, [own_rows], [], q_early, F32)
    other_rows, own_query = lax.optimization_barrier((other_rows, own_query))
    rim, other_product = project_joined(at, before, other_rows, kv_pieces)
    own_tail, other_tail = own_product[length - pad :], other_product[length - pad :]
    first_tail = jnp.where(core == 0, own_tail, other_tail)
    groups = filters.shape[1] // 2
    taps = jnp.repeat(
        lax.dynamic_slice_in_dim(filters, core * groups, groups, axis=1), half // groups, axis=1
    )
    own_filtered = causal_filter(at, own_product, jnp.where(core == 0, rim, first_tail), taps)
    other_filtered = causal_filter(at, other_product, jnp.where(core == 0, first_tail, rim), taps)

    other_rows, own_filtered, other_filtered = lax.optimization_barrier(
        (other_rows, own_filtered, other_filtered)
    )
    other_query = project(query_kernel, at, [other_rows], [], q_early, F32)
    weight_then, q_x, q_y = lax.optimization_barrier((out_weight, q_x, q_y))
    o_x = {(0, dx): from_chip(weight_then, 0, dx) for dx in range(1, nx)}
    o_y = {(dy, 0): from_chip(weight_then, dy, 0) for dy in range(1, ny)}
    o_rest = {
        (dy, dx): (
            from_chip(o_x[0, dx][:half], dy, 0),
            from_chip(o_y[dy, 0][half:], 0, dx),
        )
        for dy in range(1, ny)
        for dx in range(1, nx)
    }
    late = [piece for pair in q_rest.values() for piece in pair]
    other_gated = project(
        gate_kernel, at[early:], [other_rows], [other_filtered, other_query], late, BF16
    )
    own_gated = project(
        gate_kernel, at[early:], [own_rows], [own_filtered, own_query], late, BF16
    )
    gates = (own_gated, from_partner(other_gated), other_gated, from_partner(own_gated))

    position = lax.axis_index("tp")
    here_at = jnp.stack([core, position]).astype(jnp.int32)
    up = [(i, i + 1) for i in range(n_tp - 1)]
    down = [(i + 1, i) for i in range(n_tp - 1)]

    def plus(a, b):
        return (a.astype(F32) + b.astype(F32)).astype(BF16)

    def chained(slots):
        rising = falling = None
        for step in range(n_tp - 1):
            send_up, send_down = slots[n_tp - 1 - step], slots[step + 1]
            if step:
                send_up, send_down = plus(send_up, rising), plus(send_down, falling)
            rising = lax.ppermute(send_up, "tp", up)
            falling = lax.ppermute(send_down, "tp", down)
        total = slots[0].astype(F32) + rising.astype(F32) + falling.astype(F32)
        return total

    near = {(0, 0): (out_weight,)}
    near.update({key: (block,) for key, block in (*o_x.items(), *o_y.items())})
    found = terms(n_tp, here_at, gates, list(near.values()), False)
    gates, found = lax.optimization_barrier((gates, found))
    near_sum = lax.psum_scatter(found, "tp", scatter_dimension=0, tiled=True)
    far_sum = chained(terms(n_tp, here_at, gates, list(o_rest.values()), True))
    result = jnp.zeros((rows, model), BF16)
    for keys, mixed in ((list(near), near_sum), (list(o_rest), far_sum)):
        theirs = from_partner(mixed[rows:].astype(BF16)).astype(F32)
        mine = mixed[:rows].astype(F32)
        for index, (dy, dx) in enumerate(keys):
            start = place(my_y + dy, my_x + dx, 0) * wide
            here_columns = slice(index * wide, (index + 1) * wide)
            pair = by_core(mine[:, here_columns], theirs[:, here_columns], 1)
            kept = lax.dynamic_slice_in_dim(keep_mask, start, 2 * wide, axis=1).astype(F32)
            base = lax.dynamic_slice_in_dim(tokens, start, 2 * wide, axis=1).astype(F32)
            part = (base + kept * pair * (1.0 / 0.9)).astype(BF16)
            result = lax.dynamic_update_slice_in_dim(result, part, start, axis=1)
    return result


def solution(mesh):
    in_specs = (
        P(("seq", "tp"), None),
        P(),
        P(None, "seq", "tp"),
        P(None, "tp"),
        P("tp", "seq"),
        P(("seq", "tp"), None),
    )
    out_specs = P(("seq", "tp"), None)
    return jax.shard_map(
        on_device, mesh=mesh, in_specs=in_specs, out_specs=out_specs, check_vma=False
    )
```

```python
import functools
import math

import jax
import jax.numpy as jnp
from jax import lax
from jax.experimental import pallas as pl
from jax.experimental.pallas import tpu as pltpu
from jax.sharding import PartitionSpec as P

F32 = jnp.float32
BF16 = jnp.bfloat16
GRANT = 12 << 20
WHOLE = pl.BlockSpec(memory_space=pltpu.VMEM)


def grid_of(chips):
    ny = max(d for d in range(1, math.isqrt(chips) + 1) if chips % d == 0)
    return ny, chips // ny


def dot(a, b):
    return jnp.dot(a, b, preferred_element_type=F32)


def columns_of(x_ref, at_ref, index, deep):
    return x_ref[:, pl.ds(pl.multiple_of(at_ref[index], deep), deep)]


def tiles_of(out_ref):
    tile = math.gcd(out_ref.shape[1], 256)
    return [slice(at, at + tile) for at in range(0, out_ref.shape[1], tile)]


def blocks_of(xs, out_ref):
    tile = math.gcd(out_ref.shape[1], 256)
    size = xs[0].shape[0]
    for at in range(0, out_ref.shape[1], tile):
        for index, x_ref in enumerate(xs):
            yield x_ref, slice(index * size, (index + 1) * size), slice(at, at + tile)


def query_kernel(parts, at_ref, *refs):
    xs, pairs, out_ref = refs[:parts], refs[parts:-1], refs[-1]
    deep = pairs[0].shape[1]
    for x_ref, rows, tile in blocks_of(xs, out_ref):
        query = None
        for index in range(2 * len(pairs)):
            x = columns_of(x_ref, at_ref, index, deep)
            new = dot(x, pairs[index // 2][index % 2, :, tile])
            query = new if query is None else query + new
        out_ref[rows, tile] = query


def gate_kernel(parts, at_ref, *refs):
    xs, refs = refs[:parts], refs[parts:]
    filtered_ref, partial_ref, pieces, out_ref = refs[0], refs[1], refs[2:-1], refs[-1]
    deep = pieces[0].shape[0]
    for x_ref, rows, tile in blocks_of(xs, out_ref):
        query = partial_ref[rows, tile]
        for index, piece in enumerate(pieces):
            query = query + dot(columns_of(x_ref, at_ref, index, deep), piece[:, tile])
        gated = query.astype(BF16).astype(F32) * filtered_ref[rows, tile]
        out_ref[rows, tile] = gated.astype(BF16)


def call(kernel, scalars, operands, out, scratch=()):
    return pl.pallas_call(
        kernel,
        out_shape=out,
        in_specs=[pl.BlockSpec(memory_space=pltpu.SMEM)] + [WHOLE] * len(operands),
        out_specs=jax.tree.map(lambda _: WHOLE, out),
        scratch_shapes=scratch,
        compiler_params=pltpu.CompilerParams(vmem_limit_bytes=GRANT),
        cost_estimate=pl.CostEstimate(flops=1, bytes_accessed=1, transcendentals=0),
    )(scalars, *operands)


def project(kernel, at, xs, extra, pieces, out_dtype):
    rows = sum(x.shape[0] for x in xs)
    out = jax.ShapeDtypeStruct((rows, pieces[0].shape[-1]), out_dtype)
    return call(functools.partial(kernel, len(xs)), at, (*xs, *extra, *pieces), out)


def product_kernel(parts, count, at_ref, *refs):
    xs, refs = refs[:parts], refs[parts:]
    given, refs = refs[:count], refs[count:]
    outs, (joined, *pieces, sems) = refs[:parts], refs[parts:]
    ends = [0]
    for x_ref in xs:
        ends.append(ends[-1] + x_ref.shape[0])
    targets = [joined.at[low:high] for low, high in zip(ends, ends[1:])] + list(pieces)
    copies = [
        pltpu.make_async_copy(source, target, sems.at[index])
        for index, (source, target) in enumerate(zip((*xs, *given), targets))
    ]
    for copy in copies:
        copy.start()
    for copy in copies[:parts]:
        copy.wait()
    deep = pieces[0].shape[1]
    half = pieces[0].shape[2]
    tile = math.gcd(half, 256)
    for low in range(0, half, tile):
        columns = slice(low, low + tile)
        key = value = None
        for index, piece in enumerate(pieces):
            if low == 0:
                copies[parts + index].wait()
            x = columns_of(joined, at_ref, index, deep)
            new_key, new_value = dot(x, piece[0, :, columns]), dot(x, piece[1, :, columns])
            key = new_key if key is None else key + new_key
            value = new_value if value is None else value + new_value
        product = key.astype(BF16).astype(F32) * value.astype(BF16).astype(F32)
        for out, start, end in zip(outs, ends, ends[1:]):
            out[:, columns] = product[start:end]


def products(at, xs, pieces):
    half = pieces[0].shape[2]
    held = [pltpu.VMEM((sum(x.shape[0] for x in xs), xs[0].shape[1]), BF16)]
    held += [pltpu.VMEM(piece.shape, BF16) for piece in pieces]
    held.append(pltpu.SemaphoreType.DMA((len(xs) + len(pieces),)))
    return pl.pallas_call(
        functools.partial(product_kernel, len(xs), len(pieces)),
        out_shape=[jax.ShapeDtypeStruct((x.shape[0], half), F32) for x in xs],
        in_specs=[pl.BlockSpec(memory_space=pltpu.SMEM)]
        + [pl.BlockSpec(memory_space=pl.ANY)] * (len(xs) + len(pieces)),
        out_specs=[WHOLE] * len(xs),
        scratch_shapes=held,
        compiler_params=pltpu.CompilerParams(vmem_limit_bytes=2 * GRANT),
        cost_estimate=pl.CostEstimate(flops=1, bytes_accessed=1, transcendentals=0),
    )(at, *xs, *pieces)


def filter_kernel(_, product_ref, halo_ref, taps_ref, out_ref, held):
    length, pad = product_ref.shape[0], halo_ref.shape[0]
    held[:pad] = halo_ref[...]
    held[pad:] = product_ref[...]
    for tile in tiles_of(out_ref):
        total = None
        for offset in range(taps_ref.shape[0]):
            term = taps_ref[offset : offset + 1, tile] * held[pad - offset : pad - offset + length, tile]
            total = term if total is None else total + term
        out_ref[:, tile] = total


def causal_filter(at, product, halo, taps):
    length, half = product.shape
    out = jax.ShapeDtypeStruct(product.shape, F32)
    scratch = [pltpu.VMEM((halo.shape[0] + length, half), F32)]
    return call(filter_kernel, at, (product, halo, taps), out, scratch)


def terms_kernel(plan, turned, n_tp, at_ref, *refs):
    gates, refs, held = refs[:4], refs[4:-1], refs[-1]
    count = sum(len(parts) for parts in plan)
    weights, outs = refs[:count], refs[count:]
    half = gates[0].shape[1]
    rows = gates[0].shape[0] // n_tp
    for slot in range(n_tp):
        for index, gate in enumerate(gates):
            side, whose = index % 2, index // 2
            place = slice((2 * slot + whose) * rows, (2 * slot + whose + 1) * rows)
            owner = lax.rem(at_ref[1] + slot, n_tp) * rows if turned else slot * rows
            column = (at_ref[0] if side == 0 else 1 - at_ref[0]) * half
            taken = gate[pl.ds(pl.multiple_of(owner, rows), rows)]
            held[place, pl.ds(pl.multiple_of(column, half), half)] = taken
    wide = weights[0].shape[1]
    share = held.shape[0] // len(outs)
    used = 0
    for index, parts in enumerate(plan):
        at = slice(index * wide, (index + 1) * wide)
        for piece in range(0, held.shape[0], share):
            total, depth = None, 0
            for which in range(len(parts)):
                weight = weights[used + which]
                low, depth = depth, depth + weight.shape[0]
                new = dot(held[piece : piece + share, low:depth], weight[...])
                total = new if total is None else total + new
            outs[piece // share][:, at] = total.astype(BF16)
        used += len(parts)


def terms(n_tp, place, gates, blocks, turned):
    length, half = gates[0].shape
    weights = [part for parts in blocks for part in parts]
    cols = len(blocks) * weights[0].shape[1]
    slots = n_tp if turned else 1
    out = [jax.ShapeDtypeStruct((2 * length // slots, cols), BF16)] * slots
    kernel = functools.partial(terms_kernel, blocks_plan(blocks), turned, n_tp)
    scratch = [pltpu.VMEM((2 * length, 2 * half), BF16)]
    result = call(kernel, place, (*gates, *weights), out, scratch)
    return result if turned else result[0]


def blocks_plan(blocks):
    return [range(len(parts)) for parts in blocks]


def on_device(tokens, norm_gain, in_weight, filters, out_weight, keep_mask):
    n_seq, n_tp = lax.axis_size("seq"), lax.axis_size("tp")
    chips = n_seq // 2
    ny, nx = grid_of(chips)
    seq = lax.axis_index("seq")
    core, here = seq % 2, seq // 2
    my_y, my_x = here // nx, here % nx
    rows, model = tokens.shape
    length = rows * n_tp
    deep, channels = in_weight.shape[1:]
    half = channels // 2
    wide = out_weight.shape[1]

    def place(y, x, c):
        return ((y % ny) * nx + x % nx) * 2 + c

    def from_chip(block, dy, dx):
        route = [
            (place(y + dy, x + dx, c), place(y, x, c))
            for y in range(ny)
            for x in range(nx)
            for c in range(2)
        ]
        return lax.ppermute(block, "seq", route)

    def from_partner(block):
        return lax.ppermute(block, "seq", [(s, s ^ 1) for s in range(n_seq)])

    def direct(mine, brought):
        along_x = [(mine, brought)]
        along_y = [(mine, brought)]
        along_x += [tuple(from_chip(b, 0, dx) for b in (mine, brought)) for dx in range(1, nx)]
        along_y += [tuple(from_chip(b, dy, 0) for b in (mine, brought)) for dy in range(1, ny)]
        return along_x, along_y

    def onward(along_x, along_y):
        return {
            (dy, dx): (from_chip(along_x[dx][0], dy, 0), from_chip(along_y[dy][1], 0, dx))
            for dy in range(1, ny)
            for dx in range(1, nx)
        }

    def crossed(along_x, along_y):
        return {
            (dy, dx): (from_chip(along_x[0, dx][0], dy, 0), from_chip(along_y[dy, 0][1], 0, dx))
            for dy, _ in along_y
            for _, dx in along_x
        }

    def listed(along_x, along_y, rest):
        found = {(0, dx): pair for dx, pair in enumerate(along_x)}
        found.update({(dy, 0): pair for dy, pair in enumerate(along_y)})
        found.update(rest)
        return found

    def by_core(mine, other, axis):
        return jnp.where(
            core == 0,
            jnp.concatenate([mine, other], axis=axis),
            jnp.concatenate([other, mine], axis=axis),
        )

    def columns(array, first, count, at):
        return lax.dynamic_slice(array, (first, 0, at * half), (count, deep, half))

    mine_kv = columns(in_weight, 1, 2, core)
    away_kv = columns(in_weight, 1, 2, 1 - core)
    brought_kv = from_partner(away_kv)
    kv_x, kv_y = direct(mine_kv, brought_kv)

    tokens_then, _ = lax.optimization_barrier((tokens, away_kv))
    widened = tokens_then.astype(F32)
    mean_sq = jnp.mean(widened * widened, axis=1, keepdims=True)
    normed = (widened * lax.rsqrt(mean_sq + 1e-06) * norm_gain).astype(BF16)
    own_rows = lax.all_gather(normed, "tp", axis=0, tiled=True)
    in_weight_then, _ = lax.optimization_barrier((in_weight, normed))
    mine_q = columns(in_weight_then, 0, 1, core)[0]
    both_q = jnp.stack([mine_q, from_partner(columns(in_weight_then, 0, 1, 1 - core)[0])])

    kv_x, kv_y, both_q = lax.optimization_barrier((kv_x, kv_y, both_q))
    kv_rest = onward(kv_x, kv_y)
    q_x = {(0, dx): from_chip(both_q, 0, dx) for dx in range(1, nx)}
    q_y = {(dy, 0): from_chip(both_q, dy, 0) for dy in range(1, ny)}
    arrived = (kv_x, kv_y, kv_rest)
    own_rows, arrived = lax.optimization_barrier((own_rows, arrived))
    kv_x, kv_y, kv_rest = arrived
    kv = listed(kv_x, kv_y, kv_rest)
    order = list(kv)
    kv_pieces = [piece for key in order for piece in kv[key]]
    at = jnp.stack(
        [place(my_y + dy, my_x + dx, core ^ rc) * deep for dy, dx in order for rc in range(2)]
    ).astype(jnp.int32)
    early = 2 * (ny + nx - 1)

    (own_product,) = products(at, [own_rows], kv_pieces)
    reach = filters.shape[0] - 1
    pad = -(-reach // 16) * 16
    ends = [
        lax.ppermute(own_rows[length - pad :], "seq", [(2 * i + 1, 2 * i + 2 + c) for i in range(chips - 1)])
        for c in range(2)
    ]
    before = jnp.where(core == 0, ends[0], ends[1])
    ready = (own_rows, q_x, q_y, own_product, before)
    rows_then, q_x, q_y, own_product, before = lax.optimization_barrier(ready)
    other_rows = from_partner(rows_then)
    q_rest = crossed(q_x, q_y)
    q_pairs = {(0, 0): both_q, **q_x, **q_y}
    q_early = [q_pairs[key] for key in order if key in q_pairs]
    own_query = project(query_kernel, at, [own_rows], [], q_early, F32)
    other_rows, own_query = lax.optimization_barrier((other_rows, own_query))
    rim, other_product = products(at, [before, other_rows], kv_pieces)
    own_tail, other_tail = own_product[length - pad :], other_product[length - pad :]
    first_tail = jnp.where(core == 0, own_tail, other_tail)
    groups = filters.shape[1] // 2
    taps = jnp.repeat(
        lax.dynamic_slice_in_dim(filters, core * groups, groups, axis=1), half // groups, axis=1
    )
    own_filtered = causal_filter(at, own_product, jnp.where(core == 0, rim, first_tail), taps)
    other_filtered = causal_filter(at, other_product, jnp.where(core == 0, first_tail, rim), taps)

    other_rows, own_filtered, other_filtered = lax.optimization_barrier(
        (other_rows, own_filtered, other_filtered)
    )
    other_query = project(query_kernel, at, [other_rows], [], q_early, F32)
    weight_then, q_x, q_y = lax.optimization_barrier((out_weight, q_x, q_y))
    o_x = {(0, dx): from_chip(weight_then, 0, dx) for dx in range(1, nx)}
    o_y = {(dy, 0): from_chip(weight_then, dy, 0) for dy in range(1, ny)}
    o_rest = {
        (dy, dx): (
            from_chip(o_x[0, dx][:half], dy, 0),
            from_chip(o_y[dy, 0][half:], 0, dx),
        )
        for dy in range(1, ny)
        for dx in range(1, nx)
    }
    late = [piece for pair in q_rest.values() for piece in pair]
    other_gated = project(
        gate_kernel, at[early:], [other_rows], [other_filtered, other_query], late, BF16
    )
    own_gated = project(
        gate_kernel, at[early:], [own_rows], [own_filtered, own_query], late, BF16
    )
    gates = (own_gated, from_partner(other_gated), other_gated, from_partner(own_gated))

    position = lax.axis_index("tp")
    here_at = jnp.stack([core, position]).astype(jnp.int32)
    up = [(i, i + 1) for i in range(n_tp - 1)]
    down = [(i + 1, i) for i in range(n_tp - 1)]

    def plus(a, b):
        return (a.astype(F32) + b.astype(F32)).astype(BF16)

    def chained(slots):
        rising = falling = None
        for step in range(n_tp - 1):
            send_up, send_down = slots[n_tp - 1 - step], slots[step + 1]
            if step:
                send_up, send_down = plus(send_up, rising), plus(send_down, falling)
            rising = lax.ppermute(send_up, "tp", up)
            falling = lax.ppermute(send_down, "tp", down)
        total = slots[0].astype(F32) + rising.astype(F32) + falling.astype(F32)
        return total

    near = {(0, 0): (out_weight,)}
    near.update({key: (block,) for key, block in (*o_x.items(), *o_y.items())})
    found = terms(n_tp, here_at, gates, list(near.values()), False)
    gates, found = lax.optimization_barrier((gates, found))
    near_sum = lax.psum_scatter(found, "tp", scatter_dimension=0, tiled=True)
    far_sum = chained(terms(n_tp, here_at, gates, list(o_rest.values()), True))
    result = jnp.zeros((rows, model), BF16)
    for keys, mixed in ((list(near), near_sum), (list(o_rest), far_sum)):
        theirs = from_partner(mixed[rows:].astype(BF16)).astype(F32)
        mine = mixed[:rows].astype(F32)
        for index, (dy, dx) in enumerate(keys):
            start = place(my_y + dy, my_x + dx, 0) * wide
            here_columns = slice(index * wide, (index + 1) * wide)
            pair = by_core(mine[:, here_columns], theirs[:, here_columns], 1)
            kept = lax.dynamic_slice_in_dim(keep_mask, start, 2 * wide, axis=1).astype(F32)
            base = lax.dynamic_slice_in_dim(tokens, start, 2 * wide, axis=1).astype(F32)
            part = (base + kept * pair * (1.0 / 0.9)).astype(BF16)
            result = lax.dynamic_update_slice_in_dim(result, part, start, axis=1)
    return result


def solution(mesh):
    in_specs = (
        P(("seq", "tp"), None),
        P(),
        P(None, "seq", "tp"),
        P(None, "tp"),
        P("tp", "seq"),
        P(("seq", "tp"), None),
    )
    out_specs = P(("seq", "tp"), None)
    return jax.shard_map(
        on_device, mesh=mesh, in_specs=in_specs, out_specs=out_specs, check_vma=False
    )
```

```python
import functools
import math

import jax
import jax.numpy as jnp
from jax import lax
from jax.experimental import pallas as pl
from jax.experimental.pallas import tpu as pltpu
from jax.sharding import PartitionSpec as P

F32 = jnp.float32
BF16 = jnp.bfloat16
GRANT = 12 << 20
WHOLE = pl.BlockSpec(memory_space=pltpu.VMEM)


def grid_of(chips):
    ny = max(d for d in range(1, math.isqrt(chips) + 1) if chips % d == 0)
    return ny, chips // ny


def dot(a, b):
    return jnp.dot(a, b, preferred_element_type=F32)


def columns_of(x_ref, at_ref, index, deep):
    return x_ref[:, pl.ds(pl.multiple_of(at_ref[index], deep), deep)]


def tiles_of(out_ref):
    tile = math.gcd(out_ref.shape[1], 256)
    return [slice(at, at + tile) for at in range(0, out_ref.shape[1], tile)]


def blocks_of(xs, out_ref):
    tile = math.gcd(out_ref.shape[1], 256)
    size = xs[0].shape[0]
    for at in range(0, out_ref.shape[1], tile):
        for index, x_ref in enumerate(xs):
            yield x_ref, slice(index * size, (index + 1) * size), slice(at, at + tile)


def query_kernel(parts, at_ref, *refs):
    xs, pairs, out_ref = refs[:parts], refs[parts:-1], refs[-1]
    deep = pairs[0].shape[1]
    for x_ref, rows, tile in blocks_of(xs, out_ref):
        query = None
        for index in range(2 * len(pairs)):
            x = columns_of(x_ref, at_ref, index, deep)
            new = dot(x, pairs[index // 2][index % 2, :, tile])
            query = new if query is None else query + new
        out_ref[rows, tile] = query


def gate_kernel(parts, at_ref, *refs):
    xs, refs = refs[:parts], refs[parts:]
    filtered_ref, partial_ref, pieces, out_ref = refs[0], refs[1], refs[2:-1], refs[-1]
    deep = pieces[0].shape[0]
    for x_ref, rows, tile in blocks_of(xs, out_ref):
        query = partial_ref[rows, tile]
        for index, piece in enumerate(pieces):
            query = query + dot(columns_of(x_ref, at_ref, index, deep), piece[:, tile])
        gated = query.astype(BF16).astype(F32) * filtered_ref[rows, tile]
        out_ref[rows, tile] = gated.astype(BF16)


def call(kernel, scalars, operands, out, scratch=()):
    return pl.pallas_call(
        kernel,
        out_shape=out,
        in_specs=[pl.BlockSpec(memory_space=pltpu.SMEM)] + [WHOLE] * len(operands),
        out_specs=jax.tree.map(lambda _: WHOLE, out),
        scratch_shapes=scratch,
        compiler_params=pltpu.CompilerParams(vmem_limit_bytes=GRANT),
        cost_estimate=pl.CostEstimate(flops=1, bytes_accessed=1, transcendentals=0),
    )(scalars, *operands)


def project(kernel, at, xs, extra, pieces, out_dtype):
    rows = sum(x.shape[0] for x in xs)
    out = jax.ShapeDtypeStruct((rows, pieces[0].shape[-1]), out_dtype)
    return call(functools.partial(kernel, len(xs)), at, (*xs, *extra, *pieces), out)


def product_kernel(parts, count, at_ref, *refs):
    xs, refs = refs[:parts], refs[parts:]
    given, refs = refs[:count], refs[count:]
    outs, (joined, *pieces, sems) = refs[:parts], refs[parts:]
    ends = [0]
    for x_ref in xs:
        ends.append(ends[-1] + x_ref.shape[0])
    targets = [joined.at[low:high] for low, high in zip(ends, ends[1:])] + list(pieces)
    copies = [
        pltpu.make_async_copy(source, target, sems.at[index])
        for index, (source, target) in enumerate(zip((*xs, *given), targets))
    ]
    for copy in copies:
        copy.start()
    for copy in copies[:parts]:
        copy.wait()
    deep = pieces[0].shape[1]
    half = pieces[0].shape[2]
    tile = math.gcd(half, 256)
    for low in range(0, half, tile):
        columns = slice(low, low + tile)
        key = value = None
        for index, piece in enumerate(pieces):
            if low == 0:
                copies[parts + index].wait()
            x = columns_of(joined, at_ref, index, deep)
            new_key, new_value = dot(x, piece[0, :, columns]), dot(x, piece[1, :, columns])
            key = new_key if key is None else key + new_key
            value = new_value if value is None else value + new_value
        product = key.astype(BF16).astype(F32) * value.astype(BF16).astype(F32)
        for out, start, end in zip(outs, ends, ends[1:]):
            out[:, columns] = product[start:end]


def products(at, xs, pieces):
    half = pieces[0].shape[2]
    held = [pltpu.VMEM((sum(x.shape[0] for x in xs), xs[0].shape[1]), BF16)]
    held += [pltpu.VMEM(piece.shape, BF16) for piece in pieces]
    held.append(pltpu.SemaphoreType.DMA((len(xs) + len(pieces),)))
    return pl.pallas_call(
        functools.partial(product_kernel, len(xs), len(pieces)),
        out_shape=[jax.ShapeDtypeStruct((x.shape[0], half), F32) for x in xs],
        in_specs=[pl.BlockSpec(memory_space=pltpu.SMEM)]
        + [pl.BlockSpec(memory_space=pltpu.HBM)] * (len(xs) + len(pieces)),
        out_specs=[WHOLE] * len(xs),
        scratch_shapes=held,
        compiler_params=pltpu.CompilerParams(vmem_limit_bytes=2 * GRANT),
        cost_estimate=pl.CostEstimate(flops=1, bytes_accessed=1, transcendentals=0),
    )(at, *xs, *pieces)


def filter_kernel(_, product_ref, halo_ref, taps_ref, out_ref, held):
    length, pad = product_ref.shape[0], halo_ref.shape[0]
    held[:pad] = halo_ref[...]
    held[pad:] = product_ref[...]
    for tile in tiles_of(out_ref):
        total = None
        for offset in range(taps_ref.shape[0]):
            term = taps_ref[offset : offset + 1, tile] * held[pad - offset : pad - offset + length, tile]
            total = term if total is None else total + term
        out_ref[:, tile] = total


def causal_filter(at, product, halo, taps):
    length, half = product.shape
    out = jax.ShapeDtypeStruct(product.shape, F32)
    scratch = [pltpu.VMEM((halo.shape[0] + length, half), F32)]
    return call(filter_kernel, at, (product, halo, taps), out, scratch)


def terms_kernel(plan, turned, n_tp, at_ref, *refs):
    gates, refs, held = refs[:4], refs[4:-1], refs[-1]
    count = sum(len(parts) for parts in plan)
    weights, outs = refs[:count], refs[count:]
    half = gates[0].shape[1]
    rows = gates[0].shape[0] // n_tp
    for slot in range(n_tp):
        for index, gate in enumerate(gates):
            side, whose = index % 2, index // 2
            place = slice((2 * slot + whose) * rows, (2 * slot + whose + 1) * rows)
            owner = lax.rem(at_ref[1] + slot, n_tp) * rows if turned else slot * rows
            column = (at_ref[0] if side == 0 else 1 - at_ref[0]) * half
            taken = gate[pl.ds(pl.multiple_of(owner, rows), rows)]
            held[place, pl.ds(pl.multiple_of(column, half), half)] = taken
    wide = weights[0].shape[1]
    share = held.shape[0] // len(outs)
    used = 0
    for index, parts in enumerate(plan):
        at = slice(index * wide, (index + 1) * wide)
        for piece in range(0, held.shape[0], share):
            total, depth = None, 0
            for which in range(len(parts)):
                weight = weights[used + which]
                low, depth = depth, depth + weight.shape[0]
                new = dot(held[piece : piece + share, low:depth], weight[...])
                total = new if total is None else total + new
            outs[piece // share][:, at] = total.astype(BF16)
        used += len(parts)


def terms(n_tp, place, gates, blocks, turned):
    length, half = gates[0].shape
    weights = [part for parts in blocks for part in parts]
    cols = len(blocks) * weights[0].shape[1]
    slots = n_tp if turned else 1
    out = [jax.ShapeDtypeStruct((2 * length // slots, cols), BF16)] * slots
    kernel = functools.partial(terms_kernel, blocks_plan(blocks), turned, n_tp)
    scratch = [pltpu.VMEM((2 * length, 2 * half), BF16)]
    result = call(kernel, place, (*gates, *weights), out, scratch)
    return result if turned else result[0]


def blocks_plan(blocks):
    return [range(len(parts)) for parts in blocks]


def on_device(tokens, norm_gain, in_weight, filters, out_weight, keep_mask):
    n_seq, n_tp = lax.axis_size("seq"), lax.axis_size("tp")
    chips = n_seq // 2
    ny, nx = grid_of(chips)
    seq = lax.axis_index("seq")
    core, here = seq % 2, seq // 2
    my_y, my_x = here // nx, here % nx
    rows, model = tokens.shape
    length = rows * n_tp
    deep, channels = in_weight.shape[1:]
    half = channels // 2
    wide = out_weight.shape[1]

    def place(y, x, c):
        return ((y % ny) * nx + x % nx) * 2 + c

    def from_chip(block, dy, dx):
        route = [
            (place(y + dy, x + dx, c), place(y, x, c))
            for y in range(ny)
            for x in range(nx)
            for c in range(2)
        ]
        return lax.ppermute(block, "seq", route)

    def from_partner(block):
        return lax.ppermute(block, "seq", [(s, s ^ 1) for s in range(n_seq)])

    def direct(mine, brought):
        along_x = [(mine, brought)]
        along_y = [(mine, brought)]
        along_x += [tuple(from_chip(b, 0, dx) for b in (mine, brought)) for dx in range(1, nx)]
        along_y += [tuple(from_chip(b, dy, 0) for b in (mine, brought)) for dy in range(1, ny)]
        return along_x, along_y

    def onward(along_x, along_y):
        return {
            (dy, dx): (from_chip(along_x[dx][0], dy, 0), from_chip(along_y[dy][1], 0, dx))
            for dy in range(1, ny)
            for dx in range(1, nx)
        }

    def crossed(along_x, along_y):
        return {
            (dy, dx): (from_chip(along_x[0, dx][0], dy, 0), from_chip(along_y[dy, 0][1], 0, dx))
            for dy, _ in along_y
            for _, dx in along_x
        }

    def listed(along_x, along_y, rest):
        found = {(0, dx): pair for dx, pair in enumerate(along_x)}
        found.update({(dy, 0): pair for dy, pair in enumerate(along_y)})
        found.update(rest)
        return found

    def by_core(mine, other, axis):
        return jnp.where(
            core == 0,
            jnp.concatenate([mine, other], axis=axis),
            jnp.concatenate([other, mine], axis=axis),
        )

    def columns(array, first, count, at):
        return lax.dynamic_slice(array, (first, 0, at * half), (count, deep, half))

    mine_kv = columns(in_weight, 1, 2, core)
    away_kv = columns(in_weight, 1, 2, 1 - core)
    brought_kv = from_partner(away_kv)
    kv_x, kv_y = direct(mine_kv, brought_kv)

    tokens_then, _ = lax.optimization_barrier((tokens, away_kv))
    widened = tokens_then.astype(F32)
    mean_sq = jnp.mean(widened * widened, axis=1, keepdims=True)
    normed = (widened * lax.rsqrt(mean_sq + 1e-06) * norm_gain).astype(BF16)
    own_rows = lax.all_gather(normed, "tp", axis=0, tiled=True)
    in_weight_then, _ = lax.optimization_barrier((in_weight, normed))
    mine_q = columns(in_weight_then, 0, 1, core)[0]
    both_q = jnp.stack([mine_q, from_partner(columns(in_weight_then, 0, 1, 1 - core)[0])])

    kv_x, kv_y, both_q = lax.optimization_barrier((kv_x, kv_y, both_q))
    kv_rest = onward(kv_x, kv_y)
    q_x = {(0, dx): from_chip(both_q, 0, dx) for dx in range(1, nx)}
    q_y = {(dy, 0): from_chip(both_q, dy, 0) for dy in range(1, ny)}
    arrived = (kv_x, kv_y, kv_rest)
    own_rows, arrived = lax.optimization_barrier((own_rows, arrived))
    kv_x, kv_y, kv_rest = arrived
    kv = listed(kv_x, kv_y, kv_rest)
    order = list(kv)
    kv_pieces = [piece for key in order for piece in kv[key]]
    at = jnp.stack(
        [place(my_y + dy, my_x + dx, core ^ rc) * deep for dy, dx in order for rc in range(2)]
    ).astype(jnp.int32)
    early = 2 * (ny + nx - 1)

    (own_product,) = products(at, [own_rows], kv_pieces)
    reach = filters.shape[0] - 1
    pad = -(-reach // 16) * 16
    ends = [
        lax.ppermute(own_rows[length - pad :], "seq", [(2 * i + 1, 2 * i + 2 + c) for i in range(chips - 1)])
        for c in range(2)
    ]
    before = jnp.where(core == 0, ends[0], ends[1])
    ready = (own_rows, q_x, q_y, own_product, before)
    rows_then, q_x, q_y, own_product, before = lax.optimization_barrier(ready)
    other_rows = from_partner(rows_then)
    q_rest = crossed(q_x, q_y)
    q_pairs = {(0, 0): both_q, **q_x, **q_y}
    q_early = [q_pairs[key] for key in order if key in q_pairs]
    own_query = project(query_kernel, at, [own_rows], [], q_early, F32)
    other_rows, own_query = lax.optimization_barrier((other_rows, own_query))
    rim, other_product = products(at, [before, other_rows], kv_pieces)
    own_tail, other_tail = own_product[length - pad :], other_product[length - pad :]
    first_tail = jnp.where(core == 0, own_tail, other_tail)
    groups = filters.shape[1] // 2
    taps = jnp.repeat(
        lax.dynamic_slice_in_dim(filters, core * groups, groups, axis=1), half // groups, axis=1
    )
    own_filtered = causal_filter(at, own_product, jnp.where(core == 0, rim, first_tail), taps)
    other_filtered = causal_filter(at, other_product, jnp.where(core == 0, first_tail, rim), taps)

    other_rows, own_filtered, other_filtered = lax.optimization_barrier(
        (other_rows, own_filtered, other_filtered)
    )
    other_query = project(query_kernel, at, [other_rows], [], q_early, F32)
    weight_then, q_x, q_y = lax.optimization_barrier((out_weight, q_x, q_y))
    o_x = {(0, dx): from_chip(weight_then, 0, dx) for dx in range(1, nx)}
    o_y = {(dy, 0): from_chip(weight_then, dy, 0) for dy in range(1, ny)}
    o_rest = {
        (dy, dx): (
            from_chip(o_x[0, dx][:half], dy, 0),
            from_chip(o_y[dy, 0][half:], 0, dx),
        )
        for dy in range(1, ny)
        for dx in range(1, nx)
    }
    late = [piece for pair in q_rest.values() for piece in pair]
    other_gated = project(
        gate_kernel, at[early:], [other_rows], [other_filtered, other_query], late, BF16
    )
    own_gated = project(
        gate_kernel, at[early:], [own_rows], [own_filtered, own_query], late, BF16
    )
    gates = (own_gated, from_partner(other_gated), other_gated, from_partner(own_gated))

    position = lax.axis_index("tp")
    here_at = jnp.stack([core, position]).astype(jnp.int32)
    up = [(i, i + 1) for i in range(n_tp - 1)]
    down = [(i + 1, i) for i in range(n_tp - 1)]

    def plus(a, b):
        return (a.astype(F32) + b.astype(F32)).astype(BF16)

    def chained(slots):
        rising = falling = None
        for step in range(n_tp - 1):
            send_up, send_down = slots[n_tp - 1 - step], slots[step + 1]
            if step:
                send_up, send_down = plus(send_up, rising), plus(send_down, falling)
            rising = lax.ppermute(send_up, "tp", up)
            falling = lax.ppermute(send_down, "tp", down)
        total = slots[0].astype(F32) + rising.astype(F32) + falling.astype(F32)
        return total

    near = {(0, 0): (out_weight,)}
    near.update({key: (block,) for key, block in (*o_x.items(), *o_y.items())})
    found = terms(n_tp, here_at, gates, list(near.values()), False)
    gates, found = lax.optimization_barrier((gates, found))
    near_sum = lax.psum_scatter(found, "tp", scatter_dimension=0, tiled=True)
    far_sum = chained(terms(n_tp, here_at, gates, list(o_rest.values()), True))
    result = jnp.zeros((rows, model), BF16)
    for keys, mixed in ((list(near), near_sum), (list(o_rest), far_sum)):
        theirs = from_partner(mixed[rows:].astype(BF16)).astype(F32)
        mine = mixed[:rows].astype(F32)
        for index, (dy, dx) in enumerate(keys):
            start = place(my_y + dy, my_x + dx, 0) * wide
            here_columns = slice(index * wide, (index + 1) * wide)
            pair = by_core(mine[:, here_columns], theirs[:, here_columns], 1)
            kept = lax.dynamic_slice_in_dim(keep_mask, start, 2 * wide, axis=1).astype(F32)
            base = lax.dynamic_slice_in_dim(tokens, start, 2 * wide, axis=1).astype(F32)
            part = (base + kept * pair * (1.0 / 0.9)).astype(BF16)
            result = lax.dynamic_update_slice_in_dim(result, part, start, axis=1)
    return result


def solution(mesh):
    in_specs = (
        P(("seq", "tp"), None),
        P(),
        P(None, "seq", "tp"),
        P(None, "tp"),
        P("tp", "seq"),
        P(("seq", "tp"), None),
    )
    out_specs = P(("seq", "tp"), None)
    return jax.shard_map(
        on_device, mesh=mesh, in_specs=in_specs, out_specs=out_specs, check_vma=False
    )
```

```python
import functools
import math

import jax
import jax.numpy as jnp
from jax import lax
from jax.experimental import pallas as pl
from jax.experimental.pallas import tpu as pltpu
from jax.sharding import PartitionSpec as P

F32 = jnp.float32
BF16 = jnp.bfloat16
GRANT = 12 << 20
WHOLE = pl.BlockSpec(memory_space=pltpu.VMEM)


def grid_of(chips):
    ny = max(d for d in range(1, math.isqrt(chips) + 1) if chips % d == 0)
    return ny, chips // ny


def dot(a, b):
    return jnp.dot(a, b, preferred_element_type=F32)


def columns_of(x_ref, at_ref, index, deep):
    return x_ref[:, pl.ds(pl.multiple_of(at_ref[index], deep), deep)]


def tiles_of(out_ref):
    tile = math.gcd(out_ref.shape[1], 256)
    return [slice(at, at + tile) for at in range(0, out_ref.shape[1], tile)]


def blocks_of(xs, out_ref):
    tile = math.gcd(out_ref.shape[1], 256)
    size = xs[0].shape[0]
    for at in range(0, out_ref.shape[1], tile):
        for index, x_ref in enumerate(xs):
            yield x_ref, slice(index * size, (index + 1) * size), slice(at, at + tile)


def query_kernel(parts, at_ref, *refs):
    xs, pairs, out_ref = refs[:parts], refs[parts:-1], refs[-1]
    deep = pairs[0].shape[1]
    for x_ref, rows, tile in blocks_of(xs, out_ref):
        query = None
        for index in range(2 * len(pairs)):
            x = columns_of(x_ref, at_ref, index, deep)
            new = dot(x, pairs[index // 2][index % 2, :, tile])
            query = new if query is None else query + new
        out_ref[rows, tile] = query


def gate_kernel(parts, at_ref, *refs):
    xs, refs = refs[:parts], refs[parts:]
    filtered_ref, partial_ref, pieces, out_ref = refs[0], refs[1], refs[2:-1], refs[-1]
    deep = pieces[0].shape[0]
    for x_ref, rows, tile in blocks_of(xs, out_ref):
        query = partial_ref[rows, tile]
        for index, piece in enumerate(pieces):
            query = query + dot(columns_of(x_ref, at_ref, index, deep), piece[:, tile])
        gated = query.astype(BF16).astype(F32) * filtered_ref[rows, tile]
        out_ref[rows, tile] = gated.astype(BF16)


def call(kernel, scalars, operands, out, scratch=()):
    return pl.pallas_call(
        kernel,
        out_shape=out,
        in_specs=[pl.BlockSpec(memory_space=pltpu.SMEM)] + [WHOLE] * len(operands),
        out_specs=jax.tree.map(lambda _: WHOLE, out),
        scratch_shapes=scratch,
        compiler_params=pltpu.CompilerParams(vmem_limit_bytes=GRANT),
        cost_estimate=pl.CostEstimate(flops=1, bytes_accessed=1, transcendentals=0),
    )(scalars, *operands)


def project(kernel, at, xs, extra, pieces, out_dtype):
    rows = sum(x.shape[0] for x in xs)
    out = jax.ShapeDtypeStruct((rows, pieces[0].shape[-1]), out_dtype)
    return call(functools.partial(kernel, len(xs)), at, (*xs, *extra, *pieces), out)


def product_kernel(parts, count, at_ref, *refs):
    xs, refs = refs[:parts], refs[parts:]
    given, refs = refs[:count], refs[count:]
    outs, (joined, *pieces, sems) = refs[:parts], refs[parts:]
    ends = [0]
    for x_ref in xs:
        ends.append(ends[-1] + x_ref.shape[0])
    targets = [joined.at[low:high] for low, high in zip(ends, ends[1:])] + list(pieces)
    copies = [
        pltpu.make_async_copy(source, target, sems.at[index])
        for index, (source, target) in enumerate(zip((*xs, *given), targets))
    ]
    for copy in copies:
        copy.start()
    for copy in copies[:parts]:
        copy.wait()
    deep = pieces[0].shape[1]
    half = pieces[0].shape[2]
    tile = math.gcd(half, 256)
    for low in range(0, half, tile):
        columns = slice(low, low + tile)
        key = value = None
        for index, piece in enumerate(pieces):
            if low == 0:
                copies[parts + index].wait()
            x = columns_of(joined, at_ref, index, deep)
            new_key, new_value = dot(x, piece[0, :, columns]), dot(x, piece[1, :, columns])
            key = new_key if key is None else key + new_key
            value = new_value if value is None else value + new_value
        product = key.astype(BF16).astype(F32) * value.astype(BF16).astype(F32)
        for out, start, end in zip(outs, ends, ends[1:]):
            out[:, columns] = product[start:end]


def products(at, xs, pieces):
    half = pieces[0].shape[2]
    held = [pltpu.VMEM((sum(x.shape[0] for x in xs), xs[0].shape[1]), BF16)]
    held += [pltpu.VMEM(piece.shape, BF16) for piece in pieces]
    held.append(pltpu.SemaphoreType.DMA((len(xs) + len(pieces),)))
    return pl.pallas_call(
        functools.partial(product_kernel, len(xs), len(pieces)),
        out_shape=[jax.ShapeDtypeStruct((x.shape[0], half), F32) for x in xs],
        in_specs=[pl.BlockSpec(memory_space=pltpu.SMEM)]
        + [pl.BlockSpec(memory_space=pl.ANY)] * (len(xs) + len(pieces)),
        out_specs=[WHOLE] * len(xs),
        scratch_shapes=held,
        compiler_params=pltpu.CompilerParams(vmem_limit_bytes=56 << 20),
        cost_estimate=pl.CostEstimate(flops=1, bytes_accessed=1, transcendentals=0),
    )(at, *xs, *pieces)


def filter_kernel(_, product_ref, halo_ref, taps_ref, out_ref, held):
    length, pad = product_ref.shape[0], halo_ref.shape[0]
    held[:pad] = halo_ref[...]
    held[pad:] = product_ref[...]
    for tile in tiles_of(out_ref):
        total = None
        for offset in range(taps_ref.shape[0]):
            term = taps_ref[offset : offset + 1, tile] * held[pad - offset : pad - offset + length, tile]
            total = term if total is None else total + term
        out_ref[:, tile] = total


def causal_filter(at, product, halo, taps):
    length, half = product.shape
    out = jax.ShapeDtypeStruct(product.shape, F32)
    scratch = [pltpu.VMEM((halo.shape[0] + length, half), F32)]
    return call(filter_kernel, at, (product, halo, taps), out, scratch)


def terms_kernel(plan, turned, n_tp, at_ref, *refs):
    gates, refs, held = refs[:4], refs[4:-1], refs[-1]
    count = sum(len(parts) for parts in plan)
    weights, outs = refs[:count], refs[count:]
    half = gates[0].shape[1]
    rows = gates[0].shape[0] // n_tp
    for slot in range(n_tp):
        for index, gate in enumerate(gates):
            side, whose = index % 2, index // 2
            place = slice((2 * slot + whose) * rows, (2 * slot + whose + 1) * rows)
            owner = lax.rem(at_ref[1] + slot, n_tp) * rows if turned else slot * rows
            column = (at_ref[0] if side == 0 else 1 - at_ref[0]) * half
            taken = gate[pl.ds(pl.multiple_of(owner, rows), rows)]
            held[place, pl.ds(pl.multiple_of(column, half), half)] = taken
    wide = weights[0].shape[1]
    share = held.shape[0] // len(outs)
    used = 0
    for index, parts in enumerate(plan):
        at = slice(index * wide, (index + 1) * wide)
        for piece in range(0, held.shape[0], share):
            total, depth = None, 0
            for which in range(len(parts)):
                weight = weights[used + which]
                low, depth = depth, depth + weight.shape[0]
                new = dot(held[piece : piece + share, low:depth], weight[...])
                total = new if total is None else total + new
            outs[piece // share][:, at] = total.astype(BF16)
        used += len(parts)


def terms(n_tp, place, gates, blocks, turned):
    length, half = gates[0].shape
    weights = [part for parts in blocks for part in parts]
    cols = len(blocks) * weights[0].shape[1]
    slots = n_tp if turned else 1
    out = [jax.ShapeDtypeStruct((2 * length // slots, cols), BF16)] * slots
    kernel = functools.partial(terms_kernel, blocks_plan(blocks), turned, n_tp)
    scratch = [pltpu.VMEM((2 * length, 2 * half), BF16)]
    result = call(kernel, place, (*gates, *weights), out, scratch)
    return result if turned else result[0]


def blocks_plan(blocks):
    return [range(len(parts)) for parts in blocks]


def on_device(tokens, norm_gain, in_weight, filters, out_weight, keep_mask):
    n_seq, n_tp = lax.axis_size("seq"), lax.axis_size("tp")
    chips = n_seq // 2
    ny, nx = grid_of(chips)
    seq = lax.axis_index("seq")
    core, here = seq % 2, seq // 2
    my_y, my_x = here // nx, here % nx
    rows, model = tokens.shape
    length = rows * n_tp
    deep, channels = in_weight.shape[1:]
    half = channels // 2
    wide = out_weight.shape[1]

    def place(y, x, c):
        return ((y % ny) * nx + x % nx) * 2 + c

    def from_chip(block, dy, dx):
        route = [
            (place(y + dy, x + dx, c), place(y, x, c))
            for y in range(ny)
            for x in range(nx)
            for c in range(2)
        ]
        return lax.ppermute(block, "seq", route)

    def from_partner(block):
        return lax.ppermute(block, "seq", [(s, s ^ 1) for s in range(n_seq)])

    def direct(mine, brought):
        along_x = [(mine, brought)]
        along_y = [(mine, brought)]
        along_x += [tuple(from_chip(b, 0, dx) for b in (mine, brought)) for dx in range(1, nx)]
        along_y += [tuple(from_chip(b, dy, 0) for b in (mine, brought)) for dy in range(1, ny)]
        return along_x, along_y

    def onward(along_x, along_y):
        return {
            (dy, dx): (from_chip(along_x[dx][0], dy, 0), from_chip(along_y[dy][1], 0, dx))
            for dy in range(1, ny)
            for dx in range(1, nx)
        }

    def crossed(along_x, along_y):
        return {
            (dy, dx): (from_chip(along_x[0, dx][0], dy, 0), from_chip(along_y[dy, 0][1], 0, dx))
            for dy, _ in along_y
            for _, dx in along_x
        }

    def listed(along_x, along_y, rest):
        found = {(0, dx): pair for dx, pair in enumerate(along_x)}
        found.update({(dy, 0): pair for dy, pair in enumerate(along_y)})
        found.update(rest)
        return found

    def by_core(mine, other, axis):
        return jnp.where(
            core == 0,
            jnp.concatenate([mine, other], axis=axis),
            jnp.concatenate([other, mine], axis=axis),
        )

    def columns(array, first, count, at):
        return lax.dynamic_slice(array, (first, 0, at * half), (count, deep, half))

    mine_kv = columns(in_weight, 1, 2, core)
    away_kv = columns(in_weight, 1, 2, 1 - core)
    brought_kv = from_partner(away_kv)
    kv_x, kv_y = direct(mine_kv, brought_kv)

    tokens_then, _ = lax.optimization_barrier((tokens, away_kv))
    widened = tokens_then.astype(F32)
    mean_sq = jnp.mean(widened * widened, axis=1, keepdims=True)
    normed = (widened * lax.rsqrt(mean_sq + 1e-06) * norm_gain).astype(BF16)
    own_rows = lax.all_gather(normed, "tp", axis=0, tiled=True)
    in_weight_then, _ = lax.optimization_barrier((in_weight, normed))
    mine_q = columns(in_weight_then, 0, 1, core)[0]
    both_q = jnp.stack([mine_q, from_partner(columns(in_weight_then, 0, 1, 1 - core)[0])])

    kv_x, kv_y, both_q = lax.optimization_barrier((kv_x, kv_y, both_q))
    kv_rest = onward(kv_x, kv_y)
    q_x = {(0, dx): from_chip(both_q, 0, dx) for dx in range(1, nx)}
    q_y = {(dy, 0): from_chip(both_q, dy, 0) for dy in range(1, ny)}
    arrived = (kv_x, kv_y, kv_rest)
    own_rows, arrived = lax.optimization_barrier((own_rows, arrived))
    kv_x, kv_y, kv_rest = arrived
    kv = listed(kv_x, kv_y, kv_rest)
    order = list(kv)
    kv_pieces = [piece for key in order for piece in kv[key]]
    at = jnp.stack(
        [place(my_y + dy, my_x + dx, core ^ rc) * deep for dy, dx in order for rc in range(2)]
    ).astype(jnp.int32)
    early = 2 * (ny + nx - 1)

    (own_product,) = products(at, [own_rows], kv_pieces)
    reach = filters.shape[0] - 1
    pad = -(-reach // 16) * 16
    ends = [
        lax.ppermute(own_rows[length - pad :], "seq", [(2 * i + 1, 2 * i + 2 + c) for i in range(chips - 1)])
        for c in range(2)
    ]
    before = jnp.where(core == 0, ends[0], ends[1])
    ready = (own_rows, q_x, q_y, own_product, before)
    rows_then, q_x, q_y, own_product, before = lax.optimization_barrier(ready)
    other_rows = from_partner(rows_then)
    q_rest = crossed(q_x, q_y)
    q_pairs = {(0, 0): both_q, **q_x, **q_y}
    q_early = [q_pairs[key] for key in order if key in q_pairs]
    own_query = project(query_kernel, at, [own_rows], [], q_early, F32)
    other_rows, own_query = lax.optimization_barrier((other_rows, own_query))
    rim, other_product = products(at, [before, other_rows], kv_pieces)
    own_tail, other_tail = own_product[length - pad :], other_product[length - pad :]
    first_tail = jnp.where(core == 0, own_tail, other_tail)
    groups = filters.shape[1] // 2
    taps = jnp.repeat(
        lax.dynamic_slice_in_dim(filters, core * groups, groups, axis=1), half // groups, axis=1
    )
    own_filtered = causal_filter(at, own_product, jnp.where(core == 0, rim, first_tail), taps)
    other_filtered = causal_filter(at, other_product, jnp.where(core == 0, first_tail, rim), taps)

    other_rows, own_filtered, other_filtered = lax.optimization_barrier(
        (other_rows, own_filtered, other_filtered)
    )
    other_query = project(query_kernel, at, [other_rows], [], q_early, F32)
    weight_then, q_x, q_y = lax.optimization_barrier((out_weight, q_x, q_y))
    o_x = {(0, dx): from_chip(weight_then, 0, dx) for dx in range(1, nx)}
    o_y = {(dy, 0): from_chip(weight_then, dy, 0) for dy in range(1, ny)}
    o_rest = {
        (dy, dx): (
            from_chip(o_x[0, dx][:half], dy, 0),
            from_chip(o_y[dy, 0][half:], 0, dx),
        )
        for dy in range(1, ny)
        for dx in range(1, nx)
    }
    late = [piece for pair in q_rest.values() for piece in pair]
    other_gated = project(
        gate_kernel, at[early:], [other_rows], [other_filtered, other_query], late, BF16
    )
    own_gated = project(
        gate_kernel, at[early:], [own_rows], [own_filtered, own_query], late, BF16
    )
    gates = (own_gated, from_partner(other_gated), other_gated, from_partner(own_gated))

    position = lax.axis_index("tp")
    here_at = jnp.stack([core, position]).astype(jnp.int32)
    up = [(i, i + 1) for i in range(n_tp - 1)]
    down = [(i + 1, i) for i in range(n_tp - 1)]

    def plus(a, b):
        return (a.astype(F32) + b.astype(F32)).astype(BF16)

    def chained(slots):
        rising = falling = None
        for step in range(n_tp - 1):
            send_up, send_down = slots[n_tp - 1 - step], slots[step + 1]
            if step:
                send_up, send_down = plus(send_up, rising), plus(send_down, falling)
            rising = lax.ppermute(send_up, "tp", up)
            falling = lax.ppermute(send_down, "tp", down)
        total = slots[0].astype(F32) + rising.astype(F32) + falling.astype(F32)
        return total

    near = {(0, 0): (out_weight,)}
    near.update({key: (block,) for key, block in (*o_x.items(), *o_y.items())})
    found = terms(n_tp, here_at, gates, list(near.values()), False)
    gates, found = lax.optimization_barrier((gates, found))
    near_sum = lax.psum_scatter(found, "tp", scatter_dimension=0, tiled=True)
    far_sum = chained(terms(n_tp, here_at, gates, list(o_rest.values()), True))
    result = jnp.zeros((rows, model), BF16)
    for keys, mixed in ((list(near), near_sum), (list(o_rest), far_sum)):
        theirs = from_partner(mixed[rows:].astype(BF16)).astype(F32)
        mine = mixed[:rows].astype(F32)
        for index, (dy, dx) in enumerate(keys):
            start = place(my_y + dy, my_x + dx, 0) * wide
            here_columns = slice(index * wide, (index + 1) * wide)
            pair = by_core(mine[:, here_columns], theirs[:, here_columns], 1)
            kept = lax.dynamic_slice_in_dim(keep_mask, start, 2 * wide, axis=1).astype(F32)
            base = lax.dynamic_slice_in_dim(tokens, start, 2 * wide, axis=1).astype(F32)
            part = (base + kept * pair * (1.0 / 0.9)).astype(BF16)
            result = lax.dynamic_update_slice_in_dim(result, part, start, axis=1)
    return result


def solution(mesh):
    in_specs = (
        P(("seq", "tp"), None),
        P(),
        P(None, "seq", "tp"),
        P(None, "tp"),
        P("tp", "seq"),
        P(("seq", "tp"), None),
    )
    out_specs = P(("seq", "tp"), None)
    return jax.shard_map(
        on_device, mesh=mesh, in_specs=in_specs, out_specs=out_specs, check_vma=False
    )
```

```python
import functools
import math

import jax
import jax.numpy as jnp
from jax import lax
from jax.experimental import pallas as pl
from jax.experimental.pallas import tpu as pltpu
from jax.sharding import PartitionSpec as P

F32 = jnp.float32
BF16 = jnp.bfloat16
GRANT = 12 << 20
WHOLE = pl.BlockSpec(memory_space=pltpu.VMEM)


def grid_of(chips):
    ny = max(d for d in range(1, math.isqrt(chips) + 1) if chips % d == 0)
    return ny, chips // ny


def dot(a, b):
    return jnp.dot(a, b, preferred_element_type=F32)


def columns_of(x_ref, at_ref, index, deep):
    return x_ref[:, pl.ds(pl.multiple_of(at_ref[index], deep), deep)]


def tiles_of(out_ref):
    tile = math.gcd(out_ref.shape[1], 256)
    return [slice(at, at + tile) for at in range(0, out_ref.shape[1], tile)]


def blocks_of(xs, out_ref):
    tile = math.gcd(out_ref.shape[1], 256)
    size = xs[0].shape[0]
    for at in range(0, out_ref.shape[1], tile):
        for index, x_ref in enumerate(xs):
            yield x_ref, slice(index * size, (index + 1) * size), slice(at, at + tile)


def query_kernel(parts, at_ref, *refs):
    xs, pairs, out_ref = refs[:parts], refs[parts:-1], refs[-1]
    deep = pairs[0].shape[1]
    for x_ref, rows, tile in blocks_of(xs, out_ref):
        query = None
        for index in range(2 * len(pairs)):
            x = columns_of(x_ref, at_ref, index, deep)
            new = dot(x, pairs[index // 2][index % 2, :, tile])
            query = new if query is None else query + new
        out_ref[rows, tile] = query


def gate_kernel(parts, at_ref, *refs):
    xs, refs = refs[:parts], refs[parts:]
    filtered_ref, partial_ref, pieces, out_ref = refs[0], refs[1], refs[2:-1], refs[-1]
    deep = pieces[0].shape[0]
    for x_ref, rows, tile in blocks_of(xs, out_ref):
        query = partial_ref[rows, tile]
        for index, piece in enumerate(pieces):
            query = query + dot(columns_of(x_ref, at_ref, index, deep), piece[:, tile])
        gated = query.astype(BF16).astype(F32) * filtered_ref[rows, tile]
        out_ref[rows, tile] = gated.astype(BF16)


def call(kernel, scalars, operands, out, scratch=()):
    return pl.pallas_call(
        kernel,
        out_shape=out,
        in_specs=[pl.BlockSpec(memory_space=pltpu.SMEM)] + [WHOLE] * len(operands),
        out_specs=jax.tree.map(lambda _: WHOLE, out),
        scratch_shapes=scratch,
        compiler_params=pltpu.CompilerParams(vmem_limit_bytes=GRANT),
        cost_estimate=pl.CostEstimate(flops=1, bytes_accessed=1, transcendentals=0),
    )(scalars, *operands)


def project(kernel, at, xs, extra, pieces, out_dtype):
    rows = sum(x.shape[0] for x in xs)
    out = jax.ShapeDtypeStruct((rows, pieces[0].shape[-1]), out_dtype)
    return call(functools.partial(kernel, len(xs)), at, (*xs, *extra, *pieces), out)


def product_kernel(parts, count, at_ref, *refs):
    xs, refs = refs[:parts], refs[parts:]
    given, refs = refs[:count], refs[count:]
    outs, (joined, *pieces, sems) = refs[:parts], refs[parts:]
    ends = [0]
    for x_ref in xs:
        ends.append(ends[-1] + x_ref.shape[0])
    targets = [joined.at[low:high] for low, high in zip(ends, ends[1:])] + list(pieces)
    copies = [
        pltpu.make_async_copy(source, target, sems.at[index])
        for index, (source, target) in enumerate(zip((*xs, *given), targets))
    ]
    for copy in copies:
        copy.start()
    for copy in copies[:parts]:
        copy.wait()
    deep = pieces[0].shape[1]
    half = pieces[0].shape[2]
    tile = math.gcd(half, 256)
    for low in range(0, half, tile):
        columns = slice(low, low + tile)
        key = value = None
        for index, piece in enumerate(pieces):
            if low == 0:
                copies[parts + index].wait()
            x = columns_of(joined, at_ref, index, deep)
            new_key, new_value = dot(x, piece[0, :, columns]), dot(x, piece[1, :, columns])
            key = new_key if key is None else key + new_key
            value = new_value if value is None else value + new_value
        product = key.astype(BF16).astype(F32) * value.astype(BF16).astype(F32)
        for out, start, end in zip(outs, ends, ends[1:]):
            out[:, columns] = product[start:end]


def products(at, xs, pieces):
    half = pieces[0].shape[2]
    held = [pltpu.VMEM((sum(x.shape[0] for x in xs), xs[0].shape[1]), BF16)]
    held += [pltpu.VMEM(piece.shape, BF16) for piece in pieces]
    held.append(pltpu.SemaphoreType.DMA((len(xs) + len(pieces),)))
    return pl.pallas_call(
        functools.partial(product_kernel, len(xs), len(pieces)),
        out_shape=[jax.ShapeDtypeStruct((x.shape[0], half), F32) for x in xs],
        in_specs=[pl.BlockSpec(memory_space=pltpu.SMEM)]
        + [pl.BlockSpec(memory_space=pl.ANY)] * (len(xs) + len(pieces)),
        out_specs=[WHOLE] * len(xs),
        scratch_shapes=held,
        compiler_params=pltpu.CompilerParams(vmem_limit_bytes=56 << 20),
        cost_estimate=pl.CostEstimate(flops=1, bytes_accessed=1, transcendentals=0),
    )(at, *xs, *pieces)


def filter_kernel(_, product_ref, halo_ref, taps_ref, out_ref, held):
    length, pad = product_ref.shape[0], halo_ref.shape[0]
    held[:pad] = halo_ref[...]
    held[pad:] = product_ref[...]
    for tile in tiles_of(out_ref):
        total = None
        for offset in range(taps_ref.shape[0]):
            term = taps_ref[offset : offset + 1, tile] * held[pad - offset : pad - offset + length, tile]
            total = term if total is None else total + term
        out_ref[:, tile] = total


def causal_filter(at, product, halo, taps):
    length, half = product.shape
    out = jax.ShapeDtypeStruct(product.shape, F32)
    scratch = [pltpu.VMEM((halo.shape[0] + length, half), F32)]
    return call(filter_kernel, at, (product, halo, taps), out, scratch)


def terms_kernel(plan, turned, n_tp, at_ref, *refs):
    gates, refs, held = refs[:4], refs[4:-1], refs[-1]
    count = sum(len(parts) for parts in plan)
    weights, outs = refs[:count], refs[count:]
    half = gates[0].shape[1]
    rows = gates[0].shape[0] // n_tp
    for slot in range(n_tp):
        for index, gate in enumerate(gates):
            side, whose = index % 2, index // 2
            place = slice((2 * slot + whose) * rows, (2 * slot + whose + 1) * rows)
            owner = lax.rem(at_ref[1] + slot, n_tp) * rows if turned else slot * rows
            column = (at_ref[0] if side == 0 else 1 - at_ref[0]) * half
            taken = gate[pl.ds(pl.multiple_of(owner, rows), rows)]
            held[place, pl.ds(pl.multiple_of(column, half), half)] = taken
    wide = weights[0].shape[1]
    share = held.shape[0] // len(outs)
    used = 0
    for index, parts in enumerate(plan):
        at = slice(index * wide, (index + 1) * wide)
        for piece in range(0, held.shape[0], share):
            total, depth = None, 0
            for which in range(len(parts)):
                weight = weights[used + which]
                low, depth = depth, depth + weight.shape[0]
                new = dot(held[piece : piece + share, low:depth], weight[...])
                total = new if total is None else total + new
            outs[piece // share][:, at] = total.astype(BF16)
        used += len(parts)


def terms(n_tp, place, gates, blocks, turned):
    length, half = gates[0].shape
    weights = [part for parts in blocks for part in parts]
    cols = len(blocks) * weights[0].shape[1]
    slots = n_tp if turned else 1
    out = [jax.ShapeDtypeStruct((2 * length // slots, cols), BF16)] * slots
    kernel = functools.partial(terms_kernel, blocks_plan(blocks), turned, n_tp)
    scratch = [pltpu.VMEM((2 * length, 2 * half), BF16)]
    result = call(kernel, place, (*gates, *weights), out, scratch)
    return result if turned else result[0]


def blocks_plan(blocks):
    return [range(len(parts)) for parts in blocks]


def near_kernel(n_tp, at_ref, *refs):
    gates, refs = refs[:4], refs[4:]
    count = (len(refs) - 4) // 2
    given, (out_ref, held, *refs) = refs[:count], refs[count:]
    weights, (ready, sems, out_sems) = refs[:count], refs[count:]
    copies = [
        pltpu.make_async_copy(source, target, sems.at[index])
        for index, (source, target) in enumerate(zip(given, weights))
    ]
    for copy in copies:
        copy.start()
    half = gates[0].shape[1]
    rows = gates[0].shape[0] // n_tp
    for slot in range(n_tp):
        for index, gate in enumerate(gates):
            side, whose = index % 2, index // 2
            place = slice((2 * slot + whose) * rows, (2 * slot + whose + 1) * rows)
            column = (at_ref[0] if side == 0 else 1 - at_ref[0]) * half
            columns = pl.ds(pl.multiple_of(column, half), half)
            held[place, columns] = gate[slot * rows : (slot + 1) * rows]
    wide = weights[0].shape[1]
    leaving = []
    for index, weight in enumerate(weights):
        copies[index].wait()
        at = slice(index * wide, (index + 1) * wide)
        ready[:, at] = dot(held[...], weight[...]).astype(BF16)
        leaving.append(pltpu.make_async_copy(ready.at[:, at], out_ref.at[:, at], out_sems.at[index]))
        leaving[-1].start()
    for copy in leaving:
        copy.wait()


def near_terms(n_tp, place, gates, weights):
    length, half = gates[0].shape
    shape = (2 * length, len(weights) * weights[0].shape[1])
    anywhere = pl.BlockSpec(memory_space=pl.ANY)
    return pl.pallas_call(
        functools.partial(near_kernel, n_tp),
        out_shape=jax.ShapeDtypeStruct(shape, BF16),
        in_specs=[pl.BlockSpec(memory_space=pltpu.SMEM)]
        + [WHOLE] * 4
        + [anywhere] * len(weights),
        out_specs=anywhere,
        scratch_shapes=[pltpu.VMEM((2 * length, 2 * half), BF16)]
        + [pltpu.VMEM(weight.shape, BF16) for weight in weights]
        + [pltpu.VMEM(shape, BF16)]
        + [pltpu.SemaphoreType.DMA((len(weights),))] * 2,
        compiler_params=pltpu.CompilerParams(vmem_limit_bytes=24 << 20),
        cost_estimate=pl.CostEstimate(flops=1, bytes_accessed=1, transcendentals=0),
    )(place, *gates, *weights)


def on_device(tokens, norm_gain, in_weight, filters, out_weight, keep_mask):
    n_seq, n_tp = lax.axis_size("seq"), lax.axis_size("tp")
    chips = n_seq // 2
    ny, nx = grid_of(chips)
    seq = lax.axis_index("seq")
    core, here = seq % 2, seq // 2
    my_y, my_x = here // nx, here % nx
    rows, model = tokens.shape
    length = rows * n_tp
    deep, channels = in_weight.shape[1:]
    half = channels // 2
    wide = out_weight.shape[1]

    def place(y, x, c):
        return ((y % ny) * nx + x % nx) * 2 + c

    def from_chip(block, dy, dx):
        route = [
            (place(y + dy, x + dx, c), place(y, x, c))
            for y in range(ny)
            for x in range(nx)
            for c in range(2)
        ]
        return lax.ppermute(block, "seq", route)

    def from_partner(block):
        return lax.ppermute(block, "seq", [(s, s ^ 1) for s in range(n_seq)])

    def direct(mine, brought):
        along_x = [(mine, brought)]
        along_y = [(mine, brought)]
        along_x += [tuple(from_chip(b, 0, dx) for b in (mine, brought)) for dx in range(1, nx)]
        along_y += [tuple(from_chip(b, dy, 0) for b in (mine, brought)) for dy in range(1, ny)]
        return along_x, along_y

    def onward(along_x, along_y):
        return {
            (dy, dx): (from_chip(along_x[dx][0], dy, 0), from_chip(along_y[dy][1], 0, dx))
            for dy in range(1, ny)
            for dx in range(1, nx)
        }

    def crossed(along_x, along_y):
        return {
            (dy, dx): (from_chip(along_x[0, dx][0], dy, 0), from_chip(along_y[dy, 0][1], 0, dx))
            for dy, _ in along_y
            for _, dx in along_x
        }

    def listed(along_x, along_y, rest):
        found = {(0, dx): pair for dx, pair in enumerate(along_x)}
        found.update({(dy, 0): pair for dy, pair in enumerate(along_y)})
        found.update(rest)
        return found

    def by_core(mine, other, axis):
        return jnp.where(
            core == 0,
            jnp.concatenate([mine, other], axis=axis),
            jnp.concatenate([other, mine], axis=axis),
        )

    def columns(array, first, count, at):
        return lax.dynamic_slice(array, (first, 0, at * half), (count, deep, half))

    mine_kv = columns(in_weight, 1, 2, core)
    away_kv = columns(in_weight, 1, 2, 1 - core)
    brought_kv = from_partner(away_kv)
    kv_x, kv_y = direct(mine_kv, brought_kv)

    tokens_then, _ = lax.optimization_barrier((tokens, away_kv))
    widened = tokens_then.astype(F32)
    mean_sq = jnp.mean(widened * widened, axis=1, keepdims=True)
    normed = (widened * lax.rsqrt(mean_sq + 1e-06) * norm_gain).astype(BF16)
    own_rows = lax.all_gather(normed, "tp", axis=0, tiled=True)
    in_weight_then, _ = lax.optimization_barrier((in_weight, normed))
    mine_q = columns(in_weight_then, 0, 1, core)[0]
    both_q = jnp.stack([mine_q, from_partner(columns(in_weight_then, 0, 1, 1 - core)[0])])

    kv_x, kv_y, both_q = lax.optimization_barrier((kv_x, kv_y, both_q))
    kv_rest = onward(kv_x, kv_y)
    q_x = {(0, dx): from_chip(both_q, 0, dx) for dx in range(1, nx)}
    q_y = {(dy, 0): from_chip(both_q, dy, 0) for dy in range(1, ny)}
    arrived = (kv_x, kv_y, kv_rest)
    own_rows, arrived = lax.optimization_barrier((own_rows, arrived))
    kv_x, kv_y, kv_rest = arrived
    kv = listed(kv_x, kv_y, kv_rest)
    order = list(kv)
    kv_pieces = [piece for key in order for piece in kv[key]]
    at = jnp.stack(
        [place(my_y + dy, my_x + dx, core ^ rc) * deep for dy, dx in order for rc in range(2)]
    ).astype(jnp.int32)
    early = 2 * (ny + nx - 1)

    (own_product,) = products(at, [own_rows], kv_pieces)
    reach = filters.shape[0] - 1
    pad = -(-reach // 16) * 16
    ends = [
        lax.ppermute(own_rows[length - pad :], "seq", [(2 * i + 1, 2 * i + 2 + c) for i in range(chips - 1)])
        for c in range(2)
    ]
    before = jnp.where(core == 0, ends[0], ends[1])
    ready = (own_rows, q_x, q_y, own_product, before)
    rows_then, q_x, q_y, own_product, before = lax.optimization_barrier(ready)
    other_rows = from_partner(rows_then)
    q_rest = crossed(q_x, q_y)
    q_pairs = {(0, 0): both_q, **q_x, **q_y}
    q_early = [q_pairs[key] for key in order if key in q_pairs]
    own_query = project(query_kernel, at, [own_rows], [], q_early, F32)
    other_rows, own_query = lax.optimization_barrier((other_rows, own_query))
    rim, other_product = products(at, [before, other_rows], kv_pieces)
    own_tail, other_tail = own_product[length - pad :], other_product[length - pad :]
    first_tail = jnp.where(core == 0, own_tail, other_tail)
    groups = filters.shape[1] // 2
    taps = jnp.repeat(
        lax.dynamic_slice_in_dim(filters, core * groups, groups, axis=1), half // groups, axis=1
    )
    own_filtered = causal_filter(at, own_product, jnp.where(core == 0, rim, first_tail), taps)
    other_filtered = causal_filter(at, other_product, jnp.where(core == 0, first_tail, rim), taps)

    other_rows, own_filtered, other_filtered = lax.optimization_barrier(
        (other_rows, own_filtered, other_filtered)
    )
    other_query = project(query_kernel, at, [other_rows], [], q_early, F32)
    weight_then, q_x, q_y = lax.optimization_barrier((out_weight, q_x, q_y))
    o_x = {(0, dx): from_chip(weight_then, 0, dx) for dx in range(1, nx)}
    o_y = {(dy, 0): from_chip(weight_then, dy, 0) for dy in range(1, ny)}
    o_rest = {
        (dy, dx): (
            from_chip(o_x[0, dx][:half], dy, 0),
            from_chip(o_y[dy, 0][half:], 0, dx),
        )
        for dy in range(1, ny)
        for dx in range(1, nx)
    }
    late = [piece for pair in q_rest.values() for piece in pair]
    other_gated = project(
        gate_kernel, at[early:], [other_rows], [other_filtered, other_query], late, BF16
    )
    own_gated = project(
        gate_kernel, at[early:], [own_rows], [own_filtered, own_query], late, BF16
    )
    gates = (own_gated, from_partner(other_gated), other_gated, from_partner(own_gated))

    position = lax.axis_index("tp")
    here_at = jnp.stack([core, position]).astype(jnp.int32)
    up = [(i, i + 1) for i in range(n_tp - 1)]
    down = [(i + 1, i) for i in range(n_tp - 1)]

    def plus(a, b):
        return (a.astype(F32) + b.astype(F32)).astype(BF16)

    def chained(slots):
        rising = falling = None
        for step in range(n_tp - 1):
            send_up, send_down = slots[n_tp - 1 - step], slots[step + 1]
            if step:
                send_up, send_down = plus(send_up, rising), plus(send_down, falling)
            rising = lax.ppermute(send_up, "tp", up)
            falling = lax.ppermute(send_down, "tp", down)
        total = slots[0].astype(F32) + rising.astype(F32) + falling.astype(F32)
        return total

    near = {(0, 0): (out_weight,)}
    near.update({key: (block,) for key, block in (*o_x.items(), *o_y.items())})
    found = near_terms(n_tp, here_at, gates, [block for (block,) in near.values()])
    gates, found = lax.optimization_barrier((gates, found))
    near_sum = lax.psum_scatter(found, "tp", scatter_dimension=0, tiled=True)
    far_sum = chained(terms(n_tp, here_at, gates, list(o_rest.values()), True))
    result = jnp.zeros((rows, model), BF16)
    for keys, mixed in ((list(near), near_sum), (list(o_rest), far_sum)):
        theirs = from_partner(mixed[rows:].astype(BF16)).astype(F32)
        mine = mixed[:rows].astype(F32)
        for index, (dy, dx) in enumerate(keys):
            start = place(my_y + dy, my_x + dx, 0) * wide
            here_columns = slice(index * wide, (index + 1) * wide)
            pair = by_core(mine[:, here_columns], theirs[:, here_columns], 1)
            kept = lax.dynamic_slice_in_dim(keep_mask, start, 2 * wide, axis=1).astype(F32)
            base = lax.dynamic_slice_in_dim(tokens, start, 2 * wide, axis=1).astype(F32)
            part = (base + kept * pair * (1.0 / 0.9)).astype(BF16)
            result = lax.dynamic_update_slice_in_dim(result, part, start, axis=1)
    return result


def solution(mesh):
    in_specs = (
        P(("seq", "tp"), None),
        P(),
        P(None, "seq", "tp"),
        P(None, "tp"),
        P("tp", "seq"),
        P(("seq", "tp"), None),
    )
    out_specs = P(("seq", "tp"), None)
    return jax.shard_map(
        on_device, mesh=mesh, in_specs=in_specs, out_specs=out_specs, check_vma=False
    )
```

```python
import functools
import math

import jax
import jax.numpy as jnp
from jax import lax
from jax.experimental import pallas as pl
from jax.experimental.pallas import tpu as pltpu
from jax.sharding import PartitionSpec as P

F32 = jnp.float32
BF16 = jnp.bfloat16
GRANT = 12 << 20
WHOLE = pl.BlockSpec(memory_space=pltpu.VMEM)


def grid_of(chips):
    ny = max(d for d in range(1, math.isqrt(chips) + 1) if chips % d == 0)
    return ny, chips // ny


def dot(a, b):
    return jnp.dot(a, b, preferred_element_type=F32)


def columns_of(x_ref, at_ref, index, deep):
    return x_ref[:, pl.ds(pl.multiple_of(at_ref[index], deep), deep)]


def tiles_of(out_ref):
    tile = math.gcd(out_ref.shape[1], 256)
    return [slice(at, at + tile) for at in range(0, out_ref.shape[1], tile)]


def blocks_of(xs, out_ref):
    tile = math.gcd(out_ref.shape[1], 256)
    size = xs[0].shape[0]
    for at in range(0, out_ref.shape[1], tile):
        for index, x_ref in enumerate(xs):
            yield x_ref, slice(index * size, (index + 1) * size), slice(at, at + tile)


def query_kernel(parts, at_ref, *refs):
    xs, pairs, out_ref = refs[:parts], refs[parts:-1], refs[-1]
    deep = pairs[0].shape[1]
    for x_ref, rows, tile in blocks_of(xs, out_ref):
        query = None
        for index in range(2 * len(pairs)):
            x = columns_of(x_ref, at_ref, index, deep)
            new = dot(x, pairs[index // 2][index % 2, :, tile])
            query = new if query is None else query + new
        out_ref[rows, tile] = query


def gate_kernel(at_ref, x_ref, filtered_ref, partial_ref, *refs):
    count = (len(refs) - 2) // 2
    pieces, out_ref, (*held, sems) = refs[:count], refs[count], refs[count + 1 :]
    deep = pieces[0].shape[0]
    copies = []
    for index, target in enumerate(held):
        columns = pl.ds(pl.multiple_of(at_ref[index], deep), deep)
        copies.append(pltpu.make_async_copy(x_ref.at[:, columns], target, sems.at[index]))
        copies[-1].start()
    for copy in copies:
        copy.wait()
    for tile in tiles_of(out_ref):
        query = partial_ref[:, tile]
        for x, piece in zip(held, pieces):
            query = query + dot(x[...], piece[:, tile])
        out_ref[:, tile] = (query.astype(BF16).astype(F32) * filtered_ref[:, tile]).astype(BF16)


def gate(at, x, filtered, partial, pieces):
    length, deep = x.shape[0], pieces[0].shape[0]
    return pl.pallas_call(
        gate_kernel,
        out_shape=jax.ShapeDtypeStruct(filtered.shape, BF16),
        in_specs=[pl.BlockSpec(memory_space=pltpu.SMEM), pl.BlockSpec(memory_space=pl.ANY)]
        + [WHOLE] * (2 + len(pieces)),
        out_specs=WHOLE,
        scratch_shapes=[pltpu.VMEM((length, deep), BF16) for _ in pieces]
        + [pltpu.SemaphoreType.DMA((len(pieces),))],
        compiler_params=pltpu.CompilerParams(vmem_limit_bytes=GRANT),
        cost_estimate=pl.CostEstimate(flops=1, bytes_accessed=1, transcendentals=0),
    )(at, x, filtered, partial, *pieces)


def call(kernel, scalars, operands, out, scratch=()):
    return pl.pallas_call(
        kernel,
        out_shape=out,
        in_specs=[pl.BlockSpec(memory_space=pltpu.SMEM)] + [WHOLE] * len(operands),
        out_specs=jax.tree.map(lambda _: WHOLE, out),
        scratch_shapes=scratch,
        compiler_params=pltpu.CompilerParams(vmem_limit_bytes=GRANT),
        cost_estimate=pl.CostEstimate(flops=1, bytes_accessed=1, transcendentals=0),
    )(scalars, *operands)


def project(kernel, at, xs, extra, pieces, out_dtype):
    rows = sum(x.shape[0] for x in xs)
    out = jax.ShapeDtypeStruct((rows, pieces[0].shape[-1]), out_dtype)
    return call(functools.partial(kernel, len(xs)), at, (*xs, *extra, *pieces), out)


def product_kernel(parts, count, at_ref, *refs):
    xs, refs = refs[:parts], refs[parts:]
    given, refs = refs[:count], refs[count:]
    outs, (joined, *pieces, sems) = refs[:parts], refs[parts:]
    ends = [0]
    for x_ref in xs:
        ends.append(ends[-1] + x_ref.shape[0])
    targets = [joined.at[low:high] for low, high in zip(ends, ends[1:])] + list(pieces)
    copies = [
        pltpu.make_async_copy(source, target, sems.at[index])
        for index, (source, target) in enumerate(zip((*xs, *given), targets))
    ]
    for copy in copies:
        copy.start()
    for copy in copies[:parts]:
        copy.wait()
    deep = pieces[0].shape[1]
    half = pieces[0].shape[2]
    tile = math.gcd(half, 256)
    for low in range(0, half, tile):
        columns = slice(low, low + tile)
        key = value = None
        for index, piece in enumerate(pieces):
            if low == 0:
                copies[parts + index].wait()
            x = columns_of(joined, at_ref, index, deep)
            new_key, new_value = dot(x, piece[0, :, columns]), dot(x, piece[1, :, columns])
            key = new_key if key is None else key + new_key
            value = new_value if value is None else value + new_value
        product = key.astype(BF16).astype(F32) * value.astype(BF16).astype(F32)
        for out, start, end in zip(outs, ends, ends[1:]):
            out[:, columns] = product[start:end]


def products(at, xs, pieces):
    half = pieces[0].shape[2]
    held = [pltpu.VMEM((sum(x.shape[0] for x in xs), xs[0].shape[1]), BF16)]
    held += [pltpu.VMEM(piece.shape, BF16) for piece in pieces]
    held.append(pltpu.SemaphoreType.DMA((len(xs) + len(pieces),)))
    return pl.pallas_call(
        functools.partial(product_kernel, len(xs), len(pieces)),
        out_shape=[jax.ShapeDtypeStruct((x.shape[0], half), F32) for x in xs],
        in_specs=[pl.BlockSpec(memory_space=pltpu.SMEM)]
        + [pl.BlockSpec(memory_space=pl.ANY)] * (len(xs) + len(pieces)),
        out_specs=[WHOLE] * len(xs),
        scratch_shapes=held,
        compiler_params=pltpu.CompilerParams(vmem_limit_bytes=56 << 20),
        cost_estimate=pl.CostEstimate(flops=1, bytes_accessed=1, transcendentals=0),
    )(at, *xs, *pieces)


def filter_kernel(_, product_ref, halo_ref, taps_ref, out_ref, held):
    length, pad = product_ref.shape[0], halo_ref.shape[0]
    held[:pad] = halo_ref[...]
    held[pad:] = product_ref[...]
    for tile in tiles_of(out_ref):
        total = None
        for offset in range(taps_ref.shape[0]):
            term = taps_ref[offset : offset + 1, tile] * held[pad - offset : pad - offset + length, tile]
            total = term if total is None else total + term
        out_ref[:, tile] = total


def causal_filter(at, product, halo, taps):
    length, half = product.shape
    out = jax.ShapeDtypeStruct(product.shape, F32)
    scratch = [pltpu.VMEM((halo.shape[0] + length, half), F32)]
    return call(filter_kernel, at, (product, halo, taps), out, scratch)


def terms_kernel(plan, turned, n_tp, at_ref, *refs):
    gates, refs, held = refs[:4], refs[4:-1], refs[-1]
    count = sum(len(parts) for parts in plan)
    weights, outs = refs[:count], refs[count:]
    half = gates[0].shape[1]
    rows = gates[0].shape[0] // n_tp
    for slot in range(n_tp):
        for index, gate in enumerate(gates):
            side, whose = index % 2, index // 2
            place = slice((2 * slot + whose) * rows, (2 * slot + whose + 1) * rows)
            owner = lax.rem(at_ref[1] + slot, n_tp) * rows if turned else slot * rows
            column = (at_ref[0] if side == 0 else 1 - at_ref[0]) * half
            taken = gate[pl.ds(pl.multiple_of(owner, rows), rows)]
            held[place, pl.ds(pl.multiple_of(column, half), half)] = taken
    wide = weights[0].shape[1]
    share = held.shape[0] // len(outs)
    used = 0
    for index, parts in enumerate(plan):
        at = slice(index * wide, (index + 1) * wide)
        for piece in range(0, held.shape[0], share):
            total, depth = None, 0
            for which in range(len(parts)):
                weight = weights[used + which]
                low, depth = depth, depth + weight.shape[0]
                new = dot(held[piece : piece + share, low:depth], weight[...])
                total = new if total is None else total + new
            outs[piece // share][:, at] = total.astype(BF16)
        used += len(parts)


def terms(n_tp, place, gates, blocks, turned):
    length, half = gates[0].shape
    weights = [part for parts in blocks for part in parts]
    cols = len(blocks) * weights[0].shape[1]
    slots = n_tp if turned else 1
    out = [jax.ShapeDtypeStruct((2 * length // slots, cols), BF16)] * slots
    kernel = functools.partial(terms_kernel, blocks_plan(blocks), turned, n_tp)
    scratch = [pltpu.VMEM((2 * length, 2 * half), BF16)]
    result = call(kernel, place, (*gates, *weights), out, scratch)
    return result if turned else result[0]


def blocks_plan(blocks):
    return [range(len(parts)) for parts in blocks]


def first_kernel(n_tp, at_ref, *refs):
    gates, (weight_ref, out_ref, held, ready, sem) = refs[:4], refs[4:]
    half = gates[0].shape[1]
    rows = gates[0].shape[0] // n_tp
    for slot in range(n_tp):
        for index, taken in enumerate(gates):
            side, whose = index % 2, index // 2
            place = slice((2 * slot + whose) * rows, (2 * slot + whose + 1) * rows)
            column = (at_ref[0] if side == 0 else 1 - at_ref[0]) * half
            columns = pl.ds(pl.multiple_of(column, half), half)
            held[place, columns] = taken[slot * rows : (slot + 1) * rows]
    ready[...] = dot(held[...], weight_ref[...]).astype(BF16)
    copy = pltpu.make_async_copy(ready, out_ref.at[:, : ready.shape[1]], sem)
    copy.start()
    copy.wait()


def rest_kernel(held, *refs):
    count = (len(refs) - 5) // 2
    given, (_, out_ref), (*weights, ready, sems, out_sems) = (
        refs[:count],
        refs[count : count + 2],
        refs[count + 2 :],
    )
    copies = [
        pltpu.make_async_copy(source, target, sems.at[index])
        for index, (source, target) in enumerate(zip(given, weights))
    ]
    for copy in copies:
        copy.start()
    wide = weights[0].shape[1]
    leaving = []
    for index, weight in enumerate(weights):
        copies[index].wait()
        at = slice(index * wide, (index + 1) * wide)
        ready[:, at] = dot(held[...], weight[...]).astype(BF16)
        to = out_ref.at[:, (index + 1) * wide : (index + 2) * wide]
        leaving.append(pltpu.make_async_copy(ready.at[:, at], to, out_sems.at[index]))
        leaving[-1].start()
    for copy in leaving:
        copy.wait()


def first_terms(n_tp, place, gates, weight, blocks):
    length, half = gates[0].shape
    wide = weight.shape[1]
    return pl.pallas_call(
        functools.partial(first_kernel, n_tp),
        out_shape=[
            jax.ShapeDtypeStruct((2 * length, blocks * wide), BF16),
            jax.ShapeDtypeStruct((2 * length, 2 * half), BF16),
        ],
        in_specs=[pl.BlockSpec(memory_space=pltpu.SMEM)] + [WHOLE] * 5,
        out_specs=[pl.BlockSpec(memory_space=pl.ANY), WHOLE],
        scratch_shapes=[pltpu.VMEM((2 * length, wide), BF16), pltpu.SemaphoreType.DMA],
        compiler_params=pltpu.CompilerParams(vmem_limit_bytes=GRANT),
        cost_estimate=pl.CostEstimate(flops=1, bytes_accessed=1, transcendentals=0),
    )(place, *gates, weight)


def rest_terms(held, found, weights):
    anywhere = pl.BlockSpec(memory_space=pl.ANY)
    count, wide = len(weights), weights[0].shape[1]
    return pl.pallas_call(
        rest_kernel,
        out_shape=jax.ShapeDtypeStruct(found.shape, BF16),
        in_specs=[WHOLE] + [anywhere] * (count + 1),
        out_specs=anywhere,
        input_output_aliases={count + 1: 0},
        scratch_shapes=[pltpu.VMEM(weight.shape, BF16) for weight in weights]
        + [pltpu.VMEM((found.shape[0], count * wide), BF16)]
        + [pltpu.SemaphoreType.DMA((count,))] * 2,
        compiler_params=pltpu.CompilerParams(vmem_limit_bytes=2 * GRANT),
        cost_estimate=pl.CostEstimate(flops=1, bytes_accessed=1, transcendentals=0),
    )(held, *weights, found)


def on_device(tokens, norm_gain, in_weight, filters, out_weight, keep_mask):
    n_seq, n_tp = lax.axis_size("seq"), lax.axis_size("tp")
    chips = n_seq // 2
    ny, nx = grid_of(chips)
    seq = lax.axis_index("seq")
    core, here = seq % 2, seq // 2
    my_y, my_x = here // nx, here % nx
    rows, model = tokens.shape
    length = rows * n_tp
    deep, channels = in_weight.shape[1:]
    half = channels // 2
    wide = out_weight.shape[1]

    def place(y, x, c):
        return ((y % ny) * nx + x % nx) * 2 + c

    def from_chip(block, dy, dx):
        route = [
            (place(y + dy, x + dx, c), place(y, x, c))
            for y in range(ny)
            for x in range(nx)
            for c in range(2)
        ]
        return lax.ppermute(block, "seq", route)

    def from_partner(block):
        return lax.ppermute(block, "seq", [(s, s ^ 1) for s in range(n_seq)])

    def direct(mine, brought):
        along_x = [(mine, brought)]
        along_y = [(mine, brought)]
        along_x += [tuple(from_chip(b, 0, dx) for b in (mine, brought)) for dx in range(1, nx)]
        along_y += [tuple(from_chip(b, dy, 0) for b in (mine, brought)) for dy in range(1, ny)]
        return along_x, along_y

    def onward(along_x, along_y):
        return {
            (dy, dx): (from_chip(along_x[dx][0], dy, 0), from_chip(along_y[dy][1], 0, dx))
            for dy in range(1, ny)
            for dx in range(1, nx)
        }

    def crossed(along_x, along_y):
        return {
            (dy, dx): (from_chip(along_x[0, dx][0], dy, 0), from_chip(along_y[dy, 0][1], 0, dx))
            for dy, _ in along_y
            for _, dx in along_x
        }

    def listed(along_x, along_y, rest):
        found = {(0, dx): pair for dx, pair in enumerate(along_x)}
        found.update({(dy, 0): pair for dy, pair in enumerate(along_y)})
        found.update(rest)
        return found

    def by_core(mine, other, axis):
        return jnp.where(
            core == 0,
            jnp.concatenate([mine, other], axis=axis),
            jnp.concatenate([other, mine], axis=axis),
        )

    def columns(array, first, count, at):
        return lax.dynamic_slice(array, (first, 0, at * half), (count, deep, half))

    mine_kv = columns(in_weight, 1, 2, core)
    away_kv = columns(in_weight, 1, 2, 1 - core)
    brought_kv = from_partner(away_kv)
    kv_x, kv_y = direct(mine_kv, brought_kv)

    tokens_then, _ = lax.optimization_barrier((tokens, away_kv))
    widened = tokens_then.astype(F32)
    mean_sq = jnp.mean(widened * widened, axis=1, keepdims=True)
    normed = (widened * lax.rsqrt(mean_sq + 1e-06) * norm_gain).astype(BF16)
    own_rows = lax.all_gather(normed, "tp", axis=0, tiled=True)
    in_weight_then, _ = lax.optimization_barrier((in_weight, normed))
    mine_q = columns(in_weight_then, 0, 1, core)[0]
    both_q = jnp.stack([mine_q, from_partner(columns(in_weight_then, 0, 1, 1 - core)[0])])

    kv_x, kv_y, both_q = lax.optimization_barrier((kv_x, kv_y, both_q))
    kv_rest = onward(kv_x, kv_y)
    q_x = {(0, dx): from_chip(both_q, 0, dx) for dx in range(1, nx)}
    q_y = {(dy, 0): from_chip(both_q, dy, 0) for dy in range(1, ny)}
    arrived = (kv_x, kv_y, kv_rest)
    own_rows, arrived = lax.optimization_barrier((own_rows, arrived))
    kv_x, kv_y, kv_rest = arrived
    kv = listed(kv_x, kv_y, kv_rest)
    order = list(kv)
    kv_pieces = [piece for key in order for piece in kv[key]]
    at = jnp.stack(
        [place(my_y + dy, my_x + dx, core ^ rc) * deep for dy, dx in order for rc in range(2)]
    ).astype(jnp.int32)
    early = 2 * (ny + nx - 1)

    (own_product,) = products(at, [own_rows], kv_pieces)
    reach = filters.shape[0] - 1
    pad = -(-reach // 16) * 16
    ends = [
        lax.ppermute(own_rows[length - pad :], "seq", [(2 * i + 1, 2 * i + 2 + c) for i in range(chips - 1)])
        for c in range(2)
    ]
    before = jnp.where(core == 0, ends[0], ends[1])
    ready = (own_rows, q_x, q_y, own_product, before)
    rows_then, q_x, q_y, own_product, before = lax.optimization_barrier(ready)
    other_rows = from_partner(rows_then)
    q_rest = crossed(q_x, q_y)
    q_pairs = {(0, 0): both_q, **q_x, **q_y}
    q_early = [q_pairs[key] for key in order if key in q_pairs]
    own_query = project(query_kernel, at, [own_rows], [], q_early, F32)
    other_rows, own_query = lax.optimization_barrier((other_rows, own_query))
    rim, other_product = products(at, [before, other_rows], kv_pieces)
    own_tail, other_tail = own_product[length - pad :], other_product[length - pad :]
    first_tail = jnp.where(core == 0, own_tail, other_tail)
    groups = filters.shape[1] // 2
    taps = jnp.repeat(
        lax.dynamic_slice_in_dim(filters, core * groups, groups, axis=1), half // groups, axis=1
    )
    own_filtered = causal_filter(at, own_product, jnp.where(core == 0, rim, first_tail), taps)
    other_filtered = causal_filter(at, other_product, jnp.where(core == 0, first_tail, rim), taps)

    other_rows, own_filtered, other_filtered = lax.optimization_barrier(
        (other_rows, own_filtered, other_filtered)
    )
    other_query = project(query_kernel, at, [other_rows], [], q_early, F32)
    weight_then, q_x, q_y = lax.optimization_barrier((out_weight, q_x, q_y))
    o_x = {(0, dx): from_chip(weight_then, 0, dx) for dx in range(1, nx)}
    o_y = {(dy, 0): from_chip(weight_then, dy, 0) for dy in range(1, ny)}
    o_rest = {
        (dy, dx): (
            from_chip(o_x[0, dx][:half], dy, 0),
            from_chip(o_y[dy, 0][half:], 0, dx),
        )
        for dy in range(1, ny)
        for dx in range(1, nx)
    }
    late = [piece for pair in q_rest.values() for piece in pair]
    other_gated = gate(at[early:], other_rows, other_filtered, other_query, late)
    own_gated = gate(at[early:], own_rows, own_filtered, own_query, late)
    gates = (own_gated, from_partner(other_gated), other_gated, from_partner(own_gated))

    position = lax.axis_index("tp")
    here_at = jnp.stack([core, position]).astype(jnp.int32)
    up = [(i, i + 1) for i in range(n_tp - 1)]
    down = [(i + 1, i) for i in range(n_tp - 1)]

    def plus(a, b):
        return (a.astype(F32) + b.astype(F32)).astype(BF16)

    def chained(slots):
        rising = falling = None
        for step in range(n_tp - 1):
            send_up, send_down = slots[n_tp - 1 - step], slots[step + 1]
            if step:
                send_up, send_down = plus(send_up, rising), plus(send_down, falling)
            rising = lax.ppermute(send_up, "tp", up)
            falling = lax.ppermute(send_down, "tp", down)
        total = slots[0].astype(F32) + rising.astype(F32) + falling.astype(F32)
        return total

    near = {(0, 0): (out_weight,)}
    near.update({key: (block,) for key, block in (*o_x.items(), *o_y.items())})
    found, held = first_terms(n_tp, here_at, gates, out_weight, len(near))
    found = rest_terms(held, found, [*o_x.values(), *o_y.values()])
    gates, found = lax.optimization_barrier((gates, found))
    near_sum = lax.psum_scatter(found, "tp", scatter_dimension=0, tiled=True)
    far_sum = chained(terms(n_tp, here_at, gates, list(o_rest.values()), True))
    result = jnp.zeros((rows, model), BF16)
    for keys, mixed in ((list(near), near_sum), (list(o_rest), far_sum)):
        theirs = from_partner(mixed[rows:].astype(BF16)).astype(F32)
        mine = mixed[:rows].astype(F32)
        for index, (dy, dx) in enumerate(keys):
            start = place(my_y + dy, my_x + dx, 0) * wide
            here_columns = slice(index * wide, (index + 1) * wide)
            pair = by_core(mine[:, here_columns], theirs[:, here_columns], 1)
            kept = lax.dynamic_slice_in_dim(keep_mask, start, 2 * wide, axis=1).astype(F32)
            base = lax.dynamic_slice_in_dim(tokens, start, 2 * wide, axis=1).astype(F32)
            part = (base + kept * pair * (1.0 / 0.9)).astype(BF16)
            result = lax.dynamic_update_slice_in_dim(result, part, start, axis=1)
    return result


def solution(mesh):
    in_specs = (
        P(("seq", "tp"), None),
        P(),
        P(None, "seq", "tp"),
        P(None, "tp"),
        P("tp", "seq"),
        P(("seq", "tp"), None),
    )
    out_specs = P(("seq", "tp"), None)
    return jax.shard_map(
        on_device, mesh=mesh, in_specs=in_specs, out_specs=out_specs, check_vma=False
    )
```

```python
import functools
import math

import jax
import jax.numpy as jnp
from jax import lax
from jax.experimental import pallas as pl
from jax.experimental.pallas import tpu as pltpu
from jax.sharding import PartitionSpec as P

F32 = jnp.float32
BF16 = jnp.bfloat16
GRANT = 12 << 20
WHOLE = pl.BlockSpec(memory_space=pltpu.VMEM)


def grid_of(chips):
    ny = max(d for d in range(1, math.isqrt(chips) + 1) if chips % d == 0)
    return ny, chips // ny


def dot(a, b):
    return jnp.dot(a, b, preferred_element_type=F32)


def columns_of(x_ref, at_ref, index, deep):
    return x_ref[:, pl.ds(pl.multiple_of(at_ref[index], deep), deep)]


def tiles_of(out_ref):
    tile = math.gcd(out_ref.shape[1], 256)
    return [slice(at, at + tile) for at in range(0, out_ref.shape[1], tile)]


def blocks_of(xs, out_ref):
    tile = math.gcd(out_ref.shape[1], 256)
    size = xs[0].shape[0]
    for at in range(0, out_ref.shape[1], tile):
        for index, x_ref in enumerate(xs):
            yield x_ref, slice(index * size, (index + 1) * size), slice(at, at + tile)


def query_kernel(parts, at_ref, *refs):
    xs, pairs, out_ref = refs[:parts], refs[parts:-1], refs[-1]
    deep = pairs[0].shape[1]
    for x_ref, rows, tile in blocks_of(xs, out_ref):
        query = None
        for index in range(2 * len(pairs)):
            x = columns_of(x_ref, at_ref, index, deep)
            new = dot(x, pairs[index // 2][index % 2, :, tile])
            query = new if query is None else query + new
        out_ref[rows, tile] = query


def gate_kernel(parts, at_ref, *refs):
    xs, refs = refs[:parts], refs[parts:]
    filtered_ref, partial_ref, pieces, out_ref = refs[0], refs[1], refs[2:-1], refs[-1]
    deep = pieces[0].shape[0]
    for x_ref, rows, tile in blocks_of(xs, out_ref):
        query = partial_ref[rows, tile]
        for index, piece in enumerate(pieces):
            query = query + dot(columns_of(x_ref, at_ref, index, deep), piece[:, tile])
        gated = query.astype(BF16).astype(F32) * filtered_ref[rows, tile]
        out_ref[rows, tile] = gated.astype(BF16)


def call(kernel, scalars, operands, out, scratch=()):
    return pl.pallas_call(
        kernel,
        out_shape=out,
        in_specs=[pl.BlockSpec(memory_space=pltpu.SMEM)] + [WHOLE] * len(operands),
        out_specs=jax.tree.map(lambda _: WHOLE, out),
        scratch_shapes=scratch,
        compiler_params=pltpu.CompilerParams(vmem_limit_bytes=GRANT),
        cost_estimate=pl.CostEstimate(flops=1, bytes_accessed=1, transcendentals=0),
    )(scalars, *operands)


def project(kernel, at, xs, extra, pieces, out_dtype):
    rows = sum(x.shape[0] for x in xs)
    out = jax.ShapeDtypeStruct((rows, pieces[0].shape[-1]), out_dtype)
    return call(functools.partial(kernel, len(xs)), at, (*xs, *extra, *pieces), out)


def product_kernel(parts, count, at_ref, *refs):
    xs, refs = refs[:parts], refs[parts:]
    given, refs = refs[:count], refs[count:]
    outs, (joined, *pieces, sems) = refs[:parts], refs[parts:]
    ends = [0]
    for x_ref in xs:
        ends.append(ends[-1] + x_ref.shape[0])
    targets = [joined.at[low:high] for low, high in zip(ends, ends[1:])] + list(pieces)
    copies = [
        pltpu.make_async_copy(source, target, sems.at[index])
        for index, (source, target) in enumerate(zip((*xs, *given), targets))
    ]
    for copy in copies:
        copy.start()
    for copy in copies[:parts]:
        copy.wait()
    deep = pieces[0].shape[1]
    half = pieces[0].shape[2]
    tile = math.gcd(half, 256)
    for low in range(0, half, tile):
        columns = slice(low, low + tile)
        key = value = None
        for index, piece in enumerate(pieces):
            if low == 0:
                copies[parts + index].wait()
            x = columns_of(joined, at_ref, index, deep)
            new_key, new_value = dot(x, piece[0, :, columns]), dot(x, piece[1, :, columns])
            key = new_key if key is None else key + new_key
            value = new_value if value is None else value + new_value
        product = key.astype(BF16).astype(F32) * value.astype(BF16).astype(F32)
        for out, start, end in zip(outs, ends, ends[1:]):
            out[:, columns] = product[start:end]


def products(at, xs, pieces):
    half = pieces[0].shape[2]
    held = [pltpu.VMEM((sum(x.shape[0] for x in xs), xs[0].shape[1]), BF16)]
    held += [pltpu.VMEM(piece.shape, BF16) for piece in pieces]
    held.append(pltpu.SemaphoreType.DMA((len(xs) + len(pieces),)))
    return pl.pallas_call(
        functools.partial(product_kernel, len(xs), len(pieces)),
        out_shape=[jax.ShapeDtypeStruct((x.shape[0], half), F32) for x in xs],
        in_specs=[pl.BlockSpec(memory_space=pltpu.SMEM)]
        + [pl.BlockSpec(memory_space=pl.ANY)] * (len(xs) + len(pieces)),
        out_specs=[WHOLE] * len(xs),
        scratch_shapes=held,
        compiler_params=pltpu.CompilerParams(vmem_limit_bytes=56 << 20),
        cost_estimate=pl.CostEstimate(flops=1, bytes_accessed=1, transcendentals=0),
    )(at, *xs, *pieces)


def filter_kernel(_, product_ref, halo_ref, taps_ref, out_ref, held):
    length, pad = product_ref.shape[0], halo_ref.shape[0]
    held[:pad] = halo_ref[...]
    held[pad:] = product_ref[...]
    for tile in tiles_of(out_ref):
        total = None
        for offset in range(taps_ref.shape[0]):
            term = taps_ref[offset : offset + 1, tile] * held[pad - offset : pad - offset + length, tile]
            total = term if total is None else total + term
        out_ref[:, tile] = total


def causal_filter(at, product, halo, taps):
    length, half = product.shape
    out = jax.ShapeDtypeStruct(product.shape, F32)
    scratch = [pltpu.VMEM((halo.shape[0] + length, half), F32)]
    return call(filter_kernel, at, (product, halo, taps), out, scratch)


def terms_kernel(plan, turned, n_tp, at_ref, *refs):
    gates, refs, held = refs[:4], refs[4:-1], refs[-1]
    count = sum(len(parts) for parts in plan)
    weights, outs = refs[:count], refs[count:]
    half = gates[0].shape[1]
    rows = gates[0].shape[0] // n_tp
    for slot in range(n_tp):
        for index, gate in enumerate(gates):
            side, whose = index % 2, index // 2
            place = slice((2 * slot + whose) * rows, (2 * slot + whose + 1) * rows)
            owner = lax.rem(at_ref[1] + slot, n_tp) * rows if turned else slot * rows
            column = (at_ref[0] if side == 0 else 1 - at_ref[0]) * half
            taken = gate[pl.ds(pl.multiple_of(owner, rows), rows)]
            held[place, pl.ds(pl.multiple_of(column, half), half)] = taken
    wide = weights[0].shape[1]
    share = held.shape[0] // len(outs)
    used = 0
    for index, parts in enumerate(plan):
        at = slice(index * wide, (index + 1) * wide)
        for piece in range(0, held.shape[0], share):
            total, depth = None, 0
            for which in range(len(parts)):
                weight = weights[used + which]
                low, depth = depth, depth + weight.shape[0]
                new = dot(held[piece : piece + share, low:depth], weight[...])
                total = new if total is None else total + new
            outs[piece // share][:, at] = total.astype(BF16)
        used += len(parts)


def terms(n_tp, place, gates, blocks, turned):
    length, half = gates[0].shape
    weights = [part for parts in blocks for part in parts]
    cols = len(blocks) * weights[0].shape[1]
    slots = n_tp if turned else 1
    out = [jax.ShapeDtypeStruct((2 * length // slots, cols), BF16)] * slots
    kernel = functools.partial(terms_kernel, blocks_plan(blocks), turned, n_tp)
    scratch = [pltpu.VMEM((2 * length, 2 * half), BF16)]
    result = call(kernel, place, (*gates, *weights), out, scratch)
    return result if turned else result[0]


def blocks_plan(blocks):
    return [range(len(parts)) for parts in blocks]


def near_kernel(n_tp, at_ref, *refs):
    gates, refs = refs[:4], refs[4:]
    count = (len(refs) - 4) // 2
    given, (out_ref, held, *refs) = refs[:count], refs[count:]
    weights, (ready, sems, out_sems) = refs[:count], refs[count:]
    copies = [
        pltpu.make_async_copy(source, target, sems.at[index])
        for index, (source, target) in enumerate(zip(given, weights))
    ]
    for copy in copies:
        copy.start()
    half = gates[0].shape[1]
    rows = gates[0].shape[0] // n_tp
    for slot in range(n_tp):
        for index, gate in enumerate(gates):
            side, whose = index % 2, index // 2
            place = slice((2 * slot + whose) * rows, (2 * slot + whose + 1) * rows)
            column = (at_ref[0] if side == 0 else 1 - at_ref[0]) * half
            columns = pl.ds(pl.multiple_of(column, half), half)
            held[place, columns] = gate[slot * rows : (slot + 1) * rows]
    wide = weights[0].shape[1]
    leaving = []
    for index, weight in enumerate(weights):
        copies[index].wait()
        at = slice(index * wide, (index + 1) * wide)
        ready[:, at] = dot(held[...], weight[...]).astype(BF16)
        leaving.append(pltpu.make_async_copy(ready.at[:, at], out_ref.at[:, at], out_sems.at[index]))
        leaving[-1].start()
    for copy in leaving:
        copy.wait()


def near_terms(n_tp, place, gates, weights):
    length, half = gates[0].shape
    shape = (2 * length, len(weights) * weights[0].shape[1])
    anywhere = pl.BlockSpec(memory_space=pl.ANY)
    return pl.pallas_call(
        functools.partial(near_kernel, n_tp),
        out_shape=jax.ShapeDtypeStruct(shape, BF16),
        in_specs=[pl.BlockSpec(memory_space=pltpu.SMEM)]
        + [WHOLE] * 4
        + [anywhere] * len(weights),
        out_specs=anywhere,
        scratch_shapes=[pltpu.VMEM((2 * length, 2 * half), BF16)]
        + [pltpu.VMEM(weight.shape, BF16) for weight in weights]
        + [pltpu.VMEM(shape, BF16)]
        + [pltpu.SemaphoreType.DMA((len(weights),))] * 2,
        compiler_params=pltpu.CompilerParams(vmem_limit_bytes=24 << 20),
        cost_estimate=pl.CostEstimate(flops=1, bytes_accessed=1, transcendentals=0),
    )(place, *gates, *weights)


def on_device(tokens, norm_gain, in_weight, filters, out_weight, keep_mask):
    n_seq, n_tp = lax.axis_size("seq"), lax.axis_size("tp")
    chips = n_seq // 2
    ny, nx = grid_of(chips)
    seq = lax.axis_index("seq")
    core, here = seq % 2, seq // 2
    my_y, my_x = here // nx, here % nx
    rows, model = tokens.shape
    length = rows * n_tp
    deep, channels = in_weight.shape[1:]
    half = channels // 2
    wide = out_weight.shape[1]

    def place(y, x, c):
        return ((y % ny) * nx + x % nx) * 2 + c

    def from_chip(block, dy, dx):
        route = [
            (place(y + dy, x + dx, c), place(y, x, c))
            for y in range(ny)
            for x in range(nx)
            for c in range(2)
        ]
        return lax.ppermute(block, "seq", route)

    def from_partner(block):
        return lax.ppermute(block, "seq", [(s, s ^ 1) for s in range(n_seq)])

    def direct(mine, brought):
        along_x = [(mine, brought)]
        along_y = [(mine, brought)]
        along_x += [tuple(from_chip(b, 0, dx) for b in (mine, brought)) for dx in range(1, nx)]
        along_y += [tuple(from_chip(b, dy, 0) for b in (mine, brought)) for dy in range(1, ny)]
        return along_x, along_y

    def onward(along_x, along_y):
        return {
            (dy, dx): (from_chip(along_x[dx][0], dy, 0), from_chip(along_y[dy][1], 0, dx))
            for dy in range(1, ny)
            for dx in range(1, nx)
        }

    def crossed(along_x, along_y):
        return {
            (dy, dx): (from_chip(along_x[0, dx][0], dy, 0), from_chip(along_y[dy, 0][1], 0, dx))
            for dy, _ in along_y
            for _, dx in along_x
        }

    def listed(along_x, along_y, rest):
        found = {(0, dx): pair for dx, pair in enumerate(along_x)}
        found.update({(dy, 0): pair for dy, pair in enumerate(along_y)})
        found.update(rest)
        return found

    def by_core(mine, other, axis):
        return jnp.where(
            core == 0,
            jnp.concatenate([mine, other], axis=axis),
            jnp.concatenate([other, mine], axis=axis),
        )

    def columns(array, first, count, at):
        return lax.dynamic_slice(array, (first, 0, at * half), (count, deep, half))

    mine_kv = columns(in_weight, 1, 2, core)
    away_kv = columns(in_weight, 1, 2, 1 - core)
    brought_kv = from_partner(away_kv)
    kv_x, kv_y = direct(mine_kv, brought_kv)

    tokens_then, _ = lax.optimization_barrier((tokens, away_kv))
    widened = tokens_then.astype(F32)
    mean_sq = jnp.mean(widened * widened, axis=1, keepdims=True)
    normed = (widened * lax.rsqrt(mean_sq + 1e-06) * norm_gain).astype(BF16)
    own_rows = lax.all_gather(normed, "tp", axis=0, tiled=True)
    in_weight_then, _ = lax.optimization_barrier((in_weight, normed))
    mine_q = columns(in_weight_then, 0, 1, core)[0]
    both_q = jnp.stack([mine_q, from_partner(columns(in_weight_then, 0, 1, 1 - core)[0])])

    kv_x, kv_y, both_q = lax.optimization_barrier((kv_x, kv_y, both_q))
    kv_rest = onward(kv_x, kv_y)
    q_x = {(0, dx): from_chip(both_q, 0, dx) for dx in range(1, nx)}
    q_y = {(dy, 0): from_chip(both_q, dy, 0) for dy in range(1, ny)}
    arrived = (kv_x, kv_y, kv_rest)
    own_rows, arrived = lax.optimization_barrier((own_rows, arrived))
    kv_x, kv_y, kv_rest = arrived
    kv = listed(kv_x, kv_y, kv_rest)
    order = list(kv)
    kv_pieces = [piece for key in order for piece in kv[key]]
    at = jnp.stack(
        [place(my_y + dy, my_x + dx, core ^ rc) * deep for dy, dx in order for rc in range(2)]
    ).astype(jnp.int32)
    early = 2 * (ny + nx - 1)

    (own_product,) = products(at, [own_rows], kv_pieces)
    reach = filters.shape[0] - 1
    pad = -(-reach // 16) * 16
    ends = [
        lax.ppermute(own_rows[length - pad :], "seq", [(2 * i + 1, 2 * i + 2 + c) for i in range(chips - 1)])
        for c in range(2)
    ]
    before = jnp.where(core == 0, ends[0], ends[1])
    ready = (own_rows, q_x, q_y, own_product, before)
    rows_then, q_x, q_y, own_product, before = lax.optimization_barrier(ready)
    other_rows = from_partner(rows_then)
    q_rest = crossed(q_x, q_y)
    q_pairs = {(0, 0): both_q, **q_x, **q_y}
    q_early = [q_pairs[key] for key in order if key in q_pairs]
    own_query = project(query_kernel, at, [own_rows], [], q_early, F32)
    other_rows, own_query = lax.optimization_barrier((other_rows, own_query))
    rim, other_product = products(at, [before, other_rows], kv_pieces)
    own_tail, other_tail = own_product[length - pad :], other_product[length - pad :]
    first_tail = jnp.where(core == 0, own_tail, other_tail)
    groups = filters.shape[1] // 2
    taps = jnp.repeat(
        lax.dynamic_slice_in_dim(filters, core * groups, groups, axis=1), half // groups, axis=1
    )
    own_filtered = causal_filter(at, own_product, jnp.where(core == 0, rim, first_tail), taps)
    other_filtered = causal_filter(at, other_product, jnp.where(core == 0, first_tail, rim), taps)

    other_rows, own_filtered, other_filtered = lax.optimization_barrier(
        (other_rows, own_filtered, other_filtered)
    )
    other_query = project(query_kernel, at, [other_rows], [], q_early, F32)
    weight_then, q_x, q_y = lax.optimization_barrier((out_weight, q_x, q_y))
    o_x = {(0, dx): from_chip(weight_then, 0, dx) for dx in range(1, nx)}
    o_y = {(dy, 0): from_chip(weight_then, dy, 0) for dy in range(1, ny)}
    o_rest = {
        (dy, dx): (
            from_chip(o_x[0, dx][:half], dy, 0),
            from_chip(o_y[dy, 0][half:], 0, dx),
        )
        for dy in range(1, ny)
        for dx in range(1, nx)
    }
    late = [piece for pair in q_rest.values() for piece in pair]
    other_gated = project(
        gate_kernel, at[early:], [other_rows], [other_filtered, other_query], late, BF16
    )
    own_gated = project(
        gate_kernel, at[early:], [own_rows], [own_filtered, own_query], late, BF16
    )
    gates = (own_gated, from_partner(other_gated), other_gated, from_partner(own_gated))

    position = lax.axis_index("tp")
    here_at = jnp.stack([core, position]).astype(jnp.int32)
    def collected(slots):
        total = slots[0].astype(F32)
        for away in range(1, n_tp):
            route = [(i, (i + away) % n_tp) for i in range(n_tp)]
            total = total + lax.ppermute(slots[away], "tp", route).astype(F32)
        return total

    near = {(0, 0): (out_weight,)}
    near.update({key: (block,) for key, block in (*o_x.items(), *o_y.items())})
    found = near_terms(n_tp, here_at, gates, [block for (block,) in near.values()])
    gates, found = lax.optimization_barrier((gates, found))
    near_sum = lax.psum_scatter(found, "tp", scatter_dimension=0, tiled=True)
    far_sum = collected(terms(n_tp, here_at, gates, list(o_rest.values()), True))
    result = jnp.zeros((rows, model), BF16)
    far_theirs = from_partner(far_sum[rows:].astype(BF16))
    near_sum, far_theirs, far_sum = lax.optimization_barrier((near_sum, far_theirs, far_sum))
    near_theirs = from_partner(near_sum[rows:].astype(BF16))
    parts = (list(o_rest), far_sum, far_theirs), (list(near), near_sum, near_theirs)
    for keys, mixed, theirs in parts:
        theirs = theirs.astype(F32)
        mine = mixed[:rows].astype(F32)
        for index, (dy, dx) in enumerate(keys):
            start = place(my_y + dy, my_x + dx, 0) * wide
            here_columns = slice(index * wide, (index + 1) * wide)
            pair = by_core(mine[:, here_columns], theirs[:, here_columns], 1)
            kept = lax.dynamic_slice_in_dim(keep_mask, start, 2 * wide, axis=1).astype(F32)
            base = lax.dynamic_slice_in_dim(tokens, start, 2 * wide, axis=1).astype(F32)
            part = (base + kept * pair * (1.0 / 0.9)).astype(BF16)
            result = lax.dynamic_update_slice_in_dim(result, part, start, axis=1)
    return result


def solution(mesh):
    in_specs = (
        P(("seq", "tp"), None),
        P(),
        P(None, "seq", "tp"),
        P(None, "tp"),
        P("tp", "seq"),
        P(("seq", "tp"), None),
    )
    out_specs = P(("seq", "tp"), None)
    return jax.shard_map(
        on_device, mesh=mesh, in_specs=in_specs, out_specs=out_specs, check_vma=False
    )
```

```python
import functools
import math

import jax
import jax.numpy as jnp
from jax import lax
from jax.experimental import pallas as pl
from jax.experimental.pallas import tpu as pltpu
from jax.sharding import PartitionSpec as P

F32 = jnp.float32
BF16 = jnp.bfloat16
GRANT = 12 << 20
WHOLE = pl.BlockSpec(memory_space=pltpu.VMEM)


def grid_of(chips):
    ny = max(d for d in range(1, math.isqrt(chips) + 1) if chips % d == 0)
    return ny, chips // ny


def dot(a, b):
    return jnp.dot(a, b, preferred_element_type=F32)


def columns_of(x_ref, at_ref, index, deep):
    return x_ref[:, pl.ds(pl.multiple_of(at_ref[index], deep), deep)]


def tiles_of(out_ref):
    tile = math.gcd(out_ref.shape[1], 256)
    return [slice(at, at + tile) for at in range(0, out_ref.shape[1], tile)]


def blocks_of(xs, out_ref):
    tile = math.gcd(out_ref.shape[1], 256)
    size = xs[0].shape[0]
    for at in range(0, out_ref.shape[1], tile):
        for index, x_ref in enumerate(xs):
            yield x_ref, slice(index * size, (index + 1) * size), slice(at, at + tile)


def query_kernel(parts, at_ref, *refs):
    xs, pairs, out_ref = refs[:parts], refs[parts:-1], refs[-1]
    deep = pairs[0].shape[1]
    for x_ref, rows, tile in blocks_of(xs, out_ref):
        query = None
        for index in range(2 * len(pairs)):
            x = columns_of(x_ref, at_ref, index, deep)
            new = dot(x, pairs[index // 2][index % 2, :, tile])
            query = new if query is None else query + new
        out_ref[rows, tile] = query


def gate_kernel(parts, at_ref, *refs):
    xs, refs = refs[:parts], refs[parts:]
    filtered_ref, partial_ref, pieces, out_ref = refs[0], refs[1], refs[2:-1], refs[-1]
    deep = pieces[0].shape[0]
    for x_ref, rows, tile in blocks_of(xs, out_ref):
        query = partial_ref[rows, tile]
        for index, piece in enumerate(pieces):
            query = query + dot(columns_of(x_ref, at_ref, index, deep), piece[:, tile])
        gated = query.astype(BF16).astype(F32) * filtered_ref[rows, tile]
        out_ref[rows, tile] = gated.astype(BF16)


def call(kernel, scalars, operands, out, scratch=()):
    return pl.pallas_call(
        kernel,
        out_shape=out,
        in_specs=[pl.BlockSpec(memory_space=pltpu.SMEM)] + [WHOLE] * len(operands),
        out_specs=jax.tree.map(lambda _: WHOLE, out),
        scratch_shapes=scratch,
        compiler_params=pltpu.CompilerParams(vmem_limit_bytes=GRANT),
        cost_estimate=pl.CostEstimate(flops=1, bytes_accessed=1, transcendentals=0),
    )(scalars, *operands)


def project(kernel, at, xs, extra, pieces, out_dtype):
    rows = sum(x.shape[0] for x in xs)
    out = jax.ShapeDtypeStruct((rows, pieces[0].shape[-1]), out_dtype)
    return call(functools.partial(kernel, len(xs)), at, (*xs, *extra, *pieces), out)


def product_kernel(parts, count, at_ref, *refs):
    xs, refs = refs[:parts], refs[parts:]
    given, refs = refs[:count], refs[count:]
    outs, (joined, *pieces, sems) = refs[:parts], refs[parts:]
    ends = [0]
    for x_ref in xs:
        ends.append(ends[-1] + x_ref.shape[0])
    targets = [joined.at[low:high] for low, high in zip(ends, ends[1:])] + list(pieces)
    copies = [
        pltpu.make_async_copy(source, target, sems.at[index])
        for index, (source, target) in enumerate(zip((*xs, *given), targets))
    ]
    for copy in copies:
        copy.start()
    for copy in copies[:parts]:
        copy.wait()
    deep = pieces[0].shape[1]
    half = pieces[0].shape[2]
    tile = math.gcd(half, 256)
    for low in range(0, half, tile):
        columns = slice(low, low + tile)
        key = value = None
        for index, piece in enumerate(pieces):
            if low == 0:
                copies[parts + index].wait()
            x = columns_of(joined, at_ref, index, deep)
            new_key, new_value = dot(x, piece[0, :, columns]), dot(x, piece[1, :, columns])
            key = new_key if key is None else key + new_key
            value = new_value if value is None else value + new_value
        product = key.astype(BF16).astype(F32) * value.astype(BF16).astype(F32)
        for out, start, end in zip(outs, ends, ends[1:]):
            out[:, columns] = product[start:end]


def products(at, xs, pieces):
    half = pieces[0].shape[2]
    held = [pltpu.VMEM((sum(x.shape[0] for x in xs), xs[0].shape[1]), BF16)]
    held += [pltpu.VMEM(piece.shape, BF16) for piece in pieces]
    held.append(pltpu.SemaphoreType.DMA((len(xs) + len(pieces),)))
    return pl.pallas_call(
        functools.partial(product_kernel, len(xs), len(pieces)),
        out_shape=[jax.ShapeDtypeStruct((x.shape[0], half), F32) for x in xs],
        in_specs=[pl.BlockSpec(memory_space=pltpu.SMEM)]
        + [pl.BlockSpec(memory_space=pl.ANY)] * (len(xs) + len(pieces)),
        out_specs=[WHOLE] * len(xs),
        scratch_shapes=held,
        compiler_params=pltpu.CompilerParams(vmem_limit_bytes=56 << 20),
        cost_estimate=pl.CostEstimate(flops=1, bytes_accessed=1, transcendentals=0),
    )(at, *xs, *pieces)


def filter_kernel(_, product_ref, halo_ref, taps_ref, out_ref, held):
    length, pad = product_ref.shape[0], halo_ref.shape[0]
    held[:pad] = halo_ref[...]
    held[pad:] = product_ref[...]
    for tile in tiles_of(out_ref):
        total = None
        for offset in range(taps_ref.shape[0]):
            term = taps_ref[offset : offset + 1, tile] * held[pad - offset : pad - offset + length, tile]
            total = term if total is None else total + term
        out_ref[:, tile] = total


def causal_filter(at, product, halo, taps):
    length, half = product.shape
    out = jax.ShapeDtypeStruct(product.shape, F32)
    scratch = [pltpu.VMEM((halo.shape[0] + length, half), F32)]
    return call(filter_kernel, at, (product, halo, taps), out, scratch)


def terms_kernel(plan, turned, n_tp, at_ref, *refs):
    gates, refs, held = refs[:4], refs[4:-1], refs[-1]
    count = sum(len(parts) for parts in plan)
    weights, outs = refs[:count], refs[count:]
    half = gates[0].shape[1]
    rows = gates[0].shape[0] // n_tp
    for slot in range(n_tp):
        for index, gate in enumerate(gates):
            side, whose = index % 2, index // 2
            place = slice((2 * slot + whose) * rows, (2 * slot + whose + 1) * rows)
            owner = lax.rem(at_ref[1] + slot, n_tp) * rows if turned else slot * rows
            column = (at_ref[0] if side == 0 else 1 - at_ref[0]) * half
            taken = gate[pl.ds(pl.multiple_of(owner, rows), rows)]
            held[place, pl.ds(pl.multiple_of(column, half), half)] = taken
    wide = weights[0].shape[1]
    share = held.shape[0] // len(outs)
    used = 0
    for index, parts in enumerate(plan):
        at = slice(index * wide, (index + 1) * wide)
        for piece in range(0, held.shape[0], share):
            total, depth = None, 0
            for which in range(len(parts)):
                weight = weights[used + which]
                low, depth = depth, depth + weight.shape[0]
                new = dot(held[piece : piece + share, low:depth], weight[...])
                total = new if total is None else total + new
            outs[piece // share][:, at] = total.astype(BF16)
        used += len(parts)


def terms(n_tp, place, gates, blocks, turned):
    length, half = gates[0].shape
    weights = [part for parts in blocks for part in parts]
    cols = len(blocks) * weights[0].shape[1]
    slots = n_tp if turned else 1
    out = [jax.ShapeDtypeStruct((2 * length // slots, cols), BF16)] * slots
    kernel = functools.partial(terms_kernel, blocks_plan(blocks), turned, n_tp)
    scratch = [pltpu.VMEM((2 * length, 2 * half), BF16)]
    result = call(kernel, place, (*gates, *weights), out, scratch)
    return result if turned else result[0]


def blocks_plan(blocks):
    return [range(len(parts)) for parts in blocks]


def near_kernel(n_tp, at_ref, *refs):
    gates, refs = refs[:4], refs[4:]
    count = (len(refs) - 4) // 2
    given, (out_ref, held, *refs) = refs[:count], refs[count:]
    weights, (ready, sems, out_sems) = refs[:count], refs[count:]
    copies = [
        pltpu.make_async_copy(source, target, sems.at[index])
        for index, (source, target) in enumerate(zip(given, weights))
    ]
    for copy in copies:
        copy.start()
    half = gates[0].shape[1]
    rows = gates[0].shape[0] // n_tp
    for slot in range(n_tp):
        for index, gate in enumerate(gates):
            side, whose = index % 2, index // 2
            place = slice((2 * slot + whose) * rows, (2 * slot + whose + 1) * rows)
            column = (at_ref[0] if side == 0 else 1 - at_ref[0]) * half
            columns = pl.ds(pl.multiple_of(column, half), half)
            held[place, columns] = gate[slot * rows : (slot + 1) * rows]
    wide = weights[0].shape[1]
    leaving = []
    for index, weight in enumerate(weights):
        copies[index].wait()
        at = slice(index * wide, (index + 1) * wide)
        ready[:, at] = dot(held[...], weight[...]).astype(BF16)
        leaving.append(pltpu.make_async_copy(ready.at[:, at], out_ref.at[:, at], out_sems.at[index]))
        leaving[-1].start()
    for copy in leaving:
        copy.wait()


def near_terms(n_tp, place, gates, weights):
    length, half = gates[0].shape
    shape = (2 * length, len(weights) * weights[0].shape[1])
    anywhere = pl.BlockSpec(memory_space=pl.ANY)
    return pl.pallas_call(
        functools.partial(near_kernel, n_tp),
        out_shape=jax.ShapeDtypeStruct(shape, BF16),
        in_specs=[pl.BlockSpec(memory_space=pltpu.SMEM)]
        + [WHOLE] * 4
        + [anywhere] * len(weights),
        out_specs=anywhere,
        scratch_shapes=[pltpu.VMEM((2 * length, 2 * half), BF16)]
        + [pltpu.VMEM(weight.shape, BF16) for weight in weights]
        + [pltpu.VMEM(shape, BF16)]
        + [pltpu.SemaphoreType.DMA((len(weights),))] * 2,
        compiler_params=pltpu.CompilerParams(vmem_limit_bytes=24 << 20),
        cost_estimate=pl.CostEstimate(flops=1, bytes_accessed=1, transcendentals=0),
    )(place, *gates, *weights)


def on_device(tokens, norm_gain, in_weight, filters, out_weight, keep_mask):
    n_seq, n_tp = lax.axis_size("seq"), lax.axis_size("tp")
    chips = n_seq // 2
    ny, nx = grid_of(chips)
    seq = lax.axis_index("seq")
    core, here = seq % 2, seq // 2
    my_y, my_x = here // nx, here % nx
    rows, model = tokens.shape
    length = rows * n_tp
    deep, channels = in_weight.shape[1:]
    half = channels // 2
    wide = out_weight.shape[1]

    def place(y, x, c):
        return ((y % ny) * nx + x % nx) * 2 + c

    def from_chip(block, dy, dx):
        route = [
            (place(y + dy, x + dx, c), place(y, x, c))
            for y in range(ny)
            for x in range(nx)
            for c in range(2)
        ]
        return lax.ppermute(block, "seq", route)

    def from_partner(block):
        return lax.ppermute(block, "seq", [(s, s ^ 1) for s in range(n_seq)])

    def direct(mine, brought):
        along_x = [(mine, brought)]
        along_y = [(mine, brought)]
        along_x += [tuple(from_chip(b, 0, dx) for b in (mine, brought)) for dx in range(1, nx)]
        along_y += [tuple(from_chip(b, dy, 0) for b in (mine, brought)) for dy in range(1, ny)]
        return along_x, along_y

    def onward(along_x, along_y):
        return {
            (dy, dx): (from_chip(along_x[dx][0], dy, 0), from_chip(along_y[dy][1], 0, dx))
            for dy in range(1, ny)
            for dx in range(1, nx)
        }

    def crossed(along_x, along_y):
        return {
            (dy, dx): (from_chip(along_x[0, dx][0], dy, 0), from_chip(along_y[dy, 0][1], 0, dx))
            for dy, _ in along_y
            for _, dx in along_x
        }

    def listed(along_x, along_y, rest):
        found = {(0, dx): pair for dx, pair in enumerate(along_x)}
        found.update({(dy, 0): pair for dy, pair in enumerate(along_y)})
        found.update(rest)
        return found

    def by_core(mine, other, axis):
        return jnp.where(
            core == 0,
            jnp.concatenate([mine, other], axis=axis),
            jnp.concatenate([other, mine], axis=axis),
        )

    def columns(array, first, count, at):
        return lax.dynamic_slice(array, (first, 0, at * half), (count, deep, half))

    mine_kv = columns(in_weight, 1, 2, core)
    away_kv = columns(in_weight, 1, 2, 1 - core)
    brought_kv = from_partner(away_kv)
    kv_x, kv_y = direct(mine_kv, brought_kv)

    tokens_then, _ = lax.optimization_barrier((tokens, away_kv))
    widened = tokens_then.astype(F32)
    mean_sq = jnp.mean(widened * widened, axis=1, keepdims=True)
    normed = (widened * lax.rsqrt(mean_sq + 1e-06) * norm_gain).astype(BF16)
    own_rows = lax.all_gather(normed, "tp", axis=0, tiled=True)
    in_weight_then, _ = lax.optimization_barrier((in_weight, normed))
    mine_q = columns(in_weight_then, 0, 1, core)[0]
    both_q = jnp.stack([mine_q, from_partner(columns(in_weight_then, 0, 1, 1 - core)[0])])

    kv_x, kv_y, both_q = lax.optimization_barrier((kv_x, kv_y, both_q))
    kv_rest = onward(kv_x, kv_y)
    q_x = {(0, dx): from_chip(both_q, 0, dx) for dx in range(1, nx)}
    q_y = {(dy, 0): from_chip(both_q, dy, 0) for dy in range(1, ny)}
    arrived = (kv_x, kv_y, kv_rest)
    own_rows, arrived = lax.optimization_barrier((own_rows, arrived))
    kv_x, kv_y, kv_rest = arrived
    kv = listed(kv_x, kv_y, kv_rest)
    order = list(kv)
    kv_pieces = [piece for key in order for piece in kv[key]]
    at = jnp.stack(
        [place(my_y + dy, my_x + dx, core ^ rc) * deep for dy, dx in order for rc in range(2)]
    ).astype(jnp.int32)
    early = 2 * (ny + nx - 1)

    (own_product,) = products(at, [own_rows], kv_pieces)
    reach = filters.shape[0] - 1
    pad = -(-reach // 16) * 16
    ends = [
        lax.ppermute(own_rows[length - pad :], "seq", [(2 * i + 1, 2 * i + 2 + c) for i in range(chips - 1)])
        for c in range(2)
    ]
    before = jnp.where(core == 0, ends[0], ends[1])
    ready = (own_rows, q_x, q_y, own_product, before)
    rows_then, q_x, q_y, own_product, before = lax.optimization_barrier(ready)
    other_rows = from_partner(rows_then)
    q_rest = crossed(q_x, q_y)
    q_pairs = {(0, 0): both_q, **q_x, **q_y}
    q_early = [q_pairs[key] for key in order if key in q_pairs]
    own_query = project(query_kernel, at, [own_rows], [], q_early, F32)
    other_rows, own_query = lax.optimization_barrier((other_rows, own_query))
    rim, other_product = products(at, [before, other_rows], kv_pieces)
    own_tail, other_tail = own_product[length - pad :], other_product[length - pad :]
    first_tail = jnp.where(core == 0, own_tail, other_tail)
    groups = filters.shape[1] // 2
    taps = jnp.repeat(
        lax.dynamic_slice_in_dim(filters, core * groups, groups, axis=1), half // groups, axis=1
    )
    own_filtered = causal_filter(at, own_product, jnp.where(core == 0, rim, first_tail), taps)
    other_filtered = causal_filter(at, other_product, jnp.where(core == 0, first_tail, rim), taps)

    other_rows, own_filtered, other_filtered = lax.optimization_barrier(
        (other_rows, own_filtered, other_filtered)
    )
    other_query = project(query_kernel, at, [other_rows], [], q_early, F32)
    weight_then, q_x, q_y = lax.optimization_barrier((out_weight, q_x, q_y))
    o_x = {(0, dx): from_chip(weight_then, 0, dx) for dx in range(1, nx)}
    o_y = {(dy, 0): from_chip(weight_then, dy, 0) for dy in range(1, ny)}
    o_rest = {
        (dy, dx): (
            from_chip(o_x[0, dx][:half], dy, 0),
            from_chip(o_y[dy, 0][half:], 0, dx),
        )
        for dy in range(1, ny)
        for dx in range(1, nx)
    }
    late = [piece for pair in q_rest.values() for piece in pair]
    other_gated = project(
        gate_kernel, at[early:], [other_rows], [other_filtered, other_query], late, BF16
    )
    own_gated = project(
        gate_kernel, at[early:], [own_rows], [own_filtered, own_query], late, BF16
    )
    gates = (own_gated, from_partner(other_gated), other_gated, from_partner(own_gated))

    position = lax.axis_index("tp")
    here_at = jnp.stack([core, position]).astype(jnp.int32)
    up = [(i, i + 1) for i in range(n_tp - 1)]
    down = [(i + 1, i) for i in range(n_tp - 1)]

    def plus(a, b):
        return (a.astype(F32) + b.astype(F32)).astype(BF16)

    def chained(slots):
        rising = falling = None
        for step in range(n_tp - 1):
            send_up, send_down = slots[n_tp - 1 - step], slots[step + 1]
            if step:
                send_up, send_down = plus(send_up, rising), plus(send_down, falling)
            rising = lax.ppermute(send_up, "tp", up)
            falling = lax.ppermute(send_down, "tp", down)
        total = slots[0].astype(F32) + rising.astype(F32) + falling.astype(F32)
        return total

    near = {(0, 0): (out_weight,)}
    near.update({key: (block,) for key, block in (*o_x.items(), *o_y.items())})
    found = near_terms(n_tp, here_at, gates, [block for (block,) in near.values()])
    gates, found = lax.optimization_barrier((gates, found))
    near_sum = lax.psum_scatter(found, "tp", scatter_dimension=0, tiled=True)
    far_sum = chained(terms(n_tp, here_at, gates, list(o_rest.values()), True))
    result = jnp.zeros((rows, model), BF16)
    far_theirs = from_partner(far_sum[rows:].astype(BF16))
    near_sum, far_theirs, far_sum = lax.optimization_barrier((near_sum, far_theirs, far_sum))
    near_theirs = from_partner(near_sum[rows:].astype(BF16))
    parts = (list(o_rest), far_sum, far_theirs), (list(near), near_sum, near_theirs)
    for keys, mixed, theirs in parts:
        theirs = theirs.astype(F32)
        mine = mixed[:rows].astype(F32)
        for index, (dy, dx) in enumerate(keys):
            start = place(my_y + dy, my_x + dx, 0) * wide
            here_columns = slice(index * wide, (index + 1) * wide)
            pair = by_core(mine[:, here_columns], theirs[:, here_columns], 1)
            kept = lax.dynamic_slice_in_dim(keep_mask, start, 2 * wide, axis=1).astype(F32)
            base = lax.dynamic_slice_in_dim(tokens, start, 2 * wide, axis=1).astype(F32)
            part = (base + kept * pair * (1.0 / 0.9)).astype(BF16)
            result = lax.dynamic_update_slice_in_dim(result, part, start, axis=1)
    return result


def solution(mesh):
    in_specs = (
        P(("seq", "tp"), None),
        P(),
        P(None, "seq", "tp"),
        P(None, "tp"),
        P("tp", "seq"),
        P(("seq", "tp"), None),
    )
    out_specs = P(("seq", "tp"), None)
    return jax.shard_map(
        on_device, mesh=mesh, in_specs=in_specs, out_specs=out_specs, check_vma=False
    )
```

```python
import functools
import math

import jax
import jax.numpy as jnp
from jax import lax
from jax.experimental import pallas as pl
from jax.experimental.pallas import tpu as pltpu
from jax.sharding import PartitionSpec as P

F32 = jnp.float32
BF16 = jnp.bfloat16
GRANT = 12 << 20
WHOLE = pl.BlockSpec(memory_space=pltpu.VMEM)


def grid_of(chips):
    ny = max(d for d in range(1, math.isqrt(chips) + 1) if chips % d == 0)
    return ny, chips // ny


def dot(a, b):
    return jnp.dot(a, b, preferred_element_type=F32)


def columns_of(x_ref, at_ref, index, deep):
    return x_ref[:, pl.ds(pl.multiple_of(at_ref[index], deep), deep)]


def tiles_of(out_ref):
    tile = math.gcd(out_ref.shape[1], 256)
    return [slice(at, at + tile) for at in range(0, out_ref.shape[1], tile)]


def blocks_of(xs, out_ref):
    tile = math.gcd(out_ref.shape[1], 256)
    size = xs[0].shape[0]
    for at in range(0, out_ref.shape[1], tile):
        for index, x_ref in enumerate(xs):
            yield x_ref, slice(index * size, (index + 1) * size), slice(at, at + tile)


def query_kernel(parts, at_ref, *refs):
    xs, pairs, out_ref = refs[:parts], refs[parts:-1], refs[-1]
    deep = pairs[0].shape[1]
    for x_ref, rows, tile in blocks_of(xs, out_ref):
        query = None
        for index in range(2 * len(pairs)):
            x = columns_of(x_ref, at_ref, index, deep)
            new = dot(x, pairs[index // 2][index % 2, :, tile])
            query = new if query is None else query + new
        out_ref[rows, tile] = query


def gate_kernel(parts, at_ref, *refs):
    xs, refs = refs[:parts], refs[parts:]
    filtered_ref, partial_ref, pieces, out_ref = refs[0], refs[1], refs[2:-1], refs[-1]
    deep = pieces[0].shape[0]
    for x_ref, rows, tile in blocks_of(xs, out_ref):
        query = partial_ref[rows, tile]
        for index, piece in enumerate(pieces):
            query = query + dot(columns_of(x_ref, at_ref, index, deep), piece[:, tile])
        gated = query.astype(BF16).astype(F32) * filtered_ref[rows, tile]
        out_ref[rows, tile] = gated.astype(BF16)


def call(kernel, scalars, operands, out, scratch=()):
    return pl.pallas_call(
        kernel,
        out_shape=out,
        in_specs=[pl.BlockSpec(memory_space=pltpu.SMEM)] + [WHOLE] * len(operands),
        out_specs=jax.tree.map(lambda _: WHOLE, out),
        scratch_shapes=scratch,
        compiler_params=pltpu.CompilerParams(vmem_limit_bytes=GRANT),
        cost_estimate=pl.CostEstimate(flops=1, bytes_accessed=1, transcendentals=0),
    )(scalars, *operands)


def project(kernel, at, xs, extra, pieces, out_dtype):
    rows = sum(x.shape[0] for x in xs)
    out = jax.ShapeDtypeStruct((rows, pieces[0].shape[-1]), out_dtype)
    return call(functools.partial(kernel, len(xs)), at, (*xs, *extra, *pieces), out)


def product_kernel(parts, count, at_ref, *refs):
    xs, refs = refs[:parts], refs[parts:]
    given, refs = refs[:count], refs[count:]
    outs, (joined, *pieces, sems) = refs[:parts], refs[parts:]
    ends = [0]
    for x_ref in xs:
        ends.append(ends[-1] + x_ref.shape[0])
    targets = [joined.at[low:high] for low, high in zip(ends, ends[1:])] + list(pieces)
    copies = [
        pltpu.make_async_copy(source, target, sems.at[index])
        for index, (source, target) in enumerate(zip((*xs, *given), targets))
    ]
    for copy in copies:
        copy.start()
    for copy in copies[:parts]:
        copy.wait()
    deep = pieces[0].shape[1]
    half = pieces[0].shape[2]
    tile = math.gcd(half, 256)
    for low in range(0, half, tile):
        columns = slice(low, low + tile)
        key = value = None
        for index, piece in enumerate(pieces):
            if low == 0:
                copies[parts + index].wait()
            x = columns_of(joined, at_ref, index, deep)
            new_key, new_value = dot(x, piece[0, :, columns]), dot(x, piece[1, :, columns])
            key = new_key if key is None else key + new_key
            value = new_value if value is None else value + new_value
        product = key.astype(BF16).astype(F32) * value.astype(BF16).astype(F32)
        for out, start, end in zip(outs, ends, ends[1:]):
            out[:, columns] = product[start:end]


def products(at, xs, pieces):
    half = pieces[0].shape[2]
    held = [pltpu.VMEM((sum(x.shape[0] for x in xs), xs[0].shape[1]), BF16)]
    held += [pltpu.VMEM(piece.shape, BF16) for piece in pieces]
    held.append(pltpu.SemaphoreType.DMA((len(xs) + len(pieces),)))
    return pl.pallas_call(
        functools.partial(product_kernel, len(xs), len(pieces)),
        out_shape=[jax.ShapeDtypeStruct((x.shape[0], half), F32) for x in xs],
        in_specs=[pl.BlockSpec(memory_space=pltpu.SMEM)]
        + [pl.BlockSpec(memory_space=pl.ANY)] * (len(xs) + len(pieces)),
        out_specs=[WHOLE] * len(xs),
        scratch_shapes=held,
        compiler_params=pltpu.CompilerParams(vmem_limit_bytes=56 << 20),
        cost_estimate=pl.CostEstimate(flops=1, bytes_accessed=1, transcendentals=0),
    )(at, *xs, *pieces)


def filter_kernel(_, product_ref, halo_ref, taps_ref, out_ref, held):
    length, pad = product_ref.shape[0], halo_ref.shape[0]
    held[:pad] = halo_ref[...]
    held[pad:] = product_ref[...]
    for tile in tiles_of(out_ref):
        total = None
        for offset in range(taps_ref.shape[0]):
            term = taps_ref[offset : offset + 1, tile] * held[pad - offset : pad - offset + length, tile]
            total = term if total is None else total + term
        out_ref[:, tile] = total


def causal_filter(at, product, halo, taps):
    length, half = product.shape
    out = jax.ShapeDtypeStruct(product.shape, F32)
    scratch = [pltpu.VMEM((halo.shape[0] + length, half), F32)]
    return call(filter_kernel, at, (product, halo, taps), out, scratch)


def terms_kernel(plan, turned, n_tp, at_ref, *refs):
    gates, refs, held = refs[:4], refs[4:-1], refs[-1]
    count = sum(len(parts) for parts in plan)
    weights, outs = refs[:count], refs[count:]
    half = gates[0].shape[1]
    rows = gates[0].shape[0] // n_tp
    for slot in range(n_tp):
        for index, gate in enumerate(gates):
            side, whose = index % 2, index // 2
            place = slice((2 * slot + whose) * rows, (2 * slot + whose + 1) * rows)
            owner = lax.rem(at_ref[1] + slot, n_tp) * rows if turned else slot * rows
            column = (at_ref[0] if side == 0 else 1 - at_ref[0]) * half
            taken = gate[pl.ds(pl.multiple_of(owner, rows), rows)]
            held[place, pl.ds(pl.multiple_of(column, half), half)] = taken
    wide = weights[0].shape[1]
    share = held.shape[0] // len(outs)
    used = 0
    for index, parts in enumerate(plan):
        at = slice(index * wide, (index + 1) * wide)
        for piece in range(0, held.shape[0], share):
            total, depth = None, 0
            for which in range(len(parts)):
                weight = weights[used + which]
                low, depth = depth, depth + weight.shape[0]
                new = dot(held[piece : piece + share, low:depth], weight[...])
                total = new if total is None else total + new
            outs[piece // share][:, at] = total.astype(BF16)
        used += len(parts)


def terms(n_tp, place, gates, blocks, turned):
    length, half = gates[0].shape
    weights = [part for parts in blocks for part in parts]
    cols = len(blocks) * weights[0].shape[1]
    slots = n_tp if turned else 1
    out = [jax.ShapeDtypeStruct((2 * length // slots, cols), BF16)] * slots
    kernel = functools.partial(terms_kernel, blocks_plan(blocks), turned, n_tp)
    scratch = [pltpu.VMEM((2 * length, 2 * half), BF16)]
    result = call(kernel, place, (*gates, *weights), out, scratch)
    return result if turned else result[0]


def blocks_plan(blocks):
    return [range(len(parts)) for parts in blocks]


def near_kernel(n_tp, at_ref, *refs):
    gates, refs = refs[:4], refs[4:]
    count = (len(refs) - 4) // 2
    given, (out_ref, held, *refs) = refs[:count], refs[count:]
    weights, (ready, sems, out_sems) = refs[:count], refs[count:]
    copies = [
        pltpu.make_async_copy(source, target, sems.at[index])
        for index, (source, target) in enumerate(zip(given, weights))
    ]
    for copy in copies:
        copy.start()
    half = gates[0].shape[1]
    rows = gates[0].shape[0] // n_tp
    for slot in range(n_tp):
        for index, gate in enumerate(gates):
            side, whose = index % 2, index // 2
            place = slice((2 * slot + whose) * rows, (2 * slot + whose + 1) * rows)
            column = (at_ref[0] if side == 0 else 1 - at_ref[0]) * half
            columns = pl.ds(pl.multiple_of(column, half), half)
            held[place, columns] = gate[slot * rows : (slot + 1) * rows]
    wide = weights[0].shape[1]
    leaving = []
    for index, weight in enumerate(weights):
        copies[index].wait()
        at = slice(index * wide, (index + 1) * wide)
        tile = math.gcd(wide, 256)
        for low in range(0, wide, tile):
            total = dot(held[:, :half], weight[:half, low : low + tile])
            total = total + dot(held[:, half:], weight[half:, low : low + tile])
            ready[:, index * wide + low : index * wide + low + tile] = total.astype(BF16)
        leaving.append(pltpu.make_async_copy(ready.at[:, at], out_ref.at[:, at], out_sems.at[index]))
        leaving[-1].start()
    for copy in leaving:
        copy.wait()


def near_terms(n_tp, place, gates, weights):
    length, half = gates[0].shape
    shape = (2 * length, len(weights) * weights[0].shape[1])
    anywhere = pl.BlockSpec(memory_space=pl.ANY)
    return pl.pallas_call(
        functools.partial(near_kernel, n_tp),
        out_shape=jax.ShapeDtypeStruct(shape, BF16),
        in_specs=[pl.BlockSpec(memory_space=pltpu.SMEM)]
        + [WHOLE] * 4
        + [anywhere] * len(weights),
        out_specs=anywhere,
        scratch_shapes=[pltpu.VMEM((2 * length, 2 * half), BF16)]
        + [pltpu.VMEM(weight.shape, BF16) for weight in weights]
        + [pltpu.VMEM(shape, BF16)]
        + [pltpu.SemaphoreType.DMA((len(weights),))] * 2,
        compiler_params=pltpu.CompilerParams(vmem_limit_bytes=24 << 20),
        cost_estimate=pl.CostEstimate(flops=1, bytes_accessed=1, transcendentals=0),
    )(place, *gates, *weights)


def on_device(tokens, norm_gain, in_weight, filters, out_weight, keep_mask):
    n_seq, n_tp = lax.axis_size("seq"), lax.axis_size("tp")
    chips = n_seq // 2
    ny, nx = grid_of(chips)
    seq = lax.axis_index("seq")
    core, here = seq % 2, seq // 2
    my_y, my_x = here // nx, here % nx
    rows, model = tokens.shape
    length = rows * n_tp
    deep, channels = in_weight.shape[1:]
    half = channels // 2
    wide = out_weight.shape[1]

    def place(y, x, c):
        return ((y % ny) * nx + x % nx) * 2 + c

    def from_chip(block, dy, dx):
        route = [
            (place(y + dy, x + dx, c), place(y, x, c))
            for y in range(ny)
            for x in range(nx)
            for c in range(2)
        ]
        return lax.ppermute(block, "seq", route)

    def from_partner(block):
        return lax.ppermute(block, "seq", [(s, s ^ 1) for s in range(n_seq)])

    def direct(mine, brought):
        along_x = [(mine, brought)]
        along_y = [(mine, brought)]
        along_x += [tuple(from_chip(b, 0, dx) for b in (mine, brought)) for dx in range(1, nx)]
        along_y += [tuple(from_chip(b, dy, 0) for b in (mine, brought)) for dy in range(1, ny)]
        return along_x, along_y

    def onward(along_x, along_y):
        return {
            (dy, dx): (from_chip(along_x[dx][0], dy, 0), from_chip(along_y[dy][1], 0, dx))
            for dy in range(1, ny)
            for dx in range(1, nx)
        }

    def crossed(along_x, along_y):
        return {
            (dy, dx): (from_chip(along_x[0, dx][0], dy, 0), from_chip(along_y[dy, 0][1], 0, dx))
            for dy, _ in along_y
            for _, dx in along_x
        }

    def listed(along_x, along_y, rest):
        found = {(0, dx): pair for dx, pair in enumerate(along_x)}
        found.update({(dy, 0): pair for dy, pair in enumerate(along_y)})
        found.update(rest)
        return found

    def by_core(mine, other, axis):
        return jnp.where(
            core == 0,
            jnp.concatenate([mine, other], axis=axis),
            jnp.concatenate([other, mine], axis=axis),
        )

    def columns(array, first, count, at):
        return lax.dynamic_slice(array, (first, 0, at * half), (count, deep, half))

    mine_kv = columns(in_weight, 1, 2, core)
    away_kv = columns(in_weight, 1, 2, 1 - core)
    brought_kv = from_partner(away_kv)
    kv_x, kv_y = direct(mine_kv, brought_kv)

    tokens_then, _ = lax.optimization_barrier((tokens, away_kv))
    widened = tokens_then.astype(F32)
    mean_sq = jnp.mean(widened * widened, axis=1, keepdims=True)
    normed = (widened * lax.rsqrt(mean_sq + 1e-06) * norm_gain).astype(BF16)
    own_rows = lax.all_gather(normed, "tp", axis=0, tiled=True)
    in_weight_then, _ = lax.optimization_barrier((in_weight, normed))
    mine_q = columns(in_weight_then, 0, 1, core)[0]
    both_q = jnp.stack([mine_q, from_partner(columns(in_weight_then, 0, 1, 1 - core)[0])])

    kv_x, kv_y, both_q = lax.optimization_barrier((kv_x, kv_y, both_q))
    kv_rest = onward(kv_x, kv_y)
    q_x = {(0, dx): from_chip(both_q, 0, dx) for dx in range(1, nx)}
    q_y = {(dy, 0): from_chip(both_q, dy, 0) for dy in range(1, ny)}
    arrived = (kv_x, kv_y, kv_rest)
    own_rows, arrived = lax.optimization_barrier((own_rows, arrived))
    kv_x, kv_y, kv_rest = arrived
    kv = listed(kv_x, kv_y, kv_rest)
    order = list(kv)
    kv_pieces = [piece for key in order for piece in kv[key]]
    at = jnp.stack(
        [place(my_y + dy, my_x + dx, core ^ rc) * deep for dy, dx in order for rc in range(2)]
    ).astype(jnp.int32)
    early = 2 * (ny + nx - 1)

    (own_product,) = products(at, [own_rows], kv_pieces)
    reach = filters.shape[0] - 1
    pad = -(-reach // 16) * 16
    ends = [
        lax.ppermute(own_rows[length - pad :], "seq", [(2 * i + 1, 2 * i + 2 + c) for i in range(chips - 1)])
        for c in range(2)
    ]
    before = jnp.where(core == 0, ends[0], ends[1])
    ready = (own_rows, q_x, q_y, own_product, before)
    rows_then, q_x, q_y, own_product, before = lax.optimization_barrier(ready)
    other_rows = from_partner(rows_then)
    q_rest = crossed(q_x, q_y)
    q_pairs = {(0, 0): both_q, **q_x, **q_y}
    q_early = [q_pairs[key] for key in order if key in q_pairs]
    own_query = project(query_kernel, at, [own_rows], [], q_early, F32)
    other_rows, own_query = lax.optimization_barrier((other_rows, own_query))
    rim, other_product = products(at, [before, other_rows], kv_pieces)
    own_tail, other_tail = own_product[length - pad :], other_product[length - pad :]
    first_tail = jnp.where(core == 0, own_tail, other_tail)
    groups = filters.shape[1] // 2
    taps = jnp.repeat(
        lax.dynamic_slice_in_dim(filters, core * groups, groups, axis=1), half // groups, axis=1
    )
    own_filtered = causal_filter(at, own_product, jnp.where(core == 0, rim, first_tail), taps)
    other_filtered = causal_filter(at, other_product, jnp.where(core == 0, first_tail, rim), taps)

    other_rows, own_filtered, other_filtered = lax.optimization_barrier(
        (other_rows, own_filtered, other_filtered)
    )
    other_query = project(query_kernel, at, [other_rows], [], q_early, F32)
    weight_then, q_x, q_y = lax.optimization_barrier((out_weight, q_x, q_y))
    o_x = {(0, dx): from_chip(weight_then, 0, dx) for dx in range(1, nx)}
    o_y = {(dy, 0): from_chip(weight_then, dy, 0) for dy in range(1, ny)}
    o_rest = {
        (dy, dx): (
            from_chip(o_x[0, dx][:half], dy, 0),
            from_chip(o_y[dy, 0][half:], 0, dx),
        )
        for dy in range(1, ny)
        for dx in range(1, nx)
    }
    late = [piece for pair in q_rest.values() for piece in pair]
    other_gated = project(
        gate_kernel, at[early:], [other_rows], [other_filtered, other_query], late, BF16
    )
    own_gated = project(
        gate_kernel, at[early:], [own_rows], [own_filtered, own_query], late, BF16
    )
    gates = (own_gated, from_partner(other_gated), other_gated, from_partner(own_gated))

    position = lax.axis_index("tp")
    here_at = jnp.stack([core, position]).astype(jnp.int32)
    up = [(i, i + 1) for i in range(n_tp - 1)]
    down = [(i + 1, i) for i in range(n_tp - 1)]

    def plus(a, b):
        return (a.astype(F32) + b.astype(F32)).astype(BF16)

    def chained(slots):
        rising = falling = None
        for step in range(n_tp - 1):
            send_up, send_down = slots[n_tp - 1 - step], slots[step + 1]
            if step:
                send_up, send_down = plus(send_up, rising), plus(send_down, falling)
            rising = lax.ppermute(send_up, "tp", up)
            falling = lax.ppermute(send_down, "tp", down)
        total = slots[0].astype(F32) + rising.astype(F32) + falling.astype(F32)
        return total

    near = {(0, 0): (out_weight,)}
    near.update({key: (block,) for key, block in (*o_x.items(), *o_y.items())})
    found = near_terms(n_tp, here_at, gates, [block for (block,) in near.values()])
    gates, found = lax.optimization_barrier((gates, found))
    near_sum = lax.psum_scatter(found, "tp", scatter_dimension=0, tiled=True)
    far_sum = chained(terms(n_tp, here_at, gates, list(o_rest.values()), True))
    result = jnp.zeros((rows, model), BF16)
    far_theirs = from_partner(far_sum[rows:].astype(BF16))
    near_sum, far_theirs, far_sum = lax.optimization_barrier((near_sum, far_theirs, far_sum))
    near_theirs = from_partner(near_sum[rows:].astype(BF16))
    parts = (list(o_rest), far_sum, far_theirs), (list(near), near_sum, near_theirs)
    for keys, mixed, theirs in parts:
        theirs = theirs.astype(F32)
        mine = mixed[:rows].astype(F32)
        for index, (dy, dx) in enumerate(keys):
            start = place(my_y + dy, my_x + dx, 0) * wide
            here_columns = slice(index * wide, (index + 1) * wide)
            pair = by_core(mine[:, here_columns], theirs[:, here_columns], 1)
            kept = lax.dynamic_slice_in_dim(keep_mask, start, 2 * wide, axis=1).astype(F32)
            base = lax.dynamic_slice_in_dim(tokens, start, 2 * wide, axis=1).astype(F32)
            part = (base + kept * pair * (1.0 / 0.9)).astype(BF16)
            result = lax.dynamic_update_slice_in_dim(result, part, start, axis=1)
    return result


def solution(mesh):
    in_specs = (
        P(("seq", "tp"), None),
        P(),
        P(None, "seq", "tp"),
        P(None, "tp"),
        P("tp", "seq"),
        P(("seq", "tp"), None),
    )
    out_specs = P(("seq", "tp"), None)
    return jax.shard_map(
        on_device, mesh=mesh, in_specs=in_specs, out_specs=out_specs, check_vma=False
    )
```

```python
import functools
import math

import jax
import jax.numpy as jnp
from jax import lax
from jax.experimental import pallas as pl
from jax.experimental.pallas import tpu as pltpu
from jax.sharding import PartitionSpec as P

F32 = jnp.float32
BF16 = jnp.bfloat16
GRANT = 12 << 20
WHOLE = pl.BlockSpec(memory_space=pltpu.VMEM)


def grid_of(chips):
    ny = max(d for d in range(1, math.isqrt(chips) + 1) if chips % d == 0)
    return ny, chips // ny


def dot(a, b):
    return jnp.dot(a, b, preferred_element_type=F32)


def columns_of(x_ref, at_ref, index, deep):
    return x_ref[:, pl.ds(pl.multiple_of(at_ref[index], deep), deep)]


def tiles_of(out_ref):
    tile = math.gcd(out_ref.shape[1], 256)
    return [slice(at, at + tile) for at in range(0, out_ref.shape[1], tile)]


def blocks_of(xs, out_ref):
    tile = math.gcd(out_ref.shape[1], 256)
    size = xs[0].shape[0]
    for at in range(0, out_ref.shape[1], tile):
        for index, x_ref in enumerate(xs):
            yield x_ref, slice(index * size, (index + 1) * size), slice(at, at + tile)


def query_kernel(parts, at_ref, *refs):
    xs, pairs, out_ref = refs[:parts], refs[parts:-1], refs[-1]
    deep = pairs[0].shape[1]
    for x_ref, rows, tile in blocks_of(xs, out_ref):
        query = None
        for index in range(2 * len(pairs)):
            x = columns_of(x_ref, at_ref, index, deep)
            new = dot(x, pairs[index // 2][index % 2, :, tile])
            query = new if query is None else query + new
        out_ref[rows, tile] = query


def gate_kernel(parts, at_ref, *refs):
    xs, refs = refs[:parts], refs[parts:]
    filtered_ref, partial_ref, pieces, out_ref = refs[0], refs[1], refs[2:-1], refs[-1]
    deep = pieces[0].shape[0]
    for x_ref, rows, tile in blocks_of(xs, out_ref):
        query = partial_ref[rows, tile]
        for index, piece in enumerate(pieces):
            query = query + dot(columns_of(x_ref, at_ref, index, deep), piece[:, tile])
        gated = query.astype(BF16).astype(F32) * filtered_ref[rows, tile]
        out_ref[rows, tile] = gated.astype(BF16)


def call(kernel, scalars, operands, out, scratch=()):
    return pl.pallas_call(
        kernel,
        out_shape=out,
        in_specs=[pl.BlockSpec(memory_space=pltpu.SMEM)] + [WHOLE] * len(operands),
        out_specs=jax.tree.map(lambda _: WHOLE, out),
        scratch_shapes=scratch,
        compiler_params=pltpu.CompilerParams(vmem_limit_bytes=GRANT),
        cost_estimate=pl.CostEstimate(flops=1, bytes_accessed=1, transcendentals=0),
    )(scalars, *operands)


def project(kernel, at, xs, extra, pieces, out_dtype):
    rows = sum(x.shape[0] for x in xs)
    out = jax.ShapeDtypeStruct((rows, pieces[0].shape[-1]), out_dtype)
    return call(functools.partial(kernel, len(xs)), at, (*xs, *extra, *pieces), out)


def product_kernel(parts, count, at_ref, *refs):
    xs, refs = refs[:parts], refs[parts:]
    given, refs = refs[:count], refs[count:]
    outs, (joined, *pieces, sems) = refs[:parts], refs[parts:]
    ends = [0]
    for x_ref in xs:
        ends.append(ends[-1] + x_ref.shape[0])
    targets = [joined.at[low:high] for low, high in zip(ends, ends[1:])] + list(pieces)
    copies = [
        pltpu.make_async_copy(source, target, sems.at[index])
        for index, (source, target) in enumerate(zip((*xs, *given), targets))
    ]
    for copy in copies:
        copy.start()
    for copy in copies[:parts]:
        copy.wait()
    deep = pieces[0].shape[1]
    half = pieces[0].shape[2]
    tile = math.gcd(half, 256)
    for low in range(0, half, tile):
        columns = slice(low, low + tile)
        key = value = None
        for index, piece in enumerate(pieces):
            if low == 0:
                copies[parts + index].wait()
            x = columns_of(joined, at_ref, index, deep)
            new_key, new_value = dot(x, piece[0, :, columns]), dot(x, piece[1, :, columns])
            key = new_key if key is None else key + new_key
            value = new_value if value is None else value + new_value
        product = key.astype(BF16).astype(F32) * value.astype(BF16).astype(F32)
        for out, start, end in zip(outs, ends, ends[1:]):
            out[:, columns] = product[start:end]


def products(at, xs, pieces):
    half = pieces[0].shape[2]
    held = [pltpu.VMEM((sum(x.shape[0] for x in xs), xs[0].shape[1]), BF16)]
    held += [pltpu.VMEM(piece.shape, BF16) for piece in pieces]
    held.append(pltpu.SemaphoreType.DMA((len(xs) + len(pieces),)))
    return pl.pallas_call(
        functools.partial(product_kernel, len(xs), len(pieces)),
        out_shape=[jax.ShapeDtypeStruct((x.shape[0], half), F32) for x in xs],
        in_specs=[pl.BlockSpec(memory_space=pltpu.SMEM)]
        + [pl.BlockSpec(memory_space=pl.ANY)] * (len(xs) + len(pieces)),
        out_specs=[WHOLE] * len(xs),
        scratch_shapes=held,
        compiler_params=pltpu.CompilerParams(vmem_limit_bytes=56 << 20),
        cost_estimate=pl.CostEstimate(flops=1, bytes_accessed=1, transcendentals=0),
    )(at, *xs, *pieces)


def filter_kernel(_, product_ref, halo_ref, taps_ref, out_ref, held):
    length, pad = product_ref.shape[0], halo_ref.shape[0]
    held[:pad] = halo_ref[...]
    held[pad:] = product_ref[...]
    for tile in tiles_of(out_ref):
        total = None
        for offset in range(taps_ref.shape[0]):
            term = taps_ref[offset : offset + 1, tile] * held[pad - offset : pad - offset + length, tile]
            total = term if total is None else total + term
        out_ref[:, tile] = total


def causal_filter(at, product, halo, taps):
    length, half = product.shape
    out = jax.ShapeDtypeStruct(product.shape, F32)
    scratch = [pltpu.VMEM((halo.shape[0] + length, half), F32)]
    return call(filter_kernel, at, (product, halo, taps), out, scratch)


def terms_kernel(plan, turned, n_tp, at_ref, *refs):
    gates, refs, held = refs[:4], refs[4:-1], refs[-1]
    count = sum(len(parts) for parts in plan)
    weights, outs = refs[:count], refs[count:]
    half = gates[0].shape[1]
    rows = gates[0].shape[0] // n_tp
    for slot in range(n_tp):
        for index, gate in enumerate(gates):
            side, whose = index % 2, index // 2
            place = slice((2 * slot + whose) * rows, (2 * slot + whose + 1) * rows)
            owner = lax.rem(at_ref[1] + slot, n_tp) * rows if turned else slot * rows
            column = (at_ref[0] if side == 0 else 1 - at_ref[0]) * half
            taken = gate[pl.ds(pl.multiple_of(owner, rows), rows)]
            held[place, pl.ds(pl.multiple_of(column, half), half)] = taken
    wide = weights[0].shape[1]
    share = held.shape[0] // len(outs)
    used = 0
    for index, parts in enumerate(plan):
        at = slice(index * wide, (index + 1) * wide)
        for piece in range(0, held.shape[0], share):
            total, depth = None, 0
            for which in range(len(parts)):
                weight = weights[used + which]
                low, depth = depth, depth + weight.shape[0]
                new = dot(held[piece : piece + share, low:depth], weight[...])
                total = new if total is None else total + new
            outs[piece // share][:, at] = total.astype(BF16)
        used += len(parts)


def terms(n_tp, place, gates, blocks, turned):
    length, half = gates[0].shape
    weights = [part for parts in blocks for part in parts]
    cols = len(blocks) * weights[0].shape[1]
    slots = n_tp if turned else 1
    out = [jax.ShapeDtypeStruct((2 * length // slots, cols), BF16)] * slots
    kernel = functools.partial(terms_kernel, blocks_plan(blocks), turned, n_tp)
    scratch = [pltpu.VMEM((2 * length, 2 * half), BF16)]
    result = call(kernel, place, (*gates, *weights), out, scratch)
    return result if turned else result[0]


def blocks_plan(blocks):
    return [range(len(parts)) for parts in blocks]


def near_kernel(n_tp, at_ref, *refs):
    gates, refs = refs[:4], refs[4:]
    count = (len(refs) - 4) // 2
    given, (out_ref, held, *refs) = refs[:count], refs[count:]
    weights, (ready, sems, out_sems) = refs[:count], refs[count:]
    copies = [
        pltpu.make_async_copy(source, target, sems.at[index])
        for index, (source, target) in enumerate(zip(given, weights))
    ]
    for copy in copies:
        copy.start()
    half = gates[0].shape[1]
    rows = gates[0].shape[0] // n_tp
    for slot in range(n_tp):
        for index, gate in enumerate(gates):
            side, whose = index % 2, index // 2
            place = slice((2 * slot + whose) * rows, (2 * slot + whose + 1) * rows)
            column = (at_ref[0] if side == 0 else 1 - at_ref[0]) * half
            columns = pl.ds(pl.multiple_of(column, half), half)
            held[place, columns] = gate[slot * rows : (slot + 1) * rows]
    wide = weights[0].shape[1]
    leaving = []
    tile = math.gcd(wide, 256)
    for index in range((count + 1) // 2):
        parts = [0] if index == 0 else [2 * index - 1, 2 * index]
        for part in parts:
            copies[part].wait()
        at = slice(index * wide, (index + 1) * wide)
        for low in range(0, wide, tile):
            total, depth = None, 0
            for part in parts:
                size = weights[part].shape[0]
                new = dot(held[:, depth : depth + size], weights[part][:, low : low + tile])
                total, depth = new if total is None else total + new, depth + size
            ready[:, index * wide + low : index * wide + low + tile] = total.astype(BF16)
        leaving.append(pltpu.make_async_copy(ready.at[:, at], out_ref.at[:, at], out_sems.at[index]))
        leaving[-1].start()
    for copy in leaving:
        copy.wait()


def near_terms(n_tp, place, gates, weights):
    length, half = gates[0].shape
    shape = (2 * length, (len(weights) + 1) // 2 * weights[0].shape[1])
    anywhere = pl.BlockSpec(memory_space=pl.ANY)
    return pl.pallas_call(
        functools.partial(near_kernel, n_tp),
        out_shape=jax.ShapeDtypeStruct(shape, BF16),
        in_specs=[pl.BlockSpec(memory_space=pltpu.SMEM)]
        + [WHOLE] * 4
        + [anywhere] * len(weights),
        out_specs=anywhere,
        scratch_shapes=[pltpu.VMEM((2 * length, 2 * half), BF16)]
        + [pltpu.VMEM(weight.shape, BF16) for weight in weights]
        + [pltpu.VMEM(shape, BF16)]
        + [pltpu.SemaphoreType.DMA((len(weights),))] * 2,
        compiler_params=pltpu.CompilerParams(vmem_limit_bytes=24 << 20),
        cost_estimate=pl.CostEstimate(flops=1, bytes_accessed=1, transcendentals=0),
    )(place, *gates, *weights)


def on_device(tokens, norm_gain, in_weight, filters, out_weight, keep_mask):
    n_seq, n_tp = lax.axis_size("seq"), lax.axis_size("tp")
    chips = n_seq // 2
    ny, nx = grid_of(chips)
    seq = lax.axis_index("seq")
    core, here = seq % 2, seq // 2
    my_y, my_x = here // nx, here % nx
    rows, model = tokens.shape
    length = rows * n_tp
    deep, channels = in_weight.shape[1:]
    half = channels // 2
    wide = out_weight.shape[1]

    def place(y, x, c):
        return ((y % ny) * nx + x % nx) * 2 + c

    def from_chip(block, dy, dx):
        route = [
            (place(y + dy, x + dx, c), place(y, x, c))
            for y in range(ny)
            for x in range(nx)
            for c in range(2)
        ]
        return lax.ppermute(block, "seq", route)

    def from_partner(block):
        return lax.ppermute(block, "seq", [(s, s ^ 1) for s in range(n_seq)])

    def direct(mine, brought):
        along_x = [(mine, brought)]
        along_y = [(mine, brought)]
        along_x += [tuple(from_chip(b, 0, dx) for b in (mine, brought)) for dx in range(1, nx)]
        along_y += [tuple(from_chip(b, dy, 0) for b in (mine, brought)) for dy in range(1, ny)]
        return along_x, along_y

    def onward(along_x, along_y):
        return {
            (dy, dx): (from_chip(along_x[dx][0], dy, 0), from_chip(along_y[dy][1], 0, dx))
            for dy in range(1, ny)
            for dx in range(1, nx)
        }

    def crossed(along_x, along_y):
        return {
            (dy, dx): (from_chip(along_x[0, dx][0], dy, 0), from_chip(along_y[dy, 0][1], 0, dx))
            for dy, _ in along_y
            for _, dx in along_x
        }

    def listed(along_x, along_y, rest):
        found = {(0, dx): pair for dx, pair in enumerate(along_x)}
        found.update({(dy, 0): pair for dy, pair in enumerate(along_y)})
        found.update(rest)
        return found

    def by_core(mine, other, axis):
        return jnp.where(
            core == 0,
            jnp.concatenate([mine, other], axis=axis),
            jnp.concatenate([other, mine], axis=axis),
        )

    def columns(array, first, count, at):
        return lax.dynamic_slice(array, (first, 0, at * half), (count, deep, half))

    mine_kv = columns(in_weight, 1, 2, core)
    away_kv = columns(in_weight, 1, 2, 1 - core)
    brought_kv = from_partner(away_kv)
    kv_x, kv_y = direct(mine_kv, brought_kv)

    tokens_then, _ = lax.optimization_barrier((tokens, away_kv))
    widened = tokens_then.astype(F32)
    mean_sq = jnp.mean(widened * widened, axis=1, keepdims=True)
    normed = (widened * lax.rsqrt(mean_sq + 1e-06) * norm_gain).astype(BF16)
    own_rows = lax.all_gather(normed, "tp", axis=0, tiled=True)
    in_weight_then, _ = lax.optimization_barrier((in_weight, normed))
    mine_q = columns(in_weight_then, 0, 1, core)[0]
    both_q = jnp.stack([mine_q, from_partner(columns(in_weight_then, 0, 1, 1 - core)[0])])

    halves = (out_weight[:half], out_weight[half:])
    kv_x, kv_y, both_q, halves = lax.optimization_barrier((kv_x, kv_y, both_q, halves))
    kv_rest = onward(kv_x, kv_y)
    q_x = {(0, dx): from_chip(both_q, 0, dx) for dx in range(1, nx)}
    q_y = {(dy, 0): from_chip(both_q, dy, 0) for dy in range(1, ny)}
    arrived = (kv_x, kv_y, kv_rest)
    own_rows, arrived = lax.optimization_barrier((own_rows, arrived))
    kv_x, kv_y, kv_rest = arrived
    kv = listed(kv_x, kv_y, kv_rest)
    order = list(kv)
    kv_pieces = [piece for key in order for piece in kv[key]]
    at = jnp.stack(
        [place(my_y + dy, my_x + dx, core ^ rc) * deep for dy, dx in order for rc in range(2)]
    ).astype(jnp.int32)
    early = 2 * (ny + nx - 1)

    (own_product,) = products(at, [own_rows], kv_pieces)
    reach = filters.shape[0] - 1
    pad = -(-reach // 16) * 16
    ends = [
        lax.ppermute(own_rows[length - pad :], "seq", [(2 * i + 1, 2 * i + 2 + c) for i in range(chips - 1)])
        for c in range(2)
    ]
    before = jnp.where(core == 0, ends[0], ends[1])
    ready = (own_rows, q_x, q_y, own_product, before)
    rows_then, q_x, q_y, own_product, before = lax.optimization_barrier(ready)
    other_rows = from_partner(rows_then)
    q_rest = crossed(q_x, q_y)
    q_pairs = {(0, 0): both_q, **q_x, **q_y}
    q_early = [q_pairs[key] for key in order if key in q_pairs]
    own_query = project(query_kernel, at, [own_rows], [], q_early, F32)
    other_rows, own_query = lax.optimization_barrier((other_rows, own_query))
    rim, other_product = products(at, [before, other_rows], kv_pieces)
    own_tail, other_tail = own_product[length - pad :], other_product[length - pad :]
    first_tail = jnp.where(core == 0, own_tail, other_tail)
    groups = filters.shape[1] // 2
    taps = jnp.repeat(
        lax.dynamic_slice_in_dim(filters, core * groups, groups, axis=1), half // groups, axis=1
    )
    own_filtered = causal_filter(at, own_product, jnp.where(core == 0, rim, first_tail), taps)
    other_filtered = causal_filter(at, other_product, jnp.where(core == 0, first_tail, rim), taps)

    other_rows, own_filtered, other_filtered = lax.optimization_barrier(
        (other_rows, own_filtered, other_filtered)
    )
    other_query = project(query_kernel, at, [other_rows], [], q_early, F32)
    halves, q_x, q_y = lax.optimization_barrier((halves, q_x, q_y))
    o_x, o_y = direct(*halves)
    o_rest = onward(o_x, o_y)
    o_x = {(0, dx): o_x[dx] for dx in range(1, nx)}
    o_y = {(dy, 0): o_y[dy] for dy in range(1, ny)}
    late = [piece for pair in q_rest.values() for piece in pair]
    other_gated = project(
        gate_kernel, at[early:], [other_rows], [other_filtered, other_query], late, BF16
    )
    own_gated = project(
        gate_kernel, at[early:], [own_rows], [own_filtered, own_query], late, BF16
    )
    gates = (own_gated, from_partner(other_gated), other_gated, from_partner(own_gated))

    position = lax.axis_index("tp")
    here_at = jnp.stack([core, position]).astype(jnp.int32)
    up = [(i, i + 1) for i in range(n_tp - 1)]
    down = [(i + 1, i) for i in range(n_tp - 1)]

    def plus(a, b):
        return (a.astype(F32) + b.astype(F32)).astype(BF16)

    def chained(slots):
        rising = falling = None
        for step in range(n_tp - 1):
            send_up, send_down = slots[n_tp - 1 - step], slots[step + 1]
            if step:
                send_up, send_down = plus(send_up, rising), plus(send_down, falling)
            rising = lax.ppermute(send_up, "tp", up)
            falling = lax.ppermute(send_down, "tp", down)
        total = slots[0].astype(F32) + rising.astype(F32) + falling.astype(F32)
        return total

    near = {(0, 0): (out_weight,)}
    near.update({**o_x, **o_y})
    found = near_terms(n_tp, here_at, gates, [part for parts in near.values() for part in parts])
    gates, found = lax.optimization_barrier((gates, found))
    near_sum = lax.psum_scatter(found, "tp", scatter_dimension=0, tiled=True)
    far_sum = chained(terms(n_tp, here_at, gates, list(o_rest.values()), True))
    result = jnp.zeros((rows, model), BF16)
    far_theirs = from_partner(far_sum[rows:].astype(BF16))
    near_sum, far_theirs, far_sum = lax.optimization_barrier((near_sum, far_theirs, far_sum))
    near_theirs = from_partner(near_sum[rows:].astype(BF16))
    parts = (list(o_rest), far_sum, far_theirs), (list(near), near_sum, near_theirs)
    for keys, mixed, theirs in parts:
        theirs = theirs.astype(F32)
        mine = mixed[:rows].astype(F32)
        for index, (dy, dx) in enumerate(keys):
            start = place(my_y + dy, my_x + dx, 0) * wide
            here_columns = slice(index * wide, (index + 1) * wide)
            pair = by_core(mine[:, here_columns], theirs[:, here_columns], 1)
            kept = lax.dynamic_slice_in_dim(keep_mask, start, 2 * wide, axis=1).astype(F32)
            base = lax.dynamic_slice_in_dim(tokens, start, 2 * wide, axis=1).astype(F32)
            part = (base + kept * pair * (1.0 / 0.9)).astype(BF16)
            result = lax.dynamic_update_slice_in_dim(result, part, start, axis=1)
    return result


def solution(mesh):
    in_specs = (
        P(("seq", "tp"), None),
        P(),
        P(None, "seq", "tp"),
        P(None, "tp"),
        P("tp", "seq"),
        P(("seq", "tp"), None),
    )
    out_specs = P(("seq", "tp"), None)
    return jax.shard_map(
        on_device, mesh=mesh, in_specs=in_specs, out_specs=out_specs, check_vma=False
    )
```

```python
import functools
import math

import jax
import jax.numpy as jnp
from jax import lax
from jax.experimental import pallas as pl
from jax.experimental.pallas import tpu as pltpu
from jax.sharding import PartitionSpec as P

F32 = jnp.float32
BF16 = jnp.bfloat16
GRANT = 12 << 20
WHOLE = pl.BlockSpec(memory_space=pltpu.VMEM)


def grid_of(chips):
    ny = max(d for d in range(1, math.isqrt(chips) + 1) if chips % d == 0)
    return ny, chips // ny


def dot(a, b):
    return jnp.dot(a, b, preferred_element_type=F32)


def columns_of(x_ref, at_ref, index, deep):
    return x_ref[:, pl.ds(pl.multiple_of(at_ref[index], deep), deep)]


def tiles_of(out_ref):
    tile = math.gcd(out_ref.shape[1], 256)
    return [slice(at, at + tile) for at in range(0, out_ref.shape[1], tile)]


def blocks_of(xs, out_ref):
    tile = math.gcd(out_ref.shape[1], 256)
    size = xs[0].shape[0]
    for at in range(0, out_ref.shape[1], tile):
        for index, x_ref in enumerate(xs):
            yield x_ref, slice(index * size, (index + 1) * size), slice(at, at + tile)


def query_kernel(parts, at_ref, *refs):
    xs, pairs, out_ref = refs[:parts], refs[parts:-1], refs[-1]
    deep = pairs[0].shape[1]
    for x_ref, rows, tile in blocks_of(xs, out_ref):
        query = None
        for index in range(2 * len(pairs)):
            x = columns_of(x_ref, at_ref, index, deep)
            new = dot(x, pairs[index // 2][index % 2, :, tile])
            query = new if query is None else query + new
        out_ref[rows, tile] = query


def gate_kernel(parts, at_ref, *refs):
    xs, refs = refs[:parts], refs[parts:]
    filtered_ref, partial_ref, pieces, out_ref = refs[0], refs[1], refs[2:-1], refs[-1]
    deep = pieces[0].shape[0]
    for x_ref, rows, tile in blocks_of(xs, out_ref):
        query = partial_ref[rows, tile]
        for index, piece in enumerate(pieces):
            query = query + dot(columns_of(x_ref, at_ref, index, deep), piece[:, tile])
        gated = query.astype(BF16).astype(F32) * filtered_ref[rows, tile]
        out_ref[rows, tile] = gated.astype(BF16)


def call(kernel, scalars, operands, out, scratch=()):
    return pl.pallas_call(
        kernel,
        out_shape=out,
        in_specs=[pl.BlockSpec(memory_space=pltpu.SMEM)] + [WHOLE] * len(operands),
        out_specs=jax.tree.map(lambda _: WHOLE, out),
        scratch_shapes=scratch,
        compiler_params=pltpu.CompilerParams(vmem_limit_bytes=GRANT),
        cost_estimate=pl.CostEstimate(flops=1, bytes_accessed=1, transcendentals=0),
    )(scalars, *operands)


def project(kernel, at, xs, extra, pieces, out_dtype):
    rows = sum(x.shape[0] for x in xs)
    out = jax.ShapeDtypeStruct((rows, pieces[0].shape[-1]), out_dtype)
    return call(functools.partial(kernel, len(xs)), at, (*xs, *extra, *pieces), out)


def product_kernel(parts, count, at_ref, *refs):
    xs, refs = refs[:parts], refs[parts:]
    given, refs = refs[:count], refs[count:]
    outs, (joined, *pieces, sems) = refs[:parts], refs[parts:]
    ends = [0]
    for x_ref in xs:
        ends.append(ends[-1] + x_ref.shape[0])
    targets = [joined.at[low:high] for low, high in zip(ends, ends[1:])] + list(pieces)
    copies = [
        pltpu.make_async_copy(source, target, sems.at[index])
        for index, (source, target) in enumerate(zip((*xs, *given), targets))
    ]
    for copy in copies:
        copy.start()
    for copy in copies[:parts]:
        copy.wait()
    deep = pieces[0].shape[1]
    half = pieces[0].shape[2]
    tile = math.gcd(half, 256)
    for low in range(0, half, tile):
        columns = slice(low, low + tile)
        key = value = None
        for index, piece in enumerate(pieces):
            if low == 0:
                copies[parts + index].wait()
            x = columns_of(joined, at_ref, index, deep)
            new_key, new_value = dot(x, piece[0, :, columns]), dot(x, piece[1, :, columns])
            key = new_key if key is None else key + new_key
            value = new_value if value is None else value + new_value
        product = key.astype(BF16).astype(F32) * value.astype(BF16).astype(F32)
        for out, start, end in zip(outs, ends, ends[1:]):
            out[:, columns] = product[start:end]


def products(at, xs, pieces):
    half = pieces[0].shape[2]
    held = [pltpu.VMEM((sum(x.shape[0] for x in xs), xs[0].shape[1]), BF16)]
    held += [pltpu.VMEM(piece.shape, BF16) for piece in pieces]
    held.append(pltpu.SemaphoreType.DMA((len(xs) + len(pieces),)))
    return pl.pallas_call(
        functools.partial(product_kernel, len(xs), len(pieces)),
        out_shape=[jax.ShapeDtypeStruct((x.shape[0], half), F32) for x in xs],
        in_specs=[pl.BlockSpec(memory_space=pltpu.SMEM)]
        + [pl.BlockSpec(memory_space=pl.ANY)] * (len(xs) + len(pieces)),
        out_specs=[WHOLE] * len(xs),
        scratch_shapes=held,
        compiler_params=pltpu.CompilerParams(vmem_limit_bytes=56 << 20),
        cost_estimate=pl.CostEstimate(flops=1, bytes_accessed=1, transcendentals=0),
    )(at, *xs, *pieces)


def filter_kernel(_, product_ref, halo_ref, taps_ref, out_ref, held):
    length, pad = product_ref.shape[0], halo_ref.shape[0]
    held[:pad] = halo_ref[...]
    held[pad:] = product_ref[...]
    for tile in tiles_of(out_ref):
        total = None
        for offset in range(taps_ref.shape[0]):
            term = taps_ref[offset : offset + 1, tile] * held[pad - offset : pad - offset + length, tile]
            total = term if total is None else total + term
        out_ref[:, tile] = total


def causal_filter(at, product, halo, taps):
    length, half = product.shape
    out = jax.ShapeDtypeStruct(product.shape, F32)
    scratch = [pltpu.VMEM((halo.shape[0] + length, half), F32)]
    return call(filter_kernel, at, (product, halo, taps), out, scratch)


def terms_kernel(plan, turned, n_tp, at_ref, *refs):
    gates, refs, held = refs[:4], refs[4:-1], refs[-1]
    count = sum(len(parts) for parts in plan)
    weights, outs = refs[:count], refs[count:]
    half = gates[0].shape[1]
    rows = gates[0].shape[0] // n_tp
    for slot in range(n_tp):
        for index, gate in enumerate(gates):
            side, whose = index % 2, index // 2
            place = slice((2 * slot + whose) * rows, (2 * slot + whose + 1) * rows)
            owner = lax.rem(at_ref[1] + slot, n_tp) * rows if turned else slot * rows
            column = (at_ref[0] if side == 0 else 1 - at_ref[0]) * half
            taken = gate[pl.ds(pl.multiple_of(owner, rows), rows)]
            held[place, pl.ds(pl.multiple_of(column, half), half)] = taken
    wide = weights[0].shape[1]
    share = held.shape[0] // len(outs)
    used = 0
    for index, parts in enumerate(plan):
        at = slice(index * wide, (index + 1) * wide)
        for piece in range(0, held.shape[0], share):
            total, depth = None, 0
            for which in range(len(parts)):
                weight = weights[used + which]
                low, depth = depth, depth + weight.shape[0]
                new = dot(held[piece : piece + share, low:depth], weight[...])
                total = new if total is None else total + new
            outs[piece // share][:, at] = total.astype(BF16)
        used += len(parts)


def terms(n_tp, place, gates, blocks, turned):
    length, half = gates[0].shape
    weights = [part for parts in blocks for part in parts]
    cols = len(blocks) * weights[0].shape[1]
    slots = n_tp if turned else 1
    out = [jax.ShapeDtypeStruct((2 * length // slots, cols), BF16)] * slots
    kernel = functools.partial(terms_kernel, blocks_plan(blocks), turned, n_tp)
    scratch = [pltpu.VMEM((2 * length, 2 * half), BF16)]
    result = call(kernel, place, (*gates, *weights), out, scratch)
    return result if turned else result[0]


def blocks_plan(blocks):
    return [range(len(parts)) for parts in blocks]


def near_kernel(n_tp, at_ref, *refs):
    gates, refs = refs[:4], refs[4:]
    count = (len(refs) - 4) // 2
    given, (out_ref, held, *refs) = refs[:count], refs[count:]
    weights, (ready, sems, out_sems) = refs[:count], refs[count:]
    copies = [
        pltpu.make_async_copy(source, target, sems.at[index])
        for index, (source, target) in enumerate(zip(given, weights))
    ]
    for copy in copies:
        copy.start()
    half = gates[0].shape[1]
    rows = gates[0].shape[0] // n_tp
    for slot in range(n_tp):
        for index, gate in enumerate(gates):
            side, whose = index % 2, index // 2
            place = slice((2 * slot + whose) * rows, (2 * slot + whose + 1) * rows)
            column = (at_ref[0] if side == 0 else 1 - at_ref[0]) * half
            columns = pl.ds(pl.multiple_of(column, half), half)
            held[place, columns] = gate[slot * rows : (slot + 1) * rows]
    wide = weights[0].shape[1]
    tile = math.gcd(wide, 256)
    leaving = []
    for index, weight in enumerate(weights):
        copies[index].wait()
        at = slice(index * wide, (index + 1) * wide)
        for low in range(at.start, at.stop, tile):
            columns = slice(low, low + tile)
            inner = slice(low - at.start, low - at.start + tile)
            total = dot(held[:, :half], weight[:half, inner])
            total = total + dot(held[:, half:], weight[half:, inner])
            ready[:, columns] = total.astype(BF16)
            sem = out_sems.at[len(leaving)]
            leaving.append(pltpu.make_async_copy(ready.at[:, columns], out_ref.at[:, columns], sem))
            leaving[-1].start()
    for copy in leaving:
        copy.wait()


def near_terms(n_tp, place, gates, weights):
    length, half = gates[0].shape
    shape = (2 * length, len(weights) * weights[0].shape[1])
    anywhere = pl.BlockSpec(memory_space=pl.ANY)
    return pl.pallas_call(
        functools.partial(near_kernel, n_tp),
        out_shape=jax.ShapeDtypeStruct(shape, BF16),
        in_specs=[pl.BlockSpec(memory_space=pltpu.SMEM)]
        + [WHOLE] * 4
        + [anywhere] * len(weights),
        out_specs=anywhere,
        scratch_shapes=[pltpu.VMEM((2 * length, 2 * half), BF16)]
        + [pltpu.VMEM(weight.shape, BF16) for weight in weights]
        + [pltpu.VMEM(shape, BF16)]
        + [pltpu.SemaphoreType.DMA((len(weights),))]
        + [pltpu.SemaphoreType.DMA((shape[1] // math.gcd(weights[0].shape[1], 256),))],
        compiler_params=pltpu.CompilerParams(vmem_limit_bytes=24 << 20),
        cost_estimate=pl.CostEstimate(flops=1, bytes_accessed=1, transcendentals=0),
    )(place, *gates, *weights)


def on_device(tokens, norm_gain, in_weight, filters, out_weight, keep_mask):
    n_seq, n_tp = lax.axis_size("seq"), lax.axis_size("tp")
    chips = n_seq // 2
    ny, nx = grid_of(chips)
    seq = lax.axis_index("seq")
    core, here = seq % 2, seq // 2
    my_y, my_x = here // nx, here % nx
    rows, model = tokens.shape
    length = rows * n_tp
    deep, channels = in_weight.shape[1:]
    half = channels // 2
    wide = out_weight.shape[1]

    def place(y, x, c):
        return ((y % ny) * nx + x % nx) * 2 + c

    def from_chip(block, dy, dx):
        route = [
            (place(y + dy, x + dx, c), place(y, x, c))
            for y in range(ny)
            for x in range(nx)
            for c in range(2)
        ]
        return lax.ppermute(block, "seq", route)

    def from_partner(block):
        return lax.ppermute(block, "seq", [(s, s ^ 1) for s in range(n_seq)])

    def direct(mine, brought):
        along_x = [(mine, brought)]
        along_y = [(mine, brought)]
        along_x += [tuple(from_chip(b, 0, dx) for b in (mine, brought)) for dx in range(1, nx)]
        along_y += [tuple(from_chip(b, dy, 0) for b in (mine, brought)) for dy in range(1, ny)]
        return along_x, along_y

    def onward(along_x, along_y):
        return {
            (dy, dx): (from_chip(along_x[dx][0], dy, 0), from_chip(along_y[dy][1], 0, dx))
            for dy in range(1, ny)
            for dx in range(1, nx)
        }

    def crossed(along_x, along_y):
        return {
            (dy, dx): (from_chip(along_x[0, dx][0], dy, 0), from_chip(along_y[dy, 0][1], 0, dx))
            for dy, _ in along_y
            for _, dx in along_x
        }

    def listed(along_x, along_y, rest):
        found = {(0, dx): pair for dx, pair in enumerate(along_x)}
        found.update({(dy, 0): pair for dy, pair in enumerate(along_y)})
        found.update(rest)
        return found

    def by_core(mine, other, axis):
        return jnp.where(
            core == 0,
            jnp.concatenate([mine, other], axis=axis),
            jnp.concatenate([other, mine], axis=axis),
        )

    def columns(array, first, count, at):
        return lax.dynamic_slice(array, (first, 0, at * half), (count, deep, half))

    mine_kv = columns(in_weight, 1, 2, core)
    away_kv = columns(in_weight, 1, 2, 1 - core)
    brought_kv = from_partner(away_kv)
    kv_x, kv_y = direct(mine_kv, brought_kv)

    tokens_then, _ = lax.optimization_barrier((tokens, away_kv))
    widened = tokens_then.astype(F32)
    mean_sq = jnp.mean(widened * widened, axis=1, keepdims=True)
    normed = (widened * lax.rsqrt(mean_sq + 1e-06) * norm_gain).astype(BF16)
    own_rows = lax.all_gather(normed, "tp", axis=0, tiled=True)
    in_weight_then, _ = lax.optimization_barrier((in_weight, normed))
    mine_q = columns(in_weight_then, 0, 1, core)[0]
    both_q = jnp.stack([mine_q, from_partner(columns(in_weight_then, 0, 1, 1 - core)[0])])

    kv_x, kv_y, both_q = lax.optimization_barrier((kv_x, kv_y, both_q))
    kv_rest = onward(kv_x, kv_y)
    q_x = {(0, dx): from_chip(both_q, 0, dx) for dx in range(1, nx)}
    q_y = {(dy, 0): from_chip(both_q, dy, 0) for dy in range(1, ny)}
    arrived = (kv_x, kv_y, kv_rest)
    own_rows, arrived = lax.optimization_barrier((own_rows, arrived))
    kv_x, kv_y, kv_rest = arrived
    kv = listed(kv_x, kv_y, kv_rest)
    order = list(kv)
    kv_pieces = [piece for key in order for piece in kv[key]]
    at = jnp.stack(
        [place(my_y + dy, my_x + dx, core ^ rc) * deep for dy, dx in order for rc in range(2)]
    ).astype(jnp.int32)
    early = 2 * (ny + nx - 1)

    (own_product,) = products(at, [own_rows], kv_pieces)
    reach = filters.shape[0] - 1
    pad = -(-reach // 16) * 16
    ends = [
        lax.ppermute(own_rows[length - pad :], "seq", [(2 * i + 1, 2 * i + 2 + c) for i in range(chips - 1)])
        for c in range(2)
    ]
    before = jnp.where(core == 0, ends[0], ends[1])
    ready = (own_rows, q_x, q_y, own_product, before)
    rows_then, q_x, q_y, own_product, before = lax.optimization_barrier(ready)
    other_rows = from_partner(rows_then)
    q_rest = crossed(q_x, q_y)
    q_pairs = {(0, 0): both_q, **q_x, **q_y}
    q_early = [q_pairs[key] for key in order if key in q_pairs]
    own_query = project(query_kernel, at, [own_rows], [], q_early, F32)
    other_rows, own_query = lax.optimization_barrier((other_rows, own_query))
    rim, other_product = products(at, [before, other_rows], kv_pieces)
    own_tail, other_tail = own_product[length - pad :], other_product[length - pad :]
    first_tail = jnp.where(core == 0, own_tail, other_tail)
    groups = filters.shape[1] // 2
    taps = jnp.repeat(
        lax.dynamic_slice_in_dim(filters, core * groups, groups, axis=1), half // groups, axis=1
    )
    own_filtered = causal_filter(at, own_product, jnp.where(core == 0, rim, first_tail), taps)
    other_filtered = causal_filter(at, other_product, jnp.where(core == 0, first_tail, rim), taps)

    other_rows, own_filtered, other_filtered = lax.optimization_barrier(
        (other_rows, own_filtered, other_filtered)
    )
    other_query = project(query_kernel, at, [other_rows], [], q_early, F32)
    weight_then, q_x, q_y = lax.optimization_barrier((out_weight, q_x, q_y))
    o_x = {(0, dx): from_chip(weight_then, 0, dx) for dx in range(1, nx)}
    o_y = {(dy, 0): from_chip(weight_then, dy, 0) for dy in range(1, ny)}
    o_rest = {
        (dy, dx): (
            from_chip(o_x[0, dx][:half], dy, 0),
            from_chip(o_y[dy, 0][half:], 0, dx),
        )
        for dy in range(1, ny)
        for dx in range(1, nx)
    }
    late = [piece for pair in q_rest.values() for piece in pair]
    other_gated = project(
        gate_kernel, at[early:], [other_rows], [other_filtered, other_query], late, BF16
    )
    own_gated = project(
        gate_kernel, at[early:], [own_rows], [own_filtered, own_query], late, BF16
    )
    gates = (own_gated, from_partner(other_gated), other_gated, from_partner(own_gated))

    position = lax.axis_index("tp")
    here_at = jnp.stack([core, position]).astype(jnp.int32)
    up = [(i, i + 1) for i in range(n_tp - 1)]
    down = [(i + 1, i) for i in range(n_tp - 1)]

    def plus(a, b):
        return (a.astype(F32) + b.astype(F32)).astype(BF16)

    def chained(slots):
        rising = falling = None
        for step in range(n_tp - 1):
            send_up, send_down = slots[n_tp - 1 - step], slots[step + 1]
            if step:
                send_up, send_down = plus(send_up, rising), plus(send_down, falling)
            rising = lax.ppermute(send_up, "tp", up)
            falling = lax.ppermute(send_down, "tp", down)
        total = slots[0].astype(F32) + rising.astype(F32) + falling.astype(F32)
        return total

    near = {(0, 0): (out_weight,)}
    near.update({key: (block,) for key, block in (*o_x.items(), *o_y.items())})
    found = near_terms(n_tp, here_at, gates, [block for (block,) in near.values()])
    gates, found = lax.optimization_barrier((gates, found))
    near_sum = lax.psum_scatter(found, "tp", scatter_dimension=0, tiled=True)
    far_sum = chained(terms(n_tp, here_at, gates, list(o_rest.values()), True))
    result = jnp.zeros((rows, model), BF16)
    far_theirs = from_partner(far_sum[rows:].astype(BF16))
    near_sum, far_theirs, far_sum = lax.optimization_barrier((near_sum, far_theirs, far_sum))
    near_theirs = from_partner(near_sum[rows:].astype(BF16))
    parts = (list(o_rest), far_sum, far_theirs), (list(near), near_sum, near_theirs)
    for keys, mixed, theirs in parts:
        theirs = theirs.astype(F32)
        mine = mixed[:rows].astype(F32)
        for index, (dy, dx) in enumerate(keys):
            start = place(my_y + dy, my_x + dx, 0) * wide
            here_columns = slice(index * wide, (index + 1) * wide)
            pair = by_core(mine[:, here_columns], theirs[:, here_columns], 1)
            kept = lax.dynamic_slice_in_dim(keep_mask, start, 2 * wide, axis=1).astype(F32)
            base = lax.dynamic_slice_in_dim(tokens, start, 2 * wide, axis=1).astype(F32)
            part = (base + kept * pair * (1.0 / 0.9)).astype(BF16)
            result = lax.dynamic_update_slice_in_dim(result, part, start, axis=1)
    return result


def solution(mesh):
    in_specs = (
        P(("seq", "tp"), None),
        P(),
        P(None, "seq", "tp"),
        P(None, "tp"),
        P("tp", "seq"),
        P(("seq", "tp"), None),
    )
    out_specs = P(("seq", "tp"), None)
    return jax.shard_map(
        on_device, mesh=mesh, in_specs=in_specs, out_specs=out_specs, check_vma=False
    )
```

```python
import functools
import math

import jax
import jax.numpy as jnp
from jax import lax
from jax.experimental import pallas as pl
from jax.experimental.pallas import tpu as pltpu
from jax.sharding import PartitionSpec as P

F32 = jnp.float32
BF16 = jnp.bfloat16
GRANT = 12 << 20
WHOLE = pl.BlockSpec(memory_space=pltpu.VMEM)


def grid_of(chips):
    ny = max(d for d in range(1, math.isqrt(chips) + 1) if chips % d == 0)
    return ny, chips // ny


def dot(a, b):
    return jnp.dot(a, b, preferred_element_type=F32)


def columns_of(x_ref, at_ref, index, deep):
    return x_ref[:, pl.ds(pl.multiple_of(at_ref[index], deep), deep)]


def tiles_of(out_ref):
    tile = math.gcd(out_ref.shape[1], 256)
    return [slice(at, at + tile) for at in range(0, out_ref.shape[1], tile)]


def blocks_of(xs, out_ref):
    tile = math.gcd(out_ref.shape[1], 256)
    size = xs[0].shape[0]
    for at in range(0, out_ref.shape[1], tile):
        for index, x_ref in enumerate(xs):
            yield x_ref, slice(index * size, (index + 1) * size), slice(at, at + tile)


def query_kernel(parts, at_ref, *refs):
    xs, pairs, out_ref = refs[:parts], refs[parts:-1], refs[-1]
    deep = pairs[0].shape[1]
    for x_ref, rows, tile in blocks_of(xs, out_ref):
        query = None
        for index in range(2 * len(pairs)):
            x = columns_of(x_ref, at_ref, index, deep)
            new = dot(x, pairs[index // 2][index % 2, :, tile])
            query = new if query is None else query + new
        out_ref[rows, tile] = query


def gate_kernel(parts, at_ref, *refs):
    xs, refs = refs[:parts], refs[parts:]
    filtered_ref, partial_ref, pieces, out_ref = refs[0], refs[1], refs[2:-1], refs[-1]
    deep = pieces[0].shape[0]
    for x_ref, rows, tile in blocks_of(xs, out_ref):
        query = partial_ref[rows, tile]
        for index, piece in enumerate(pieces):
            query = query + dot(columns_of(x_ref, at_ref, index, deep), piece[:, tile])
        gated = query.astype(BF16).astype(F32) * filtered_ref[rows, tile]
        out_ref[rows, tile] = gated.astype(BF16)


def call(kernel, scalars, operands, out, scratch=()):
    return pl.pallas_call(
        kernel,
        out_shape=out,
        in_specs=[pl.BlockSpec(memory_space=pltpu.SMEM)] + [WHOLE] * len(operands),
        out_specs=jax.tree.map(lambda _: WHOLE, out),
        scratch_shapes=scratch,
        compiler_params=pltpu.CompilerParams(vmem_limit_bytes=GRANT),
        cost_estimate=pl.CostEstimate(flops=1, bytes_accessed=1, transcendentals=0),
    )(scalars, *operands)


def project(kernel, at, xs, extra, pieces, out_dtype):
    rows = sum(x.shape[0] for x in xs)
    out = jax.ShapeDtypeStruct((rows, pieces[0].shape[-1]), out_dtype)
    return call(functools.partial(kernel, len(xs)), at, (*xs, *extra, *pieces), out)


def product_kernel(parts, count, at_ref, *refs):
    xs, refs = refs[:parts], refs[parts:]
    given, refs = refs[:count], refs[count:]
    outs, (joined, *pieces, sems) = refs[:parts], refs[parts:]
    ends = [0]
    for x_ref in xs:
        ends.append(ends[-1] + x_ref.shape[0])
    targets = [joined.at[low:high] for low, high in zip(ends, ends[1:])] + list(pieces)
    copies = [
        pltpu.make_async_copy(source, target, sems.at[index])
        for index, (source, target) in enumerate(zip((*xs, *given), targets))
    ]
    for copy in copies:
        copy.start()
    for copy in copies[:parts]:
        copy.wait()
    deep = pieces[0].shape[1]
    half = pieces[0].shape[2]
    tile = math.gcd(half, 256)
    for low in range(0, half, tile):
        columns = slice(low, low + tile)
        key = value = None
        for index, piece in enumerate(pieces):
            if low == 0:
                copies[parts + index].wait()
            x = columns_of(joined, at_ref, index, deep)
            new_key, new_value = dot(x, piece[0, :, columns]), dot(x, piece[1, :, columns])
            key = new_key if key is None else key + new_key
            value = new_value if value is None else value + new_value
        product = key.astype(BF16).astype(F32) * value.astype(BF16).astype(F32)
        for out, start, end in zip(outs, ends, ends[1:]):
            out[:, columns] = product[start:end]


def products(at, xs, pieces):
    half = pieces[0].shape[2]
    held = [pltpu.VMEM((sum(x.shape[0] for x in xs), xs[0].shape[1]), BF16)]
    held += [pltpu.VMEM(piece.shape, BF16) for piece in pieces]
    held.append(pltpu.SemaphoreType.DMA((len(xs) + len(pieces),)))
    return pl.pallas_call(
        functools.partial(product_kernel, len(xs), len(pieces)),
        out_shape=[jax.ShapeDtypeStruct((x.shape[0], half), F32) for x in xs],
        in_specs=[pl.BlockSpec(memory_space=pltpu.SMEM)]
        + [pl.BlockSpec(memory_space=pl.ANY)] * (len(xs) + len(pieces)),
        out_specs=[WHOLE] * len(xs),
        scratch_shapes=held,
        compiler_params=pltpu.CompilerParams(vmem_limit_bytes=56 << 20),
        cost_estimate=pl.CostEstimate(flops=1, bytes_accessed=1, transcendentals=0),
    )(at, *xs, *pieces)


def filter_kernel(_, product_ref, halo_ref, taps_ref, out_ref, held):
    length, pad = product_ref.shape[0], halo_ref.shape[0]
    held[:pad] = halo_ref[...]
    held[pad:] = product_ref[...]
    for tile in tiles_of(out_ref):
        total = None
        for offset in range(taps_ref.shape[0]):
            term = taps_ref[offset : offset + 1, tile] * held[pad - offset : pad - offset + length, tile]
            total = term if total is None else total + term
        out_ref[:, tile] = total


def causal_filter(at, product, halo, taps):
    length, half = product.shape
    out = jax.ShapeDtypeStruct(product.shape, F32)
    scratch = [pltpu.VMEM((halo.shape[0] + length, half), F32)]
    return call(filter_kernel, at, (product, halo, taps), out, scratch)


def terms_kernel(plan, turned, n_tp, at_ref, *refs):
    gates, refs, held = refs[:4], refs[4:-1], refs[-1]
    count = sum(len(parts) for parts in plan)
    weights, outs = refs[:count], refs[count:]
    half = gates[0].shape[1]
    rows = gates[0].shape[0] // n_tp
    for slot in range(n_tp):
        for index, gate in enumerate(gates):
            side, whose = index % 2, index // 2
            place = slice((2 * slot + whose) * rows, (2 * slot + whose + 1) * rows)
            owner = lax.rem(at_ref[1] + slot, n_tp) * rows if turned else slot * rows
            column = (at_ref[0] if side == 0 else 1 - at_ref[0]) * half
            taken = gate[pl.ds(pl.multiple_of(owner, rows), rows)]
            held[place, pl.ds(pl.multiple_of(column, half), half)] = taken
    wide = weights[0].shape[1]
    share = held.shape[0] // len(outs)
    used = 0
    for index, parts in enumerate(plan):
        at = slice(index * wide, (index + 1) * wide)
        for piece in range(0, held.shape[0], share):
            total, depth = None, 0
            for which in range(len(parts)):
                weight = weights[used + which]
                low, depth = depth, depth + weight.shape[0]
                new = dot(held[piece : piece + share, low:depth], weight[...])
                total = new if total is None else total + new
            outs[piece // share][:, at] = total.astype(BF16)
        used += len(parts)


def terms(n_tp, place, gates, blocks, turned):
    length, half = gates[0].shape
    weights = [part for parts in blocks for part in parts]
    cols = len(blocks) * weights[0].shape[1]
    slots = n_tp if turned else 1
    out = [jax.ShapeDtypeStruct((2 * length // slots, cols), BF16)] * slots
    kernel = functools.partial(terms_kernel, blocks_plan(blocks), turned, n_tp)
    scratch = [pltpu.VMEM((2 * length, 2 * half), BF16)]
    result = call(kernel, place, (*gates, *weights), out, scratch)
    return result if turned else result[0]


def blocks_plan(blocks):
    return [range(len(parts)) for parts in blocks]


def near_kernel(n_tp, at_ref, *refs):
    gates, refs = refs[:4], refs[4:]
    count = (len(refs) - 4) // 2
    given, (out_ref, held, *refs) = refs[:count], refs[count:]
    weights, (ready, sems, out_sems) = refs[:count], refs[count:]
    copies = [
        pltpu.make_async_copy(source, target, sems.at[index])
        for index, (source, target) in enumerate(zip(given, weights))
    ]
    for copy in copies:
        copy.start()
    half = gates[0].shape[1]
    rows = gates[0].shape[0] // n_tp
    for slot in range(n_tp):
        for index, gate in enumerate(gates):
            side, whose = index % 2, index // 2
            place = slice((2 * slot + whose) * rows, (2 * slot + whose + 1) * rows)
            column = (at_ref[0] if side == 0 else 1 - at_ref[0]) * half
            columns = pl.ds(pl.multiple_of(column, half), half)
            held[place, columns] = gate[slot * rows : (slot + 1) * rows]
    wide = weights[0].shape[1]
    leaving = []
    for index, weight in enumerate(weights):
        copies[index].wait()
        at = slice(index * wide, (index + 1) * wide)
        tile = math.gcd(wide, 256)
        for low in range(0, wide, tile):
            total = dot(held[:, :half], weight[:half, low : low + tile])
            total = total + dot(held[:, half:], weight[half:, low : low + tile])
            ready[:, index * wide + low : index * wide + low + tile] = total.astype(BF16)
        leaving.append(pltpu.make_async_copy(ready.at[:, at], out_ref.at[:, at], out_sems.at[index]))
        leaving[-1].start()
    for copy in leaving:
        copy.wait()


def near_terms(n_tp, place, gates, weights):
    length, half = gates[0].shape
    shape = (2 * length, len(weights) * weights[0].shape[1])
    anywhere = pl.BlockSpec(memory_space=pl.ANY)
    return pl.pallas_call(
        functools.partial(near_kernel, n_tp),
        out_shape=jax.ShapeDtypeStruct(shape, BF16),
        in_specs=[pl.BlockSpec(memory_space=pltpu.SMEM)]
        + [WHOLE] * 4
        + [anywhere] * len(weights),
        out_specs=anywhere,
        scratch_shapes=[pltpu.VMEM((2 * length, 2 * half), BF16)]
        + [pltpu.VMEM(weight.shape, BF16) for weight in weights]
        + [pltpu.VMEM(shape, BF16)]
        + [pltpu.SemaphoreType.DMA((len(weights),))] * 2,
        compiler_params=pltpu.CompilerParams(vmem_limit_bytes=24 << 20),
        cost_estimate=pl.CostEstimate(flops=1, bytes_accessed=1, transcendentals=0),
    )(place, *gates, *weights)


def on_device(tokens, norm_gain, in_weight, filters, out_weight, keep_mask):
    n_seq, n_tp = lax.axis_size("seq"), lax.axis_size("tp")
    chips = n_seq // 2
    ny, nx = grid_of(chips)
    seq = lax.axis_index("seq")
    core, here = seq % 2, seq // 2
    my_y, my_x = here // nx, here % nx
    rows, model = tokens.shape
    length = rows * n_tp
    deep, channels = in_weight.shape[1:]
    half = channels // 2
    wide = out_weight.shape[1]

    def place(y, x, c):
        return ((y % ny) * nx + x % nx) * 2 + c

    def from_chip(block, dy, dx):
        route = [
            (place(y + dy, x + dx, c), place(y, x, c))
            for y in range(ny)
            for x in range(nx)
            for c in range(2)
        ]
        return lax.ppermute(block, "seq", route)

    def from_partner(block):
        return lax.ppermute(block, "seq", [(s, s ^ 1) for s in range(n_seq)])

    def direct(mine, brought):
        along_x = [(mine, brought)]
        along_y = [(mine, brought)]
        along_x += [tuple(from_chip(b, 0, dx) for b in (mine, brought)) for dx in range(1, nx)]
        along_y += [tuple(from_chip(b, dy, 0) for b in (mine, brought)) for dy in range(1, ny)]
        return along_x, along_y

    def onward(along_x, along_y):
        return {
            (dy, dx): (from_chip(along_x[dx][0], dy, 0), from_chip(along_y[dy][1], 0, dx))
            for dy in range(1, ny)
            for dx in range(1, nx)
        }

    def crossed(along_x, along_y):
        return {
            (dy, dx): (from_chip(along_x[0, dx][0], dy, 0), from_chip(along_y[dy, 0][1], 0, dx))
            for dy, _ in along_y
            for _, dx in along_x
        }

    def listed(along_x, along_y, rest):
        found = {(0, dx): pair for dx, pair in enumerate(along_x)}
        found.update({(dy, 0): pair for dy, pair in enumerate(along_y)})
        found.update(rest)
        return found

    def by_core(mine, other, axis):
        return jnp.where(
            core == 0,
            jnp.concatenate([mine, other], axis=axis),
            jnp.concatenate([other, mine], axis=axis),
        )

    def columns(array, first, count, at):
        return lax.dynamic_slice(array, (first, 0, at * half), (count, deep, half))

    mine_kv = columns(in_weight, 1, 2, core)
    away_kv = columns(in_weight, 1, 2, 1 - core)
    brought_kv = from_partner(away_kv)
    kv_x, kv_y = direct(mine_kv, brought_kv)

    tokens_then, _ = lax.optimization_barrier((tokens, away_kv))
    widened = tokens_then.astype(F32)
    mean_sq = jnp.mean(widened * widened, axis=1, keepdims=True)
    normed = (widened * lax.rsqrt(mean_sq + 1e-06) * norm_gain).astype(BF16)
    own_rows = lax.all_gather(normed, "tp", axis=0, tiled=True)
    in_weight_then, _ = lax.optimization_barrier((in_weight, normed))
    mine_q = columns(in_weight_then, 0, 1, core)[0]
    both_q = jnp.stack([mine_q, from_partner(columns(in_weight_then, 0, 1, 1 - core)[0])])

    kv_x, kv_y, both_q = lax.optimization_barrier((kv_x, kv_y, both_q))
    kv_rest = onward(kv_x, kv_y)
    q_x = {(0, dx): from_chip(both_q, 0, dx) for dx in range(1, nx)}
    q_y = {(dy, 0): from_chip(both_q, dy, 0) for dy in range(1, ny)}
    arrived = (kv_x, kv_y, kv_rest)
    own_rows, arrived = lax.optimization_barrier((own_rows, arrived))
    kv_x, kv_y, kv_rest = arrived
    kv = listed(kv_x, kv_y, kv_rest)
    order = list(kv)
    kv_pieces = [piece for key in order for piece in kv[key]]
    at = jnp.stack(
        [place(my_y + dy, my_x + dx, core ^ rc) * deep for dy, dx in order for rc in range(2)]
    ).astype(jnp.int32)
    early = 2 * (ny + nx - 1)

    (own_product,) = products(at, [own_rows], kv_pieces)
    reach = filters.shape[0] - 1
    pad = -(-reach // 16) * 16
    ends = [
        lax.ppermute(own_rows[length - pad :], "seq", [(2 * i + 1, 2 * i + 2 + c) for i in range(chips - 1)])
        for c in range(2)
    ]
    before = jnp.where(core == 0, ends[0], ends[1])
    ready = (own_rows, q_x, q_y, own_product, before)
    rows_then, q_x, q_y, own_product, before = lax.optimization_barrier(ready)
    other_rows = from_partner(rows_then)
    q_rest = crossed(q_x, q_y)
    q_pairs = {(0, 0): both_q, **q_x, **q_y}
    q_early = [q_pairs[key] for key in order if key in q_pairs]
    own_query = project(query_kernel, at, [own_rows], [], q_early, F32)
    other_rows, own_query = lax.optimization_barrier((other_rows, own_query))
    rim, other_product = products(at, [before, other_rows], kv_pieces)
    own_tail, other_tail = own_product[length - pad :], other_product[length - pad :]
    first_tail = jnp.where(core == 0, own_tail, other_tail)
    groups = filters.shape[1] // 2
    taps = jnp.repeat(
        lax.dynamic_slice_in_dim(filters, core * groups, groups, axis=1), half // groups, axis=1
    )
    own_filtered = causal_filter(at, own_product, jnp.where(core == 0, rim, first_tail), taps)
    other_filtered = causal_filter(at, other_product, jnp.where(core == 0, first_tail, rim), taps)

    other_rows, own_filtered, other_filtered = lax.optimization_barrier(
        (other_rows, own_filtered, other_filtered)
    )
    other_query = project(query_kernel, at, [other_rows], [], q_early, F32)
    weight_then, q_x, q_y = lax.optimization_barrier((out_weight, q_x, q_y))
    o_x = {(0, dx): from_chip(weight_then, 0, dx) for dx in range(1, nx)}
    o_y = {(dy, 0): from_chip(weight_then, dy, 0) for dy in range(1, ny)}
    o_rest = {
        (dy, dx): (
            from_chip(o_x[0, dx][:half], dy, 0),
            from_chip(o_y[dy, 0][half:], 0, dx),
        )
        for dy in range(1, ny)
        for dx in range(1, nx)
    }
    late = [piece for pair in q_rest.values() for piece in pair]
    other_gated = project(
        gate_kernel, at[early:], [other_rows], [other_filtered, other_query], late, BF16
    )
    own_gated = project(
        gate_kernel, at[early:], [own_rows], [own_filtered, own_query], late, BF16
    )
    gates = (own_gated, from_partner(other_gated), other_gated, from_partner(own_gated))

    position = lax.axis_index("tp")
    here_at = jnp.stack([core, position]).astype(jnp.int32)
    up = [(i, i + 1) for i in range(n_tp - 1)]
    down = [(i + 1, i) for i in range(n_tp - 1)]

    def plus(a, b):
        return (a.astype(F32) + b.astype(F32)).astype(BF16)

    def chained(slots):
        rising = falling = None
        for step in range(n_tp - 1):
            send_up, send_down = slots[n_tp - 1 - step], slots[step + 1]
            if step:
                send_up, send_down = plus(send_up, rising), plus(send_down, falling)
            rising = lax.ppermute(send_up, "tp", up)
            falling = lax.ppermute(send_down, "tp", down)
        total = slots[0].astype(F32) + rising.astype(F32) + falling.astype(F32)
        return total

    near = {key: (block,) for key, block in (*o_x.items(), *o_y.items())}
    far = {(0, 0): (out_weight,), **o_rest}
    found = near_terms(n_tp, here_at, gates, [block for (block,) in near.values()])
    gates, found = lax.optimization_barrier((gates, found))
    near_sum = lax.psum_scatter(found, "tp", scatter_dimension=0, tiled=True)
    far_sum = chained(terms(n_tp, here_at, gates, list(far.values()), True))
    result = jnp.zeros((rows, model), BF16)
    far_theirs = from_partner(far_sum[rows:].astype(BF16))
    near_sum, far_theirs, far_sum = lax.optimization_barrier((near_sum, far_theirs, far_sum))
    near_theirs = from_partner(near_sum[rows:].astype(BF16))
    parts = (list(far), far_sum, far_theirs), (list(near), near_sum, near_theirs)
    for keys, mixed, theirs in parts:
        theirs = theirs.astype(F32)
        mine = mixed[:rows].astype(F32)
        for index, (dy, dx) in enumerate(keys):
            start = place(my_y + dy, my_x + dx, 0) * wide
            here_columns = slice(index * wide, (index + 1) * wide)
            pair = by_core(mine[:, here_columns], theirs[:, here_columns], 1)
            kept = lax.dynamic_slice_in_dim(keep_mask, start, 2 * wide, axis=1).astype(F32)
            base = lax.dynamic_slice_in_dim(tokens, start, 2 * wide, axis=1).astype(F32)
            part = (base + kept * pair * (1.0 / 0.9)).astype(BF16)
            result = lax.dynamic_update_slice_in_dim(result, part, start, axis=1)
    return result


def solution(mesh):
    in_specs = (
        P(("seq", "tp"), None),
        P(),
        P(None, "seq", "tp"),
        P(None, "tp"),
        P("tp", "seq"),
        P(("seq", "tp"), None),
    )
    out_specs = P(("seq", "tp"), None)
    return jax.shard_map(
        on_device, mesh=mesh, in_specs=in_specs, out_specs=out_specs, check_vma=False
    )
```
